512 devices in a mesh: tile: 128 (over z_hi, x, y), rep: 4 (over z_lo, core).
Axes of the slice: x: 4, y: 8, z: 8 (z_hi: 4, z_lo: 2; z = z_hi * 2 + z_lo), core: 2. Of those that a mesh axis runs over, the one named last changes fastest.
Arguments:
- features: bfloat16 [4, 8, 4096, 384], P('rep', None, 'tile'), may hold values from -6 to 6
- cotangent: bfloat16 [4, 8, 4096, 384], P('rep', None, 'tile'), may hold values from -6 to 6
- kernel: float32 [7, 7, 384], replicated, may hold values from -0.875 to 0.875
- conv_bias: float32 [384], replicated, may hold values from -3 to 3
- ln_gain: float32 [384], replicated, may hold values from 0.5 to 2
- ln_bias: float32 [384], replicated, may hold values from -3 to 3
- w_in: bfloat16 [384, 1536], replicated, may hold values from -0.3125 to 0.3125
- b_in: float32 [1536], replicated, may hold values from -3 to 3
- w_out: bfloat16 [1536, 384], replicated, may hold values from -0.15625 to 0.15625
- layer_scale: float32 [384], replicated, may hold values from 0.5 to 2
- tissue: int32 [4, 512], P('rep', 'tile'), may hold values from 0 to 1, as said below
Outputs:
- grad_features: bfloat16 [4, 8, 4096, 384], P('rep', None, 'tile')
- grad_w_in: float32 [1536, 384], P(('tile', 'rep'))
- grad_w_out: bfloat16 [1536, 384], replicated
The draws below stay inside these ranges and needn't reach their ends.
Inputs may be any that keep to these rules, and one draw needn't show every extreme that they name: Within each band, among the 4 tiles of one index of tile (aligned blocks along the second dimension), at least 1 and at most 3 are tissue, and in every band some index has exactly 3.
All inputs are finite; a program needn't handle non-finite values.
Results may differ from the reference program's by a relative error of at most 0.0069.
Values may be sent and summed in bfloat16 or wider, within the bound.
No kernel may reach another device: no remote copies, remote signals or barrier semaphores. Data moves between devices by JAX's collectives and lax.ppermute only.
A program may use at most 64 MiB of HBM per device.

```python
import math
import jax
import jax.numpy as jnp
from jax import lax

WIDTH = 384
HIDDEN_SIZE = 1536
TILE_SIDE = 8
TILES_DEV = 4
CAPACITY = 3
BANDS = 4
TILES = 512
BAND_COLS = 4096
POSITIONS = 131072


def draw_tissue(key, part):
    key = jax.random.fold_in(key, 11)
    groups = TILES // TILES_DEV
    first, second, third = jax.random.split(key, 3)
    counts = jax.random.randint(first, (BANDS, groups), 1, CAPACITY + 1)
    chosen = jax.random.randint(second, (BANDS, 1), 0, groups)
    places = jnp.arange(groups).astype(jnp.int32)[None, :]
    counts = jnp.where(places == chosen, CAPACITY, counts)
    scores = jax.random.randint(third, (BANDS, groups, TILES_DEV), 0, 1 << 20) * TILES_DEV
    scores = scores + jnp.arange(TILES_DEV).astype(jnp.int32)
    ranks = jnp.argsort(jnp.argsort(scores, axis=-1), axis=-1)
    flags = (ranks < counts[:, :, None]).astype(jnp.int32)
    return flags.reshape(BANDS, TILES)


def block_levels(own_key, dims, shards, low, high):
    gain = 1.0
    for dim, shards_of in shards:
        steps = jax.random.uniform(jax.random.fold_in(jax.random.fold_in(own_key, 6), dim), (shards_of,), jnp.float32, low / len(shards), high / len(shards))
        gain = gain * jnp.repeat(jnp.exp(steps), dims[dim] // shards_of).reshape((-1,) + (1,) * (len(dims) - 1 - dim))
    return gain


def noise(key, shape, spread, limit, shards=(), kind=jnp.bfloat16):
    drawn = jax.random.normal(key, shape, jnp.float32) * spread
    if len(shards) > 0:
        drawn = block_levels(key, shape, shards, -0.22, 0.18) * drawn
    return jnp.clip(drawn, min=-limit, max=limit).astype(kind)


def setup_inputs(seed: int = 0) -> dict:
    key_of = jax.random.split(jax.random.key(seed), 12)
    features = noise(key_of[0], (BANDS, TILE_SIDE, BAND_COLS, WIDTH), 1.0, 6.0, ((0, 4), (2, 128)))
    cotangent = noise(key_of[1], (BANDS, TILE_SIDE, BAND_COLS, WIDTH), 1.0, 6.0, ((0, 4), (2, 128)))
    kernel = noise(key_of[2], (7, 7, WIDTH), 49 ** -0.5, 0.875, (), jnp.float32)
    conv_bias = noise(key_of[3], (WIDTH,), 0.5, 3.0, (), jnp.float32)
    ln_gain = jnp.clip(jnp.exp(jax.random.uniform(key_of[4], (WIDTH,), jnp.float32, math.log(0.5), math.log(2.0))), 0.5, 2.0)
    ln_bias = noise(key_of[5], (WIDTH,), 0.5, 3.0, (), jnp.float32)
    w_in = noise(key_of[6], (WIDTH, HIDDEN_SIZE), WIDTH ** -0.5, 0.3125)
    b_in = noise(key_of[7], (HIDDEN_SIZE,), 0.5, 3.0, (), jnp.float32)
    w_out = noise(key_of[8], (HIDDEN_SIZE, WIDTH), HIDDEN_SIZE ** -0.5, 0.15625)
    layer_scale = jnp.clip(jnp.exp(jax.random.uniform(key_of[9], (WIDTH,), jnp.float32, math.log(0.5), math.log(2.0))), 0.5, 2.0)
    tissue = draw_tissue(jax.random.fold_in(key_of[11], 71), 0)
    return dict(features=features, cotangent=cotangent, kernel=kernel, conv_bias=conv_bias, ln_gain=ln_gain, ln_bias=ln_bias, w_in=w_in, b_in=b_in, w_out=w_out, layer_scale=layer_scale, tissue=tissue)


EPSILON = 1e-06

def depthwise(padded, kernel, height, breadth):
    total = jnp.zeros((height, breadth, padded.shape[-1]), jnp.float32)
    for a in range(7):
        for e in range(7):
            total = total + padded[a:a + height, e:e + breadth].astype(jnp.float32) * kernel[a, e]
    return total

def transposed(padded, kernel, height, breadth):
    total = jnp.zeros((height, breadth, padded.shape[-1]), jnp.float32)
    for a in range(7):
        for e in range(7):
            total = total + padded[6 - a:6 - a + height, 6 - e:6 - e + breadth] * kernel[a, e]
    return total

def gelu_slope(preact):
    normal_cdf = 0.5 * (1.0 + lax.erf(preact * 0.7071067811865476))
    density = jnp.exp(-0.5 * preact * preact) * 0.3989422804014327
    return normal_cdf + preact * density

def contract(left, right):
    return lax.dot_general(left, right, (((0,), (0,)), ((), ())), preferred_element_type=jnp.float32)

def branch_back(conv_rows, grad_rows, gate_rows, ln_gain, ln_bias, w_in, b_in, w_out, layer_scale):
    centre = conv_rows - lax.optimization_barrier(jnp.mean(conv_rows, axis=-1, keepdims=True))
    inverse = lax.rsqrt(lax.optimization_barrier(jnp.mean(centre * centre, axis=-1, keepdims=True)) + EPSILON)
    standard = centre * inverse
    normed = (standard * ln_gain + ln_bias).astype(jnp.bfloat16)
    preact = jnp.dot(normed, w_in, preferred_element_type=jnp.float32) + b_in
    hidden = jax.nn.gelu(preact, approximate=False).astype(jnp.bfloat16)
    out_grad = (grad_rows.astype(jnp.float32) * layer_scale * gate_rows).astype(jnp.bfloat16)
    back_hidden = lax.dot_general(out_grad, w_out, (((1,), (1,)), ((), ())), preferred_element_type=jnp.float32)
    grad_pre = (back_hidden * gelu_slope(preact)).astype(jnp.bfloat16)
    grad_std = lax.dot_general(grad_pre, w_in, (((1,), (1,)), ((), ())), preferred_element_type=jnp.float32) * ln_gain
    grad_conv = inverse * (grad_std - lax.optimization_barrier(jnp.mean(grad_std, axis=-1, keepdims=True)) - standard * lax.optimization_barrier(jnp.mean(grad_std * standard, axis=-1, keepdims=True)))
    return (normed, hidden, out_grad, grad_pre, grad_conv)

def reference(features, cotangent, kernel, conv_bias, ln_gain, ln_bias, w_in, b_in, w_out, layer_scale, tissue):

    def one_band(carry, inputs):
        image, upstream, flags = inputs
        height, breadth, channels = image.shape
        padded = jnp.pad(image, ((3, 3), (3, 3), (0, 0)))
        conv_out = depthwise(padded, kernel, height, breadth) + conv_bias
        column_gate = jnp.repeat(flags.astype(jnp.float32), TILE_SIDE)
        gate_rows = jnp.broadcast_to(column_gate[None, :], (height, breadth)).reshape(-1, 1)
        normed, hidden, out_grad, grad_pre, grad_conv = branch_back(conv_out.reshape(-1, channels), upstream.reshape(-1, channels), gate_rows, ln_gain, ln_bias, w_in, b_in, w_out, layer_scale)
        out_total = carry[0] + contract(hidden, out_grad)
        in_total = carry[1] + contract(grad_pre, normed)
        grad_pad = jnp.pad(grad_conv.reshape(height, breadth, channels), ((3, 3), (3, 3), (0, 0)))
        grad_image = (upstream.astype(jnp.float32) + transposed(grad_pad, kernel, height, breadth)).astype(jnp.bfloat16)
        return ((out_total, in_total), grad_image)
    start = (jnp.zeros((HIDDEN_SIZE, WIDTH), jnp.float32), jnp.zeros((HIDDEN_SIZE, WIDTH), jnp.float32))
    totals, grad_features = lax.scan(one_band, start, (features, cotangent, tissue))
    scale = 1.0 / math.sqrt(POSITIONS)
    grad_w_out = (totals[0] * scale).astype(jnp.bfloat16)
    grad_w_in = totals[1] * scale
    return (grad_features, grad_w_in, grad_w_out)
```

```python
import math

import jax
import jax.numpy as jnp
from jax import lax
from jax.sharding import PartitionSpec as P

TILE_SIDE = 8


EPSILON = 1e-06


def extended(block, sides, width):
    for axis, dim in sides:
        count = lax.axis_size(axis)
        forward = [(i, i + 1) for i in range(count - 1)]
        backward = [(target, source) for source, target in forward]
        low = lax.ppermute(
            lax.slice_in_dim(block, block.shape[dim] - width, None, axis=dim), axis, forward
        )
        high = lax.ppermute(lax.slice_in_dim(block, 0, width, axis=dim), axis, backward)
        block = jnp.concatenate([low, block, high], axis=dim)
    return block


def depthwise(padded, kernel, height, breadth):
    total = jnp.zeros((height, breadth, padded.shape[-1]), jnp.float32)
    for a in range(7):
        for e in range(7):
            total = (
                total + padded[a : a + height, e : e + breadth].astype(jnp.float32) * kernel[a, e]
            )
    return total


def transposed(padded, kernel, height, breadth):
    total = jnp.zeros((height, breadth, padded.shape[-1]), jnp.float32)
    for a in range(7):
        for e in range(7):
            total = total + padded[6 - a : 6 - a + height, 6 - e : 6 - e + breadth] * kernel[a, e]
    return total


def gelu_slope(preact):
    normal_cdf = 0.5 * (1.0 + lax.erf(preact * 0.7071067811865476))
    density = jnp.exp(-0.5 * preact * preact) * 0.3989422804014327
    return normal_cdf + preact * density


def contract(left, right):
    return lax.dot_general(
        left, right, (((0,), (0,)), ((), ())), preferred_element_type=jnp.float32
    )


def branch_back(conv_rows, grad_rows, gate_rows, ln_gain, ln_bias, w_in, b_in, w_out, layer_scale):
    centre = conv_rows - jnp.mean(conv_rows, axis=-1, keepdims=True)
    inverse = lax.rsqrt(jnp.mean(centre * centre, axis=-1, keepdims=True) + EPSILON)
    standard = centre * inverse
    normed = (standard * ln_gain + ln_bias).astype(jnp.bfloat16)
    preact = jnp.dot(normed, w_in, preferred_element_type=jnp.float32) + b_in
    hidden = jax.nn.gelu(preact, approximate=False).astype(jnp.bfloat16)
    out_grad = (grad_rows.astype(jnp.float32) * layer_scale * gate_rows).astype(jnp.bfloat16)
    back_hidden = lax.dot_general(
        out_grad, w_out, (((1,), (1,)), ((), ())), preferred_element_type=jnp.float32
    )
    grad_pre = (back_hidden * gelu_slope(preact)).astype(jnp.bfloat16)
    grad_std = (
        lax.dot_general(
            grad_pre, w_in, (((1,), (1,)), ((), ())), preferred_element_type=jnp.float32
        )
        * ln_gain
    )
    grad_conv = inverse * (
        grad_std
        - jnp.mean(grad_std, axis=-1, keepdims=True)
        - standard * jnp.mean(grad_std * standard, axis=-1, keepdims=True)
    )
    return (normed, hidden, out_grad, grad_pre, grad_conv)


TILE = ("zh", "x", "y")
RING = ("zh", "y", "zl")
EVERY = ("zh", "x", "y", "zl", "c")
SWAP = [(0, 1), (1, 0)]


def from_core(total):
    core = lax.axis_index("c")
    half = total.shape[0] // 2
    sent = lax.dynamic_slice_in_dim(total, (1 - core) * half, half).astype(jnp.bfloat16)
    kept = lax.dynamic_slice_in_dim(total, core * half, half)
    return kept + lax.ppermute(sent, "c", SWAP).astype(jnp.float32)


def scatter_sum(total, axes, count):
    rows = total.shape[0] // count
    blocks = total.astype(jnp.bfloat16).reshape(count, rows, total.shape[1])
    blocks = lax.all_to_all(blocks, axes, split_axis=0, concat_axis=0, tiled=True)
    return jnp.sum(blocks.astype(jnp.float32), axis=0)


def gather(block, axes, count):
    blocks = jnp.broadcast_to(block[None], (count,) + block.shape)
    blocks = lax.all_to_all(blocks, axes, split_axis=0, concat_axis=0, tiled=True)
    return blocks.reshape(count * block.shape[0], block.shape[1])


def both_cores(half):
    core = lax.axis_index("c")
    rows = half.shape[0]
    other = lax.ppermute(half, "c", SWAP)
    whole = jnp.zeros((2 * rows, half.shape[1]), half.dtype)
    whole = lax.dynamic_update_slice_in_dim(whole, half, core * rows, 0)
    return lax.dynamic_update_slice_in_dim(whole, other, (1 - core) * rows, 0)


def owners(sizes):
    zh_n, x_n, y_n, zl_n, c_n = sizes
    pairs = []
    for source in range(zh_n * x_n * y_n * zl_n * c_n):
        rest, c = divmod(source, c_n)
        rest, zl = divmod(rest, zl_n)
        rest, y = divmod(rest, y_n)
        zh, x = divmod(rest, x_n)
        pairs.append((source, (((c * x_n + x) * zh_n + zh) * y_n + y) * zl_n + zl))
    return pairs


def body(
    features, cotangent, kernel, conv_bias, ln_gain, ln_bias, w_in, b_in, w_out, layer_scale, tissue
):
    image = features[0]
    upstream = cotangent[0]
    flags = tissue[0]
    height, breadth, channels = image.shape
    tiles = flags.shape[0]
    padded = extended(image, ((TILE, 1),), 3)
    padded = jnp.pad(padded, ((3, 3), (0, 0), (0, 0)))
    conv_out = depthwise(padded, kernel, height, breadth) + conv_bias
    column_gate = jnp.broadcast_to(flags.astype(jnp.float32)[:, None], (tiles, TILE_SIDE)).reshape(
        breadth
    )
    gate_rows = jnp.broadcast_to(column_gate[None, :], (height, breadth)).reshape(-1, 1)
    normed, hidden, out_grad, grad_pre, grad_conv = branch_back(
        conv_out.reshape(-1, channels),
        upstream.reshape(-1, channels),
        gate_rows,
        ln_gain,
        ln_bias,
        w_in,
        b_in,
        w_out,
        layer_scale,
    )
    grad_band = grad_conv.reshape(height, breadth, channels)
    sizes = [lax.axis_size(axis) for axis in EVERY]
    ring = sizes[0] * sizes[2] * sizes[3]
    scale = 1.0 / math.sqrt(height * breadth * math.prod(sizes))
    out_total = scatter_sum(from_core(contract(hidden, out_grad)), "x", sizes[1])
    out_total = scatter_sum(out_total, RING, ring)
    grad_w_out = gather((out_total * scale).astype(jnp.bfloat16), RING, ring)
    grad_w_out = both_cores(gather(grad_w_out, "x", sizes[1]))
    in_total = scatter_sum(from_core(contract(grad_pre, normed)), "x", sizes[1])
    in_total = scatter_sum(in_total, RING, ring)
    grad_w_in = lax.ppermute(in_total * scale, EVERY, owners(sizes))
    grad_pad = extended(grad_band, ((TILE, 1),), 3)
    grad_pad = jnp.pad(grad_pad, ((3, 3), (0, 0), (0, 0)))
    grad_image = (
        upstream.astype(jnp.float32) + transposed(grad_pad, kernel, height, breadth)
    ).astype(jnp.bfloat16)
    return (grad_image[None], grad_w_in, grad_w_out)


def solution(mesh):
    devices = mesh.devices.reshape(4, 4, 8, 2, 2)
    fine = jax.sharding.Mesh(devices, EVERY)
    band = P(("zl", "c"), None, TILE, None)
    placed = (band, band) + (P(),) * 8 + (P(("zl", "c"), TILE),)
    return jax.shard_map(
        body,
        mesh=fine,
        in_specs=placed,
        out_specs=(band, P(EVERY, None), P()),
        check_vma=False,
    )
```

```python
import functools
import math

import jax
import jax.numpy as jnp
from jax import lax
from jax.experimental import pallas as pl
from jax.experimental.pallas import tpu as pltpu
from jax.sharding import PartitionSpec as P

SIDE = 8
HALO = 3
TAPS = 7
COLS = 32
LANES = 128
CHUNK = 32
EPSILON = 1e-06
VMEM_LIMIT = 48 * 1024 * 1024
NT = (((1,), (1,)), ((), ()))

TILE = ("zh", "x", "y")
RING = ("zh", "y", "zl")
EVERY = ("zh", "x", "y", "zl", "c")
SWAP = [(0, 1), (1, 0)]


def matmul(left, right, dims=(((1,), (0,)), ((), ()))):
    return lax.dot_general(left, right, dims, preferred_element_type=jnp.float32)


def shifted(column, a):
    move = a - HALO
    if move == 0:
        return column
    row = lax.broadcasted_iota(jnp.int32, column.shape, 0)
    inside = (row + move >= 0) & (row + move < SIDE)
    return jnp.where(inside, pltpu.roll(column, (-move) % SIDE, 0), 0.0)


def convolve(columns, taps, lanes, flip):
    count = len(columns) - 2 * HALO
    totals = [None] * count
    for a in range(TAPS):
        sums = [None] * count
        for e in range(TAPS):
            place = (TAPS - 1 - a) * TAPS + TAPS - 1 - e if flip else a * TAPS + e
            tap = taps[place : place + 1, lanes]
            for j in range(count):
                if columns[j + e] is None:
                    continue
                term = columns[j + e] * tap
                sums[j] = term if sums[j] is None else sums[j] + term
        for j in range(count):
            if sums[j] is None:
                continue
            moved = shifted(sums[j], a)
            totals[j] = moved if totals[j] is None else totals[j] + moved
    return totals


def lane_blocks(width):
    return [slice(start, start + LANES) for start in range(0, width, LANES)]


def widen(source, wide):
    for k, lanes in enumerate(lane_blocks(source.shape[1])):
        wide[k] = source[:, lanes].astype(jnp.float32)


def first_kernel(
    flags, features, cotangent, w_out, w_in, b_in, taps, scale,
    conv, out_grad, back, w_in_t, b_cols, wide
):
    width = features.shape[1]
    widen(cotangent, wide)
    rows = SIDE * SIDE
    for k, lanes in enumerate(lane_blocks(width)):
        for t in range(COLS // SIDE):
            gate = flags[t].astype(jnp.float32)
            tile = jnp.concatenate(
                [wide[k, pl.ds(t * SIDE + j, SIDE, stride=COLS), :] for j in range(SIDE)], axis=0
            )
            tile = (tile * scale[:, lanes] * gate).astype(jnp.bfloat16)
            out_grad[t * rows : (t + 1) * rows, lanes] = tile
    back[...] = matmul(w_out[...], out_grad[...], NT)
    widen(features, wide)
    for k, lanes in enumerate(lane_blocks(width)):
        for t in range(COLS // SIDE):
            columns = []
            for j in range(t * SIDE - HALO, (t + 1) * SIDE + HALO):
                inside = 0 <= j < COLS
                columns.append(wide[k, pl.ds(j, SIDE, stride=COLS), :] if inside else None)
            for j, total in enumerate(convolve(columns, taps, lanes, False)):
                start = (t * SIDE + j) * SIDE
                conv[start : start + SIDE, lanes] = total
    hidden = w_in.shape[1]
    for start in range(0, hidden, LANES):
        w_in_t[start : start + LANES, :] = w_in[:, start : start + LANES].T
        b_cols[start : start + LANES, :] = jnp.broadcast_to(
            b_in[:, start : start + LANES], (LANES, LANES)
        ).T


def second_kernel(
    core, conv, low, high, taps, conv_bias, gain, bias, w_in_t, b_cols, out_grad,
    kept, sent, standard, inverse, normed, preact, cdf, rows, low_wide, high_wide, hidden
):
    width = conv.shape[1]
    rows[...] = conv[...]
    widen(low, low_wide)
    widen(high, high_wide)
    for k, lanes in enumerate(lane_blocks(width)):
        near = [low_wide[k, pl.ds(j, SIDE, stride=HALO), :] for j in range(HALO)]
        for j, total in enumerate(convolve(near + [None] * (2 * HALO), taps, lanes, False)):
            rows[j * SIDE : (j + 1) * SIDE, lanes] += total
        near = [high_wide[k, pl.ds(j, SIDE, stride=HALO), :] for j in range(HALO)]
        for j, total in enumerate(convolve([None] * (2 * HALO) + near, taps, lanes, False)):
            start = (COLS - HALO + j) * SIDE
            rows[start : start + SIDE, lanes] += total
    conv_out = rows[...] + conv_bias[...]
    centre = conv_out - jnp.mean(conv_out, axis=-1, keepdims=True)
    scale = lax.rsqrt(jnp.mean(centre * centre, axis=-1, keepdims=True) + EPSILON)
    inverse[...] = jnp.broadcast_to(scale, inverse.shape)
    standard[...] = centre * scale
    normed[...] = (standard[...] * gain[...] + bias[...]).astype(jnp.bfloat16)
    preact[...] = matmul(w_in_t[...], normed[...], NT)

    def step(i, carry):
        part = pl.ds(pl.multiple_of(i * CHUNK, CHUNK), CHUNK)
        for lanes in lane_blocks(preact.shape[1]):
            z = preact[part, lanes] + b_cols[part, :]
            below = 0.5 * (1.0 + lax.erf(z * 0.7071067811865476))
            preact[part, lanes] = z
            cdf[part, lanes] = below
            hidden[part, lanes] = (z * below).astype(jnp.bfloat16)
        return carry

    lax.fori_loop(0, preact.shape[0] // CHUNK, step, 0, unroll=2)
    half = hidden.shape[0] // 2
    other = pl.ds(pl.multiple_of((1 - core[0]) * half, half), half)
    own = pl.ds(pl.multiple_of(core[0] * half, half), half)
    sent[...] = matmul(hidden[other, :], out_grad[...]).astype(jnp.bfloat16)
    kept[...] = matmul(hidden[own, :], out_grad[...])


def third_kernel(
    core, back, preact, cdf, w_in, normed, standard, inverse, gain,
    kept, sent, grad_conv, low, high, grad_pre
):
    def step(i, carry):
        part = pl.ds(pl.multiple_of(i * CHUNK, CHUNK), CHUNK)
        for lanes in lane_blocks(preact.shape[1]):
            z = preact[part, lanes]
            density = jnp.exp(-0.5 * z * z) * 0.3989422804014327
            slope = cdf[part, lanes] + z * density
            grad_pre[part, lanes] = (back[part, lanes] * slope).astype(jnp.bfloat16)
        return carry

    lax.fori_loop(0, preact.shape[0] // CHUNK, step, 0, unroll=2)
    half = grad_pre.shape[0] // 2
    other = pl.ds(pl.multiple_of((1 - core[0]) * half, half), half)
    own = pl.ds(pl.multiple_of(core[0] * half, half), half)
    grad_std = matmul(w_in[...], grad_pre[...]).T * gain[...]
    sent[...] = matmul(grad_pre[other, :], normed[...]).astype(jnp.bfloat16)
    kept[...] = matmul(grad_pre[own, :], normed[...])
    norm = standard[...]
    mean = jnp.mean(grad_std, axis=-1, keepdims=True)
    along = jnp.mean(grad_std * norm, axis=-1, keepdims=True)
    result = inverse[:, :1] * (grad_std - mean - norm * along)
    grad_conv[...] = result
    edge = HALO * SIDE
    low[...] = result[:edge, :]
    high[...] = result[result.shape[0] - edge :, :]


def last_kernel(grad_conv, low, high, taps, cotangent, grad_features, wide):
    for k, lanes in enumerate(lane_blocks(grad_conv.shape[1])):
        for t in range(COLS // SIDE):
            columns = []
            for j in range(t * SIDE - HALO, (t + 1) * SIDE + HALO):
                if j < 0:
                    source, place = low, j + HALO
                elif j >= COLS:
                    source, place = high, j - COLS
                else:
                    source, place = grad_conv, j
                columns.append(source[place * SIDE : (place + 1) * SIDE, lanes])
            for j, total in enumerate(convolve(columns, taps, lanes, True)):
                wide[k, pl.ds(t * SIDE + j, SIDE, stride=COLS), :] = total
        result = cotangent[:, lanes].astype(jnp.float32) + wide[k]
        grad_features[:, lanes] = result.astype(jnp.bfloat16)


def call(kernel, outs, scratch, scalars, arrays, flops, nbytes):
    in_specs = [pl.BlockSpec(memory_space=pltpu.SMEM)] * len(scalars)
    in_specs += [pl.BlockSpec(memory_space=pltpu.VMEM)] * len(arrays)
    return pl.pallas_call(
        kernel,
        out_shape=[jax.ShapeDtypeStruct(shape, kind) for shape, kind in outs],
        in_specs=in_specs,
        out_specs=[pl.BlockSpec(memory_space=pltpu.VMEM)] * len(outs),
        scratch_shapes=[pltpu.VMEM(shape, kind) for shape, kind in scratch],
        compiler_params=pltpu.CompilerParams(vmem_limit_bytes=VMEM_LIMIT),
        cost_estimate=pl.CostEstimate(flops=flops, bytes_accessed=nbytes, transcendentals=0),
    )(*scalars, *arrays)


def before_halos(flags, features, cotangent, w_out, w_in, b_in, taps, layer_scale):
    rows, width = features.shape
    hidden = w_out.shape[0]
    f32, b16 = jnp.float32, jnp.bfloat16
    return call(
        first_kernel,
        [((rows, width), f32), ((rows, width), b16), ((hidden, rows), f32), ((hidden, width), b16), ((hidden, LANES), f32)],
        [((width // LANES, rows, LANES), f32)],
        [flags],
        [features, cotangent, w_out, w_in, b_in[None], taps, layer_scale[None]],
        2 * rows * width * hidden, 8 * 1024 * 1024,
    )


def forward(core, conv, low, high, taps, conv_bias, gain, bias, w_in_t, b_cols, out_grad):
    rows, width = conv.shape
    hidden = w_in_t.shape[0]
    f32, b16 = jnp.float32, jnp.bfloat16
    return call(
        second_kernel,
        [((hidden // 2, width), f32), ((hidden // 2, width), b16), ((rows, width), f32), ((rows, LANES), f32),
         ((rows, width), b16), ((hidden, rows), f32), ((hidden, rows), f32)],
        [((rows, width), f32), ((width // LANES, HALO * SIDE, LANES), f32), ((width // LANES, HALO * SIDE, LANES), f32),
         ((hidden, rows), b16)],
        [core],
        [conv, low, high, taps, conv_bias[None], gain[None], bias[None], w_in_t, b_cols, out_grad],
        4 * rows * width * hidden, 8 * 1024 * 1024,
    )


def backward(core, back, preact, cdf, w_in, normed, standard, inverse, gain):
    rows, width = standard.shape
    hidden = back.shape[0]
    f32, b16 = jnp.float32, jnp.bfloat16
    return call(
        third_kernel,
        [((hidden // 2, width), f32), ((hidden // 2, width), b16), ((rows, width), f32),
         ((HALO * SIDE, width), f32), ((HALO * SIDE, width), f32)],
        [((hidden, rows), b16)],
        [core],
        [back, preact, cdf, w_in, normed, standard, inverse, gain[None]],
        4 * rows * width * hidden, 8 * 1024 * 1024,
    )


def to_features(grad_conv, low, high, taps, cotangent):
    rows, width = grad_conv.shape
    return call(
        last_kernel,
        [((rows, width), jnp.bfloat16)],
        [((width // LANES, rows, LANES), jnp.float32)],
        [],
        [grad_conv, low, high, taps, cotangent],
        2 * 49 * rows * width, 2 * 1024 * 1024,
    )[0]


def from_left(block):
    count = lax.axis_size(TILE)
    return lax.ppermute(block, TILE, [(i, i + 1) for i in range(count - 1)])


def from_right(block):
    count = lax.axis_size(TILE)
    return lax.ppermute(block, TILE, [(i + 1, i) for i in range(count - 1)])


def core_sum(kept, sent):
    return kept + lax.ppermute(sent, "c", SWAP).astype(jnp.float32)


def exchange(blocks, axes):
    return lax.all_to_all(blocks, axes, split_axis=0, concat_axis=0, tiled=True)


def in_blocks(total, count):
    rows, width = total.shape
    return total.astype(jnp.bfloat16).reshape(count, rows // count, width)


def added(blocks):
    return jnp.sum(blocks.astype(jnp.float32), axis=0)


def copies(block, count):
    return jnp.broadcast_to(block[None], (count,) + block.shape)


def joined(blocks):
    return blocks.reshape(-1, blocks.shape[-1])


def both_cores(half):
    core = lax.axis_index("c")
    rows, width = half.shape
    other = lax.ppermute(half, "c", SWAP)
    whole = jnp.zeros((2 * rows, width), half.dtype)
    whole = lax.dynamic_update_slice_in_dim(whole, half, core * rows, 0)
    return lax.dynamic_update_slice_in_dim(whole, other, (1 - core) * rows, 0)


def owners(sizes):
    zh_n, x_n, y_n, zl_n, c_n = sizes
    pairs = []
    for source in range(zh_n * x_n * y_n * zl_n * c_n):
        rest, c = divmod(source, c_n)
        rest, zl = divmod(rest, zl_n)
        rest, y = divmod(rest, y_n)
        zh, x = divmod(rest, x_n)
        pairs.append((source, (((c * x_n + x) * zh_n + zh) * y_n + y) * zl_n + zl))
    return pairs


def body(
    features, cotangent, kernel, conv_bias, ln_gain, ln_bias, w_in, b_in, w_out, layer_scale, tissue
):
    image = features[0]
    height, breadth, channels = image.shape
    low = from_left(image[:, breadth - HALO :]).reshape(-1, channels)
    high = from_right(image[:, :HALO]).reshape(-1, channels)
    rows = image.reshape(-1, channels)
    upstream = cotangent[0].reshape(-1, channels)
    taps = kernel.reshape(-1, channels)
    core = lax.axis_index("c").astype(jnp.int32).reshape(1)
    sizes = [lax.axis_size(axis) for axis in EVERY]
    lines, ring = sizes[1], sizes[0] * sizes[2] * sizes[3]
    scale = 1.0 / math.sqrt(height * breadth * math.prod(sizes))

    conv, out_grad, back, w_in_t, b_cols = before_halos(
        tissue[0], rows, upstream, w_out, w_in, b_in, taps, layer_scale
    )
    kept, sent, standard, inverse, normed, preact, cdf = forward(
        core, conv, low, high, taps, conv_bias, ln_gain, ln_bias, w_in_t, b_cols, out_grad
    )
    out_total = core_sum(kept, sent)
    kept, sent, grad_conv, low, high = backward(
        core, back, preact, cdf, w_in, normed, standard, inverse, ln_gain
    )
    in_total = core_sum(kept, sent)
    low, high = from_left(high), from_right(low)

    out_total = added(exchange(in_blocks(out_total, lines), "x"))
    in_total = added(exchange(in_blocks(in_total, lines), "x"))
    out_total = added(exchange(in_blocks(out_total, ring), RING))
    own = copies((out_total * scale).astype(jnp.bfloat16), ring)
    mixed = exchange(jnp.stack([own, in_blocks(in_total, ring)], axis=1), RING)
    grad_w_out = joined(mixed[:, 0])
    grad_w_in = lax.ppermute(added(mixed[:, 1]) * scale, EVERY, owners(sizes))
    grad_w_out = both_cores(joined(exchange(copies(grad_w_out, lines), "x")))
    grad_image = to_features(grad_conv, low, high, taps, upstream)
    return (grad_image.reshape(1, height, breadth, channels), grad_w_in, grad_w_out)


def solution(mesh):
    fine = jax.sharding.Mesh(mesh.devices.reshape(4, 4, 8, 2, 2), EVERY)
    band = P(("zl", "c"), None, TILE, None)
    placed = (band, band) + (P(),) * 8 + (P(("zl", "c"), TILE),)
    return jax.shard_map(
        body,
        mesh=fine,
        in_specs=placed,
        out_specs=(band, P(EVERY, None), P()),
        check_vma=False,
    )
```

```python
import functools
import math

import jax
import jax.numpy as jnp
from jax import lax
from jax.experimental import pallas as pl
from jax.experimental.pallas import tpu as pltpu
from jax.sharding import PartitionSpec as P

SIDE = 8
HALO = 3
TAPS = 7
COLS = 32
LANES = 128
CHUNK = 32
ROWS = 3
PLACES = 32
EPSILON = 1e-06
VMEM_LIMIT = 48 * 1024 * 1024
NT = (((1,), (1,)), ((), ()))

TILE = ("zh", "x", "y")
RING = ("zh", "y", "zl")
EVERY = ("zh", "x", "y", "zl", "c")
SWAP = [(0, 1), (1, 0)]


def matmul(left, right, dims=(((1,), (0,)), ((), ()))):
    return lax.dot_general(left, right, dims, preferred_element_type=jnp.float32)


def shifted(column, a):
    move = a - HALO
    if move == 0:
        return column
    row = lax.broadcasted_iota(jnp.int32, column.shape, 0)
    inside = (row + move >= 0) & (row + move < SIDE)
    return jnp.where(inside, pltpu.roll(column, (-move) % SIDE, 0), 0.0)


def convolve(columns, taps, lanes, flip):
    count = len(columns) - 2 * HALO
    totals = [None] * count
    for a in range(TAPS):
        sums = [None] * count
        for e in range(TAPS):
            row, place = (TAPS - 1 - a, TAPS - 1 - e) if flip else (a, e)
            tap = taps[row, place : place + 1, lanes]
            for j in range(count):
                if columns[j + e] is None:
                    continue
                term = columns[j + e] * tap
                sums[j] = term if sums[j] is None else sums[j] + term
        for j in range(count):
            if sums[j] is None:
                continue
            moved = shifted(sums[j], a)
            totals[j] = moved if totals[j] is None else totals[j] + moved
    return totals


def lane_blocks(width):
    return [slice(start, start + LANES) for start in range(0, width, LANES)]


def widen(source, wide):
    for k, lanes in enumerate(lane_blocks(source.shape[1])):
        wide[k] = source[:, lanes].astype(jnp.float32)


def first_kernel(
    flags, features, cotangent, w_out, w_in, b_in, taps, scale, conv_bias, gain, bias,
    conv, out_grad, back, w_in_t, b_cols, w_in_here, taps_here, vectors,
    wide, flags_here, image, upstream, w_out_here, b_here, scale_here, conv_bias_here, gain_here, bias_here, sems
):
    width = features.shape[1]
    pairs = [
        (flags, flags_here), (cotangent, upstream), (scale, scale_here), (w_out, w_out_here),
        (features, image), (taps, taps_here), (w_in, w_in_here), (b_in, b_here),
        (conv_bias, conv_bias_here), (gain, gain_here), (bias, bias_here),
    ]
    copies = [pltpu.make_async_copy(src, dst, sems.at[i]) for i, (src, dst) in enumerate(pairs)]
    for copy in copies:
        copy.start()
    for copy in copies[:3]:
        copy.wait()
    widen(upstream, wide)
    rows = SIDE * SIDE
    by_lane = scale_here[...].reshape(1, width)
    for k, lanes in enumerate(lane_blocks(width)):
        for t in range(COLS // SIDE):
            gate = flags_here[0, t].astype(jnp.float32)
            tile = jnp.concatenate(
                [wide[k, pl.ds(t * SIDE + j, SIDE, stride=COLS), :] for j in range(SIDE)], axis=0
            )
            tile = (tile * by_lane[:, lanes] * gate).astype(jnp.bfloat16)
            out_grad[t * rows : (t + 1) * rows, lanes] = tile
    copies[3].wait()
    back[...] = matmul(w_out_here[...], out_grad[...], NT)
    copies[4].wait()
    copies[5].wait()
    widen(image, wide)
    for k, lanes in enumerate(lane_blocks(width)):
        for t in range(COLS // SIDE):
            columns = []
            for j in range(t * SIDE - HALO, (t + 1) * SIDE + HALO):
                inside = 0 <= j < COLS
                columns.append(wide[k, pl.ds(j, SIDE, stride=COLS), :] if inside else None)
            for j, total in enumerate(convolve(columns, taps_here, lanes, False)):
                start = (t * SIDE + j) * SIDE
                conv[start : start + SIDE, lanes] = total
    for copy in copies[6:]:
        copy.wait()
    hidden = w_in.shape[1]
    for start in range(0, hidden, LANES):
        w_in_t[start : start + LANES, :] = w_in_here[:, start : start + LANES].T
        b_cols[start : start + LANES, :] = jnp.broadcast_to(
            b_here[start : start + LANES].reshape(1, LANES), (LANES, LANES)
        ).T
    for i, vector in enumerate((conv_bias_here, gain_here, bias_here)):
        vectors[i * SIDE : (i + 1) * SIDE, :] = jnp.broadcast_to(
            vector[...].reshape(1, width), (SIDE, width)
        )


def second_kernel(
    core, conv, low, high, taps, vectors, w_in_t, b_cols, out_grad,
    kept, sent, standard, inverse, normed, preact, cdf, rows, low_wide, high_wide, hidden
):
    width = conv.shape[1]
    rows[...] = conv[...]
    widen(low, low_wide)
    widen(high, high_wide)
    for k, lanes in enumerate(lane_blocks(width)):
        near = [low_wide[k, pl.ds(j, SIDE, stride=HALO), :] for j in range(HALO)]
        for j, total in enumerate(convolve(near + [None] * (2 * HALO), taps, lanes, False)):
            rows[j * SIDE : (j + 1) * SIDE, lanes] += total
        near = [high_wide[k, pl.ds(j, SIDE, stride=HALO), :] for j in range(HALO)]
        for j, total in enumerate(convolve([None] * (2 * HALO) + near, taps, lanes, False)):
            start = (COLS - HALO + j) * SIDE
            rows[start : start + SIDE, lanes] += total
    conv_out = rows[...] + vectors[:1, :]
    centre = conv_out - jnp.mean(conv_out, axis=-1, keepdims=True)
    scale = lax.rsqrt(jnp.mean(centre * centre, axis=-1, keepdims=True) + EPSILON)
    inverse[...] = jnp.broadcast_to(scale, inverse.shape)
    standard[...] = centre * scale
    normed[...] = (standard[...] * vectors[SIDE : SIDE + 1, :] + vectors[2 * SIDE : 2 * SIDE + 1, :]).astype(jnp.bfloat16)
    preact[...] = matmul(w_in_t[...], normed[...], NT)

    def step(i, carry):
        part = pl.ds(pl.multiple_of(i * CHUNK, CHUNK), CHUNK)
        for lanes in lane_blocks(preact.shape[1]):
            z = preact[part, lanes] + b_cols[part, :]
            below = 0.5 * (1.0 + lax.erf(z * 0.7071067811865476))
            preact[part, lanes] = z
            cdf[part, lanes] = below
            hidden[part, lanes] = (z * below).astype(jnp.bfloat16)
        return carry

    lax.fori_loop(0, preact.shape[0] // CHUNK, step, 0, unroll=2)
    half = hidden.shape[0] // 2
    other = pl.ds(pl.multiple_of((1 - core[0]) * half, half), half)
    own = pl.ds(pl.multiple_of(core[0] * half, half), half)
    sent[...] = matmul(hidden[other, :], out_grad[...]).astype(jnp.bfloat16)
    kept[...] = matmul(hidden[own, :], out_grad[...])


def slope_kernel(back, preact, cdf, grad_pre):
    def step(i, carry):
        part = pl.ds(pl.multiple_of(i * CHUNK, CHUNK), CHUNK)
        for lanes in lane_blocks(preact.shape[1]):
            z = preact[part, lanes]
            density = jnp.exp(-0.5 * z * z) * 0.3989422804014327
            slope = cdf[part, lanes] + z * density
            grad_pre[part, lanes] = (back[part, lanes] * slope).astype(jnp.bfloat16)
        return carry

    lax.fori_loop(0, preact.shape[0] // CHUNK, step, 0, unroll=2)


def third_kernel(
    core, grad_pre, w_in, normed, standard, inverse, vectors,
    kept, sent, grad_conv, low, high
):
    grad_std = matmul(w_in[...], grad_pre[...]).T * vectors[SIDE : SIDE + 1, :]
    half = grad_pre.shape[0] // 2
    other = pl.ds(pl.multiple_of((1 - core[0]) * half, half), half)
    own = pl.ds(pl.multiple_of(core[0] * half, half), half)
    sent[...] = matmul(grad_pre[other, :], normed[...]).astype(jnp.bfloat16)
    kept[...] = matmul(grad_pre[own, :], normed[...])
    norm = standard[...]
    mean = jnp.mean(grad_std, axis=-1, keepdims=True)
    along = jnp.mean(grad_std * norm, axis=-1, keepdims=True)
    result = inverse[:, :1] * (grad_std - mean - norm * along)
    grad_conv[...] = result
    edge = HALO * SIDE
    low[...] = result[:edge, :]
    high[...] = result[result.shape[0] - edge :, :]


def last_kernel(grad_conv, low, high, taps, cotangent, grad_features, wide):
    for k, lanes in enumerate(lane_blocks(grad_conv.shape[1])):
        for t in range(COLS // SIDE):
            columns = []
            for j in range(t * SIDE - HALO, (t + 1) * SIDE + HALO):
                if j < 0:
                    source, place = low, j + HALO
                elif j >= COLS:
                    source, place = high, j - COLS
                else:
                    source, place = grad_conv, j
                columns.append(source[place * SIDE : (place + 1) * SIDE, lanes])
            for j, total in enumerate(convolve(columns, taps, lanes, True)):
                wide[k, pl.ds(t * SIDE + j, SIDE, stride=COLS), :] = total
        result = cotangent[:, lanes].astype(jnp.float32) + wide[k]
        grad_features[:, lanes] = result.astype(jnp.bfloat16)


def pack_kernel(out_blocks, kept, received, first, second, spread, total):
    members, places, _ = first.shape
    width = kept.shape[1]
    for k, lanes in enumerate(lane_blocks(width)):
        total[k] = kept[:, lanes] + received[:, lanes].astype(jnp.float32)
    blocks = len(lane_blocks(width))
    for message in (first, second):
        spread[...] = jnp.zeros_like(spread)
        if message is first:
            for r in range(ROWS):
                part = slice(r * members, (r + 1) * members)
                for k, lanes in enumerate(lane_blocks(width)):
                    summed = out_blocks[0, part, lanes].astype(jnp.float32)
                    for i in range(1, out_blocks.shape[0]):
                        summed += out_blocks[i, part, lanes].astype(jnp.float32)
                    spread[pl.ds(r * blocks + k, members, stride=places), :] = summed
        offset = 0 if message is first else 2
        for b in range(2):
            for r in range(ROWS):
                start = (offset + b) * ROWS * members + r
                for k in range(blocks):
                    place = ((1 + b) * ROWS + r) * blocks + k
                    spread[pl.ds(place, members, stride=places), :] = total[
                        k, pl.ds(start, members, stride=ROWS), :
                    ]
        message[...] = spread[...].reshape(message.shape).astype(jnp.bfloat16)


def add_members(received):
    summed = received[0].astype(jnp.float32)
    for i in range(1, received.shape[0]):
        summed += received[i].astype(jnp.float32)
    return summed


def turn_kernel(scale, received, second, message, kept_sums):
    summed = add_members(received)
    kept_sums[...] = summed
    finished = (summed * scale).astype(jnp.bfloat16)
    place = lax.broadcasted_iota(jnp.int32, finished.shape, 0)
    of_out = place < ROWS * ROWS
    for m in range(message.shape[0]):
        message[m] = jnp.where(of_out, finished, second[m])


def unpack_kernel(kept_sums, received, message, spread):
    members, places, _ = received.shape
    lines, rows, width = message.shape
    count = ROWS * members
    spread[...] = received[...].astype(jnp.float32).reshape(spread.shape)
    blocks = len(lane_blocks(width))
    for r in range(ROWS):
        for k, lanes in enumerate(lane_blocks(width)):
            part = spread[pl.ds(r * blocks + k, members, stride=places), :].astype(jnp.bfloat16)
            for i in range(lines):
                message[i, r * members : (r + 1) * members, lanes] = part
    last_sums = add_members(received)
    size = ROWS * blocks
    for i in range(lines):
        sums = kept_sums[...] if i < 2 else last_sums
        start = size * (1 + i % 2)
        part = jnp.concatenate([sums[start : start + size, :], jnp.zeros((rows - count - size, LANES), jnp.float32)], axis=0)
        message[i, count:, :LANES] = part.astype(jnp.bfloat16)
        message[i, count:, LANES:] = jnp.zeros((rows - count, width - LANES), jnp.bfloat16)


def line_kernel(scale, received, grad_w_in, spread):
    count = received.shape[1] - 16
    spread[...] = received[0, count:, :LANES].astype(jnp.float32)
    for i in range(1, received.shape[0]):
        spread[...] += received[i, count:, :LANES].astype(jnp.float32)
    blocks = grad_w_in.shape[1] // LANES
    for k in range(blocks):
        grad_w_in[:, k * LANES : (k + 1) * LANES] = (
            spread[pl.ds(k, ROWS, stride=blocks), :] * scale
        )


def join_kernel(core, own, other, grad_w_out):
    lines, rows, _ = own.shape
    rows -= 16
    half = lines * rows
    for place, source in ((core[0], own), (1 - core[0], other)):
        for i in range(lines):
            start = pl.multiple_of(place * half + i * rows, rows)
            grad_w_out[pl.ds(start, rows), :] = source[i, :rows, :]


def call(kernel, outs, scratch, scalars, arrays, flops, nbytes, space=pltpu.VMEM):
    in_specs = [pl.BlockSpec(memory_space=pltpu.SMEM)] * len(scalars)
    in_specs += [pl.BlockSpec(memory_space=space)] * len(arrays)
    return pl.pallas_call(
        kernel,
        out_shape=[jax.ShapeDtypeStruct(shape, kind) for shape, kind in outs],
        in_specs=in_specs,
        out_specs=[pl.BlockSpec(memory_space=pltpu.VMEM)] * len(outs),
        scratch_shapes=scratch,
        compiler_params=pltpu.CompilerParams(vmem_limit_bytes=VMEM_LIMIT),
        cost_estimate=pl.CostEstimate(flops=flops, bytes_accessed=nbytes, transcendentals=0),
    )(*scalars, *arrays)


F32, B16 = jnp.float32, jnp.bfloat16


def before_halos(flags, features, cotangent, kernel, conv_bias, gain, bias, w_in, b_in, w_out, layer_scale):
    rows, width = features.shape
    hidden = w_out.shape[0]
    return call(
        first_kernel,
        [((rows, width), F32), ((rows, width), B16), ((hidden, rows), F32), ((hidden, width), B16),
         ((hidden, LANES), F32), (w_in.shape, B16), (kernel.shape, F32), ((3 * SIDE, width), F32)],
        [pltpu.VMEM((width // LANES, rows, LANES), F32), pltpu.SMEM(flags.shape, jnp.int32),
         pltpu.VMEM((rows, width), B16), pltpu.VMEM((rows, width), B16), pltpu.VMEM(w_out.shape, B16),
         pltpu.VMEM(b_in.shape, F32), pltpu.VMEM((width,), F32), pltpu.VMEM((width,), F32),
         pltpu.VMEM((width,), F32), pltpu.VMEM((width,), F32),
         pltpu.SemaphoreType.DMA((11,))],
        [],
        [flags, features, cotangent, w_out, w_in, b_in, kernel, layer_scale, conv_bias, gain, bias],
        2 * rows * width * hidden, 8 * 1024 * 1024, pltpu.HBM,
    )


def forward(core, conv, low, high, taps, vectors, w_in_t, b_cols, out_grad):
    rows, width = conv.shape
    hidden = w_in_t.shape[0]
    halo = pltpu.VMEM((width // LANES, HALO * SIDE, LANES), F32)
    return call(
        second_kernel,
        [((hidden // 2, width), F32), ((hidden // 2, width), B16), ((rows, width), F32), ((rows, LANES), F32),
         ((rows, width), B16), ((hidden, rows), F32), ((hidden, rows), F32)],
        [pltpu.VMEM((rows, width), F32), halo, halo, pltpu.VMEM((hidden, rows), B16)],
        [core],
        [conv, low, high, taps, vectors, w_in_t, b_cols, out_grad],
        4 * rows * width * hidden, 8 * 1024 * 1024,
    )


def slopes(back, preact, cdf):
    return call(slope_kernel, [(back.shape, B16)], [], [], [back, preact, cdf], 10 * back.size, 14 * back.size)[0]


def backward(core, grad_pre, w_in, normed, standard, inverse, vectors):
    rows, width = standard.shape
    hidden = grad_pre.shape[0]
    edge = (HALO * SIDE, width)
    return call(
        third_kernel,
        [((hidden // 2, width), F32), ((hidden // 2, width), B16), ((rows, width), F32), (edge, F32), (edge, F32)],
        [],
        [core],
        [grad_pre, w_in, normed, standard, inverse, vectors],
        4 * rows * width * hidden, 8 * 1024 * 1024,
    )


def to_features(grad_conv, low, high, taps, cotangent):
    rows, width = grad_conv.shape
    return call(
        last_kernel,
        [((rows, width), B16)],
        [pltpu.VMEM((width // LANES, rows, LANES), F32)],
        [],
        [grad_conv, low, high, taps, cotangent],
        2 * 49 * rows * width, 2 * 1024 * 1024,
    )[0]


def pack(out_blocks, kept, received, members):
    width = kept.shape[1]
    message = ((members, PLACES, LANES), B16)
    return call(
        pack_kernel,
        [message, message],
        [pltpu.VMEM((members * PLACES, LANES), F32), pltpu.VMEM((width // LANES,) + kept.shape[:1] + (LANES,), F32)],
        [],
        [out_blocks, kept, received],
        kept.size, 8 * kept.size,
    )


def turn(scale, received, second):
    return call(
        functools.partial(turn_kernel, scale),
        [(received.shape, B16), ((PLACES, LANES), F32)], [], [], [received, second],
        received.size, 6 * received.size,
    )


def unpack(kept_sums, received, lines, rows, width):
    return call(
        unpack_kernel,
        [((lines, rows + 16, width), B16)],
        [pltpu.VMEM((received.shape[0] * received.shape[1], LANES), F32)],
        [],
        [kept_sums, received],
        received.size, 6 * received.size,
    )[0]


def over_lines(scale, received):
    return call(
        functools.partial(line_kernel, scale),
        [((ROWS, received.shape[2]), F32)],
        [pltpu.VMEM((16, LANES), F32)],
        [],
        [received],
        received.size, received.size,
    )[0]


def join(core, own, other):
    lines, rows, width = own.shape
    return call(
        join_kernel, [((2 * lines * (rows - 16), width), B16)], [], [core], [own, other],
        own.size, 8 * own.size,
    )[0]


def from_left(block):
    count = lax.axis_size(TILE)
    return lax.ppermute(block, TILE, [(i, i + 1) for i in range(count - 1)])


def from_right(block):
    count = lax.axis_size(TILE)
    return lax.ppermute(block, TILE, [(i + 1, i) for i in range(count - 1)])


def exchange(blocks, axes):
    return lax.all_to_all(blocks, axes, split_axis=0, concat_axis=0, tiled=True)


def swap(block):
    return lax.ppermute(block, "c", SWAP)


def owners(sizes):
    zh_n, x_n, y_n, zl_n, c_n = sizes
    pairs = []
    for source in range(zh_n * x_n * y_n * zl_n * c_n):
        rest, c = divmod(source, c_n)
        rest, zl = divmod(rest, zl_n)
        rest, y = divmod(rest, y_n)
        zh, x = divmod(rest, x_n)
        pairs.append((source, (((c * x_n + x) * zh_n + zh) * y_n + y) * zl_n + zl))
    return pairs


def body(
    features, cotangent, kernel, conv_bias, ln_gain, ln_bias, w_in, b_in, w_out, layer_scale, tissue
):
    image = features[0]
    height, breadth, channels = image.shape
    low = from_left(image[:, breadth - HALO :]).reshape(-1, channels)
    high = from_right(image[:, :HALO]).reshape(-1, channels)
    rows = image.reshape(-1, channels)
    upstream = cotangent[0].reshape(-1, channels)
    core = lax.axis_index("c").astype(jnp.int32).reshape(1)
    sizes = [lax.axis_size(axis) for axis in EVERY]
    lines, ring = sizes[1], sizes[0] * sizes[2] * sizes[3]
    scale = 1.0 / math.sqrt(height * breadth * math.prod(sizes))

    conv, out_grad, back, w_in_t, b_cols, w_in_here, taps, vectors = before_halos(
        tissue, rows, upstream, kernel, conv_bias, ln_gain, ln_bias, w_in, b_in, w_out, layer_scale
    )
    kept, sent, standard, inverse, normed, preact, cdf = forward(
        core, conv, low, high, taps, vectors, w_in_t, b_cols, out_grad
    )
    grad_pre = slopes(back, preact, cdf)
    total = (kept + swap(sent).astype(F32)).astype(B16).reshape(lines, -1, channels)
    total, grad_pre = lax.optimization_barrier((total, grad_pre))
    out_blocks = exchange(total, "x")
    kept, sent, grad_conv, low, high = backward(
        core, grad_pre, w_in_here, normed, standard, inverse, vectors
    )
    received = swap(sent)
    low, high = from_left(high), from_right(low)
    out_blocks, received, low, high = lax.optimization_barrier((out_blocks, received, low, high))

    first, second = pack(out_blocks, kept, received, ring)
    message, kept_sums = turn(scale, exchange(first, RING), second)
    message = unpack(kept_sums, exchange(message, RING), lines, out_blocks.shape[1], channels)
    own = exchange(message, "x")
    own, low, high = lax.optimization_barrier((own, low, high))
    other = swap(own)
    grad_w_in = lax.ppermute(over_lines(scale, own), EVERY, owners(sizes))
    grad_image = to_features(grad_conv, low, high, taps, upstream)
    grad_w_out = join(core, own, other)
    return (grad_image.reshape(1, height, breadth, channels), grad_w_in, grad_w_out)


def solution(mesh):
    fine = jax.sharding.Mesh(mesh.devices.reshape(4, 4, 8, 2, 2), EVERY)
    band = P(("zl", "c"), None, TILE, None)
    placed = (band, band) + (P(),) * 8 + (P(("zl", "c"), TILE),)
    return jax.shard_map(
        body,
        mesh=fine,
        in_specs=placed,
        out_specs=(band, P(EVERY, None), P()),
        check_vma=False,
    )
```

```python
import functools
import math

import jax
import jax.numpy as jnp
from jax import lax
from jax.experimental import pallas as pl
from jax.experimental.pallas import tpu as pltpu
from jax.sharding import PartitionSpec as P

SIDE = 8
HALO = 3
TAPS = 7
COLS = 32
LANES = 128
CHUNK = 32
ROWS = 3
EDGE = 4 * SIDE
EPSILON = 1e-06
VMEM_LIMIT = 24 * 1024 * 1024
NT = (((1,), (1,)), ((), ()))

TILE = ("zh", "x", "y")
RING = ("zh", "y", "zl")
EVERY = ("zh", "x", "y", "zl", "c")
SWAP = [(0, 1), (1, 0)]


def matmul(left, right, dims=(((1,), (0,)), ((), ()))):
    return lax.dot_general(left, right, dims, preferred_element_type=jnp.float32)


def shifted(column, a):
    move = a - HALO
    if move == 0:
        return column
    row = lax.broadcasted_iota(jnp.int32, column.shape, 0)
    inside = (row + move >= 0) & (row + move < SIDE)
    return jnp.where(inside, pltpu.roll(column, (-move) % SIDE, 0), 0.0)


def convolve(columns, taps, lanes, flip):
    count = len(columns) - 2 * HALO
    totals = [None] * count
    for a in range(TAPS):
        sums = [None] * count
        for e in range(TAPS):
            row, place = (TAPS - 1 - a, TAPS - 1 - e) if flip else (a, e)
            tap = taps[row, place : place + 1, lanes]
            for j in range(count):
                if columns[j + e] is None:
                    continue
                term = columns[j + e] * tap
                sums[j] = term if sums[j] is None else sums[j] + term
        for j in range(count):
            if sums[j] is None:
                continue
            moved = shifted(sums[j], a)
            totals[j] = moved if totals[j] is None else totals[j] + moved
    return totals


def lane_blocks(width):
    return [slice(start, start + LANES) for start in range(0, width, LANES)]


def widen(source, wide):
    for k, lanes in enumerate(lane_blocks(source.shape[1])):
        wide[k] = source[:, lanes].astype(jnp.float32)


def edge_kernel(features, low, high, image, wide, sem):
    copy = pltpu.make_async_copy(features, image, sem)
    copy.start()
    copy.wait()
    widen(image, wide)
    count = EDGE // SIDE
    for k, lanes in enumerate(lane_blocks(features.shape[1])):
        for first, edge in ((0, low), (COLS - count, high)):
            columns = [wide[k, pl.ds(first + j, SIDE, stride=COLS), :] for j in range(count)]
            edge[:, lanes] = jnp.concatenate(columns, axis=0).astype(jnp.bfloat16)


def first_kernel(
    flags, features, cotangent, w_out, w_in, b_in, taps, scale, conv_bias, gain, bias,
    conv, out_grad, back, w_in_t, b_cols, w_in_here, taps_here, vectors,
    wide, flags_here, image, upstream, w_out_here, b_here, scale_here, conv_bias_here, gain_here, bias_here, sems
):
    width = features.shape[1]
    pairs = [
        (flags, flags_here), (cotangent, upstream), (scale, scale_here), (w_out, w_out_here),
        (features, image), (taps, taps_here), (w_in, w_in_here), (b_in, b_here),
        (conv_bias, conv_bias_here), (gain, gain_here), (bias, bias_here),
    ]
    copies = [pltpu.make_async_copy(src, dst, sems.at[i]) for i, (src, dst) in enumerate(pairs)]
    for copy in copies:
        copy.start()
    for copy in copies[:3]:
        copy.wait()
    widen(upstream, wide)
    rows = SIDE * SIDE
    by_lane = scale_here[...].reshape(1, width)
    for k, lanes in enumerate(lane_blocks(width)):
        for t in range(COLS // SIDE):
            gate = flags_here[0, t].astype(jnp.float32)
            tile = jnp.concatenate(
                [wide[k, pl.ds(t * SIDE + j, SIDE, stride=COLS), :] for j in range(SIDE)], axis=0
            )
            tile = (tile * by_lane[:, lanes] * gate).astype(jnp.bfloat16)
            out_grad[t * rows : (t + 1) * rows, lanes] = tile
    copies[3].wait()
    back[...] = matmul(w_out_here[...], out_grad[...], NT)
    copies[4].wait()
    copies[5].wait()
    widen(image, wide)
    for k, lanes in enumerate(lane_blocks(width)):
        for t in range(COLS // SIDE):
            columns = []
            for j in range(t * SIDE - HALO, (t + 1) * SIDE + HALO):
                inside = 0 <= j < COLS
                columns.append(wide[k, pl.ds(j, SIDE, stride=COLS), :] if inside else None)
            for j, total in enumerate(convolve(columns, taps_here, lanes, False)):
                start = (t * SIDE + j) * SIDE
                conv[start : start + SIDE, lanes] = total
    for copy in copies[6:]:
        copy.wait()
    hidden = w_in.shape[1]
    for start in range(0, hidden, LANES):
        w_in_t[start : start + LANES, :] = w_in_here[:, start : start + LANES].T
        b_cols[start : start + LANES, :] = jnp.broadcast_to(
            b_here[start : start + LANES].reshape(1, LANES), (LANES, LANES)
        ).T
    for i, vector in enumerate((conv_bias_here, gain_here, bias_here)):
        vectors[i * SIDE : (i + 1) * SIDE, :] = jnp.broadcast_to(
            vector[...].reshape(1, width), (SIDE, width)
        )


def second_kernel(
    core, conv, low, high, taps, vectors, w_in_t, b_cols, out_grad,
    kept, sent, standard, inverse, normed, preact, cdf, rows, low_wide, high_wide, hidden
):
    width = conv.shape[1]
    rows[...] = conv[...]
    low_wide[...] = low[...].astype(jnp.float32)
    high_wide[...] = high[...].astype(jnp.float32)
    for lanes in lane_blocks(width):
        near = [low_wide[(j + 1) * SIDE : (j + 2) * SIDE, lanes] for j in range(HALO)]
        for j, total in enumerate(convolve(near + [None] * (2 * HALO), taps, lanes, False)):
            rows[j * SIDE : (j + 1) * SIDE, lanes] += total
        near = [high_wide[j * SIDE : (j + 1) * SIDE, lanes] for j in range(HALO)]
        for j, total in enumerate(convolve([None] * (2 * HALO) + near, taps, lanes, False)):
            start = (COLS - HALO + j) * SIDE
            rows[start : start + SIDE, lanes] += total
    conv_out = rows[...] + vectors[:1, :]
    centre = conv_out - jnp.mean(conv_out, axis=-1, keepdims=True)
    scale = lax.rsqrt(jnp.mean(centre * centre, axis=-1, keepdims=True) + EPSILON)
    inverse[...] = jnp.broadcast_to(scale, inverse.shape)
    standard[...] = centre * scale
    normed[...] = (standard[...] * vectors[SIDE : SIDE + 1, :] + vectors[2 * SIDE : 2 * SIDE + 1, :]).astype(jnp.bfloat16)
    preact[...] = matmul(w_in_t[...], normed[...], NT)

    def step(i, carry):
        part = pl.ds(pl.multiple_of(i * CHUNK, CHUNK), CHUNK)
        for lanes in lane_blocks(preact.shape[1]):
            z = preact[part, lanes] + b_cols[part, :]
            below = 0.5 * (1.0 + lax.erf(z * 0.7071067811865476))
            preact[part, lanes] = z
            cdf[part, lanes] = below
            hidden[part, lanes] = (z * below).astype(jnp.bfloat16)
        return carry

    lax.fori_loop(0, preact.shape[0] // CHUNK, step, 0, unroll=2)
    half = hidden.shape[0] // 2
    other = pl.ds(pl.multiple_of((1 - core[0]) * half, half), half)
    own = pl.ds(pl.multiple_of(core[0] * half, half), half)
    sent[...] = matmul(hidden[other, :], out_grad[...]).astype(jnp.bfloat16)
    kept[...] = matmul(hidden[own, :], out_grad[...])


def slope_kernel(back, preact, cdf, grad_pre):
    def step(i, carry):
        part = pl.ds(pl.multiple_of(i * CHUNK, CHUNK), CHUNK)
        for lanes in lane_blocks(preact.shape[1]):
            z = preact[part, lanes]
            density = jnp.exp(-0.5 * z * z) * 0.3989422804014327
            slope = cdf[part, lanes] + z * density
            grad_pre[part, lanes] = (back[part, lanes] * slope).astype(jnp.bfloat16)
        return carry

    lax.fori_loop(0, preact.shape[0] // CHUNK, step, 0, unroll=2)


def third_kernel(
    core, grad_pre, w_in, normed, standard, inverse, vectors,
    kept, sent, grad_conv, low, high
):
    grad_std = matmul(w_in[...], grad_pre[...]).T * vectors[SIDE : SIDE + 1, :]
    half = grad_pre.shape[0] // 2
    other = pl.ds(pl.multiple_of((1 - core[0]) * half, half), half)
    own = pl.ds(pl.multiple_of(core[0] * half, half), half)
    sent[...] = matmul(grad_pre[other, :], normed[...]).astype(jnp.bfloat16)
    kept[...] = matmul(grad_pre[own, :], normed[...])
    norm = standard[...]
    mean = jnp.mean(grad_std, axis=-1, keepdims=True)
    along = jnp.mean(grad_std * norm, axis=-1, keepdims=True)
    result = inverse[:, :1] * (grad_std - mean - norm * along)
    grad_conv[...] = result
    edge = HALO * SIDE
    low[...] = result[:edge, :]
    high[...] = result[result.shape[0] - edge :, :]


def last_kernel(grad_conv, low, high, taps, cotangent, grad_features, wide):
    for k, lanes in enumerate(lane_blocks(grad_conv.shape[1])):
        for t in range(COLS // SIDE):
            columns = []
            for j in range(t * SIDE - HALO, (t + 1) * SIDE + HALO):
                if j < 0:
                    source, place = low, j + HALO
                elif j >= COLS:
                    source, place = high, j - COLS
                else:
                    source, place = grad_conv, j
                columns.append(source[place * SIDE : (place + 1) * SIDE, lanes])
            for j, total in enumerate(convolve(columns, taps, lanes, True)):
                wide[k, pl.ds(t * SIDE + j, SIDE, stride=COLS), :] = total
        result = cotangent[:, lanes].astype(jnp.float32) + wide[k]
        grad_features[:, lanes] = result.astype(jnp.bfloat16)


def pack_kernel(out_blocks, message, spread):
    members, places, _ = message.shape
    blocks = lane_blocks(out_blocks.shape[2])
    spread[...] = jnp.zeros_like(spread)
    for r in range(ROWS):
        part = slice(r * members, (r + 1) * members)
        for k, lanes in enumerate(blocks):
            summed = out_blocks[0, part, lanes].astype(jnp.float32)
            for i in range(1, out_blocks.shape[0]):
                summed += out_blocks[i, part, lanes].astype(jnp.float32)
            spread[pl.ds(r * len(blocks) + k, members, stride=places), :] = summed
    message[...] = spread[...].reshape(message.shape).astype(jnp.bfloat16)


def add_members(received):
    summed = received[0].astype(jnp.float32)
    for i in range(1, received.shape[0]):
        summed += received[i].astype(jnp.float32)
    return summed


def turn_kernel(scale, received, in_rows, message, spread, total):
    members, places, _ = message.shape
    blocks = lane_blocks(in_rows.shape[1])
    summed = add_members(received) * scale
    spread[...] = jnp.zeros_like(spread)
    size = ROWS * len(blocks)
    for place in range(size):
        row = jnp.broadcast_to(summed[place : place + 1, :], (members, LANES))
        spread[pl.ds(place, members, stride=places), :] = row
    for k, lanes in enumerate(blocks):
        total[k] = in_rows[:, lanes]
        for r in range(ROWS):
            place = size + r * len(blocks) + k
            part = total[k, pl.ds(r, members, stride=ROWS), :]
            spread[pl.ds(place, members, stride=places), :] = part
    message[...] = spread[...].reshape(message.shape).astype(jnp.bfloat16)


def unpack_kernel(scale, received, message, grad_w_in, spread, sums):
    members, places, _ = received.shape
    blocks = lane_blocks(message.shape[2])
    spread[...] = received[...].astype(jnp.float32).reshape(spread.shape)
    for r in range(ROWS):
        for k, lanes in enumerate(blocks):
            part = spread[pl.ds(r * len(blocks) + k, members, stride=places), :]
            part = part.astype(jnp.bfloat16)
            for i in range(message.shape[0]):
                message[i, r * members : (r + 1) * members, lanes] = part
    sums[...] = add_members(received)
    size = ROWS * len(blocks)
    for k, lanes in enumerate(blocks):
        grad_w_in[:, lanes] = sums[pl.ds(size + k, ROWS, stride=len(blocks)), :] * scale


def join_kernel(core, own, other, in_rows, grad_w_out, grad_w_in):
    half = own.shape[0]
    grad_w_out[pl.ds(pl.multiple_of(core[0] * half, half), half), :] = own[...]
    grad_w_out[pl.ds(pl.multiple_of((1 - core[0]) * half, half), half), :] = other[...]
    grad_w_in[...] = in_rows[...]


def call(kernel, outs, scratch, scalars, arrays, flops, nbytes, space=pltpu.VMEM):
    if space == pltpu.HBM:
        arrays = [pltpu.with_memory_space_constraint(array, pltpu.HBM) for array in arrays]
    in_specs = [pl.BlockSpec(memory_space=pltpu.SMEM)] * len(scalars)
    in_specs += [pl.BlockSpec(memory_space=space)] * len(arrays)
    return pl.pallas_call(
        kernel,
        out_shape=[jax.ShapeDtypeStruct(shape, kind) for shape, kind in outs],
        in_specs=in_specs,
        out_specs=[pl.BlockSpec(memory_space=pltpu.VMEM)] * len(outs),
        scratch_shapes=scratch,
        compiler_params=pltpu.CompilerParams(vmem_limit_bytes=VMEM_LIMIT),
        cost_estimate=pl.CostEstimate(flops=flops, bytes_accessed=nbytes, transcendentals=0),
    )(*scalars, *arrays)


F32, B16 = jnp.float32, jnp.bfloat16


def edges(features):
    rows, width = features.shape
    return call(
        edge_kernel,
        [((EDGE, width), B16), ((EDGE, width), B16)],
        [pltpu.VMEM((rows, width), B16), pltpu.VMEM((width // LANES, rows, LANES), F32), pltpu.SemaphoreType.DMA],
        [],
        [features],
        features.size, 2 * features.size, pltpu.HBM,
    )


def before_halos(flags, features, cotangent, kernel, conv_bias, gain, bias, w_in, b_in, w_out, layer_scale):
    rows, width = features.shape
    hidden = w_out.shape[0]
    return call(
        first_kernel,
        [((rows, width), F32), ((rows, width), B16), ((hidden, rows), F32), ((hidden, width), B16),
         ((hidden, LANES), F32), (w_in.shape, B16), (kernel.shape, F32), ((3 * SIDE, width), F32)],
        [pltpu.VMEM((width // LANES, rows, LANES), F32), pltpu.SMEM(flags.shape, jnp.int32),
         pltpu.VMEM((rows, width), B16), pltpu.VMEM((rows, width), B16), pltpu.VMEM(w_out.shape, B16),
         pltpu.VMEM(b_in.shape, F32), pltpu.VMEM((width,), F32), pltpu.VMEM((width,), F32),
         pltpu.VMEM((width,), F32), pltpu.VMEM((width,), F32),
         pltpu.SemaphoreType.DMA((11,))],
        [],
        [flags, features, cotangent, w_out, w_in, b_in, kernel, layer_scale, conv_bias, gain, bias],
        2 * rows * width * hidden, 8 * 1024 * 1024, pltpu.HBM,
    )


def forward(core, conv, low, high, taps, vectors, w_in_t, b_cols, out_grad):
    rows, width = conv.shape
    hidden = w_in_t.shape[0]
    halo = pltpu.VMEM((EDGE, width), F32)
    return call(
        second_kernel,
        [((hidden // 2, width), F32), ((hidden // 2, width), B16), ((rows, width), F32), ((rows, LANES), F32),
         ((rows, width), B16), ((hidden, rows), F32), ((hidden, rows), F32)],
        [pltpu.VMEM((rows, width), F32), halo, halo, pltpu.VMEM((hidden, rows), B16)],
        [core],
        [conv, low, high, taps, vectors, w_in_t, b_cols, out_grad],
        4 * rows * width * hidden, 8 * 1024 * 1024,
    )


def slopes(back, preact, cdf):
    return call(slope_kernel, [(back.shape, B16)], [], [], [back, preact, cdf], 10 * back.size, 14 * back.size)[0]


def backward(core, grad_pre, w_in, normed, standard, inverse, vectors):
    rows, width = standard.shape
    hidden = grad_pre.shape[0]
    edge = (HALO * SIDE, width)
    return call(
        third_kernel,
        [((hidden // 2, width), F32), ((hidden // 2, width), B16), ((rows, width), F32), (edge, F32), (edge, F32)],
        [],
        [core],
        [grad_pre, w_in, normed, standard, inverse, vectors],
        4 * rows * width * hidden, 8 * 1024 * 1024,
    )


def to_features(grad_conv, low, high, taps, cotangent):
    rows, width = grad_conv.shape
    return call(
        last_kernel,
        [((rows, width), B16)],
        [pltpu.VMEM((width // LANES, rows, LANES), F32)],
        [],
        [grad_conv, low, high, taps, cotangent],
        2 * 49 * rows * width, 2 * 1024 * 1024,
    )[0]


def pack(out_blocks, members, places):
    return call(
        pack_kernel,
        [((members, places, LANES), B16)],
        [pltpu.VMEM((members * places, LANES), F32)],
        [],
        [out_blocks],
        out_blocks.size, 3 * out_blocks.size,
    )[0]


def turn(scale, received, in_rows, places):
    members = received.shape[0]
    rows, width = in_rows.shape
    return call(
        functools.partial(turn_kernel, scale),
        [((members, places, LANES), B16)],
        [pltpu.VMEM((members * places, LANES), F32), pltpu.VMEM((width // LANES, rows, LANES), F32)],
        [],
        [received, in_rows],
        received.size, 6 * received.size,
    )[0]


def unpack(scale, received, lines, rows, width):
    return call(
        functools.partial(unpack_kernel, scale),
        [((lines, rows, width), B16), ((ROWS, width), F32)],
        [pltpu.VMEM((received.shape[0] * received.shape[1], LANES), F32), pltpu.VMEM(received.shape[1:], F32)],
        [],
        [received],
        received.size, 6 * received.size,
    )


def join(core, own, other, in_rows):
    rows, width = own.shape
    return call(
        join_kernel, [((2 * rows, width), B16), (in_rows.shape, F32)], [], [core], [own, other, in_rows],
        own.size, 8 * own.size,
    )


def from_left(block):
    count = lax.axis_size(TILE)
    return lax.ppermute(block, TILE, [(i, i + 1) for i in range(count - 1)])


def from_right(block):
    count = lax.axis_size(TILE)
    return lax.ppermute(block, TILE, [(i + 1, i) for i in range(count - 1)])


def exchange(blocks, axes):
    return lax.all_to_all(blocks, axes, split_axis=0, concat_axis=0, tiled=True)


def swap(block):
    return lax.ppermute(block, "c", SWAP)


def owners(sizes):
    zh_n, x_n, y_n, zl_n, c_n = sizes
    pairs = []
    for source in range(zh_n * x_n * y_n * zl_n * c_n):
        rest, c = divmod(source, c_n)
        rest, zl = divmod(rest, zl_n)
        rest, y = divmod(rest, y_n)
        zh, x = divmod(rest, x_n)
        pairs.append((source, (((c * x_n + x) * zh_n + zh) * y_n + y) * zl_n + zl))
    return pairs


def body(
    features, cotangent, kernel, conv_bias, ln_gain, ln_bias, w_in, b_in, w_out, layer_scale, tissue
):
    image = features[0]
    height, breadth, channels = image.shape
    rows = image.reshape(-1, channels)
    low, high = edges(rows)
    low, high = from_left(high), from_right(low)
    upstream = cotangent[0].reshape(-1, channels)
    core = lax.axis_index("c").astype(jnp.int32).reshape(1)
    sizes = [lax.axis_size(axis) for axis in EVERY]
    lines, ring = sizes[1], sizes[0] * sizes[2] * sizes[3]
    scale = 1.0 / math.sqrt(height * breadth * math.prod(sizes))

    conv, out_grad, back, w_in_t, b_cols, w_in_here, taps, vectors = before_halos(
        tissue, rows, upstream, kernel, conv_bias, ln_gain, ln_bias, w_in, b_in, w_out, layer_scale
    )
    kept, sent, standard, inverse, normed, preact, cdf = forward(
        core, conv, low, high, taps, vectors, w_in_t, b_cols, out_grad
    )
    grad_pre = slopes(back, preact, cdf)
    total = (kept + swap(sent).astype(F32)).astype(B16).reshape(lines, -1, channels)
    total, grad_pre = lax.optimization_barrier((total, grad_pre))
    out_blocks = exchange(total, "x")
    kept, sent, grad_conv, low, high = backward(
        core, grad_pre, w_in_here, normed, standard, inverse, vectors
    )
    in_total = kept + swap(sent).astype(F32)
    low, high = from_left(high), from_right(low)
    out_blocks, low, high, _ = lax.optimization_barrier((out_blocks, low, high, in_total))
    in_rows = lax.psum_scatter(in_total, "x", scatter_dimension=0, tiled=True)

    received = exchange(pack(out_blocks, ring, 16), RING)
    received = exchange(turn(scale, received, in_rows, 24), RING)
    message, in_rows = unpack(scale, received, lines, out_blocks.shape[1], channels)
    own = exchange(message, "x").reshape(-1, channels)
    own, in_rows, low, high = lax.optimization_barrier((own, in_rows, low, high))
    other = swap(own)
    in_rows = lax.ppermute(in_rows, EVERY, owners(sizes))
    grad_image = to_features(grad_conv, low, high, taps, upstream)
    grad_w_out, grad_w_in = join(core, own, other, in_rows)
    return (grad_image.reshape(1, height, breadth, channels), grad_w_in, grad_w_out)


def solution(mesh):
    fine = jax.sharding.Mesh(mesh.devices.reshape(4, 4, 8, 2, 2), EVERY)
    band = P(("zl", "c"), None, TILE, None)
    placed = (band, band) + (P(),) * 8 + (P(("zl", "c"), TILE),)
    return jax.shard_map(
        body,
        mesh=fine,
        in_specs=placed,
        out_specs=(band, P(EVERY, None), P()),
        check_vma=False,
    )
```

```python
import functools
import math

import jax
import jax.numpy as jnp
from jax import lax
from jax.experimental import pallas as pl
from jax.experimental.pallas import tpu as pltpu
from jax.sharding import PartitionSpec as P

SIDE = 8
HALO = 3
TAPS = 7
COLS = 32
LANES = 128
CHUNK = 32
ROWS = 3
EDGE = 4 * SIDE
EPSILON = 1e-06
VMEM_LIMIT = 16 * 1024 * 1024
NT = (((1,), (1,)), ((), ()))

TILE = ("zh", "x", "y")
RING = ("zh", "y", "zl")
EVERY = ("zh", "x", "y", "zl", "c")
SWAP = [(0, 1), (1, 0)]


def matmul(left, right, dims=(((1,), (0,)), ((), ()))):
    return lax.dot_general(left, right, dims, preferred_element_type=jnp.float32)


def shifted(column, a):
    move = a - HALO
    if move == 0:
        return column
    row = lax.broadcasted_iota(jnp.int32, column.shape, 0)
    inside = (row + move >= 0) & (row + move < SIDE)
    return jnp.where(inside, pltpu.roll(column, (-move) % SIDE, 0), 0.0)


def convolve(columns, taps, lanes, flip):
    count = len(columns) - 2 * HALO
    totals = [None] * count
    for a in range(TAPS):
        sums = [None] * count
        for e in range(TAPS):
            row, place = (TAPS - 1 - a, TAPS - 1 - e) if flip else (a, e)
            tap = taps[row, place : place + 1, lanes]
            for j in range(count):
                if columns[j + e] is None:
                    continue
                term = columns[j + e] * tap
                sums[j] = term if sums[j] is None else sums[j] + term
        for j in range(count):
            if sums[j] is None:
                continue
            moved = shifted(sums[j], a)
            totals[j] = moved if totals[j] is None else totals[j] + moved
    return totals


def lane_blocks(width):
    return [slice(start, start + LANES) for start in range(0, width, LANES)]


def widen(source, wide):
    for k, lanes in enumerate(lane_blocks(source.shape[1])):
        wide[k] = source[:, lanes].astype(jnp.float32)


def edge_kernel(features, low, high, image, wide, sem):
    copy = pltpu.make_async_copy(features, image, sem)
    copy.start()
    copy.wait()
    widen(image, wide)
    count = EDGE // SIDE
    for k, lanes in enumerate(lane_blocks(features.shape[1])):
        for first, edge in ((0, low), (COLS - count, high)):
            columns = [wide[k, pl.ds(first + j, SIDE, stride=COLS), :] for j in range(count)]
            edge[:, lanes] = jnp.concatenate(columns, axis=0).astype(jnp.bfloat16)


def first_kernel(
    flags, features, cotangent, w_out, w_in, b_in, taps, scale, conv_bias, gain, bias,
    conv, out_grad, back, w_in_t, b_cols, w_in_here, taps_here, vectors,
    wide, flags_here, image, upstream, w_out_here, b_here, scale_here, conv_bias_here, gain_here, bias_here, sems
):
    width = features.shape[1]
    pairs = [
        (flags, flags_here), (cotangent, upstream), (scale, scale_here), (w_out, w_out_here),
        (features, image), (taps, taps_here), (w_in, w_in_here), (b_in, b_here),
        (conv_bias, conv_bias_here), (gain, gain_here), (bias, bias_here),
    ]
    copies = [pltpu.make_async_copy(src, dst, sems.at[i]) for i, (src, dst) in enumerate(pairs)]
    for copy in copies:
        copy.start()
    for copy in copies[:3]:
        copy.wait()
    widen(upstream, wide)
    rows = SIDE * SIDE
    by_lane = scale_here[...].reshape(1, width)
    for k, lanes in enumerate(lane_blocks(width)):
        for t in range(COLS // SIDE):
            gate = flags_here[0, t].astype(jnp.float32)
            tile = jnp.concatenate(
                [wide[k, pl.ds(t * SIDE + j, SIDE, stride=COLS), :] for j in range(SIDE)], axis=0
            )
            tile = (tile * by_lane[:, lanes] * gate).astype(jnp.bfloat16)
            out_grad[t * rows : (t + 1) * rows, lanes] = tile
    copies[3].wait()
    back[...] = matmul(w_out_here[...], out_grad[...], NT)
    copies[4].wait()
    copies[5].wait()
    widen(image, wide)
    for k, lanes in enumerate(lane_blocks(width)):
        for t in range(COLS // SIDE):
            columns = []
            for j in range(t * SIDE - HALO, (t + 1) * SIDE + HALO):
                inside = 0 <= j < COLS
                columns.append(wide[k, pl.ds(j, SIDE, stride=COLS), :] if inside else None)
            for j, total in enumerate(convolve(columns, taps_here, lanes, False)):
                start = (t * SIDE + j) * SIDE
                conv[start : start + SIDE, lanes] = total
    for copy in copies[6:]:
        copy.wait()
    hidden = w_in.shape[1]
    for start in range(0, hidden, LANES):
        w_in_t[start : start + LANES, :] = w_in_here[:, start : start + LANES].T
        b_cols[start : start + LANES, :] = jnp.broadcast_to(
            b_here[start : start + LANES].reshape(1, LANES), (LANES, LANES)
        ).T
    for i, vector in enumerate((conv_bias_here, gain_here, bias_here)):
        vectors[i * SIDE : (i + 1) * SIDE, :] = jnp.broadcast_to(
            vector[...].reshape(1, width), (SIDE, width)
        )


def second_kernel(
    core, conv, low, high, taps, vectors, w_in_t, b_cols, out_grad,
    kept, sent, standard, inverse, normed, preact, cdf, rows, low_wide, high_wide, hidden
):
    width = conv.shape[1]
    rows[...] = conv[...]
    low_wide[...] = low[...].astype(jnp.float32)
    high_wide[...] = high[...].astype(jnp.float32)
    for lanes in lane_blocks(width):
        near = [low_wide[(j + 1) * SIDE : (j + 2) * SIDE, lanes] for j in range(HALO)]
        for j, total in enumerate(convolve(near + [None] * (2 * HALO), taps, lanes, False)):
            rows[j * SIDE : (j + 1) * SIDE, lanes] += total
        near = [high_wide[j * SIDE : (j + 1) * SIDE, lanes] for j in range(HALO)]
        for j, total in enumerate(convolve([None] * (2 * HALO) + near, taps, lanes, False)):
            start = (COLS - HALO + j) * SIDE
            rows[start : start + SIDE, lanes] += total
    conv_out = rows[...] + vectors[:1, :]
    centre = conv_out - jnp.mean(conv_out, axis=-1, keepdims=True)
    scale = lax.rsqrt(jnp.mean(centre * centre, axis=-1, keepdims=True) + EPSILON)
    inverse[...] = jnp.broadcast_to(scale, inverse.shape)
    standard[...] = centre * scale
    normed[...] = (standard[...] * vectors[SIDE : SIDE + 1, :] + vectors[2 * SIDE : 2 * SIDE + 1, :]).astype(jnp.bfloat16)
    preact[...] = matmul(w_in_t[...], normed[...], NT)

    def step(i, carry):
        part = pl.ds(pl.multiple_of(i * CHUNK, CHUNK), CHUNK)
        for lanes in lane_blocks(preact.shape[1]):
            z = preact[part, lanes] + b_cols[part, :]
            below = 0.5 * (1.0 + lax.erf(z * 0.7071067811865476))
            preact[part, lanes] = z
            cdf[part, lanes] = below
            hidden[part, lanes] = (z * below).astype(jnp.bfloat16)
        return carry

    lax.fori_loop(0, preact.shape[0] // CHUNK, step, 0, unroll=2)
    half = hidden.shape[0] // 2
    other = pl.ds(pl.multiple_of((1 - core[0]) * half, half), half)
    own = pl.ds(pl.multiple_of(core[0] * half, half), half)
    sent[...] = matmul(hidden[other, :], out_grad[...]).astype(jnp.bfloat16)
    kept[...] = matmul(hidden[own, :], out_grad[...])


def slope_kernel(back, preact, cdf, grad_pre):
    def step(i, carry):
        part = pl.ds(pl.multiple_of(i * CHUNK, CHUNK), CHUNK)
        for lanes in lane_blocks(preact.shape[1]):
            z = preact[part, lanes]
            density = jnp.exp(-0.5 * z * z) * 0.3989422804014327
            slope = cdf[part, lanes] + z * density
            grad_pre[part, lanes] = (back[part, lanes] * slope).astype(jnp.bfloat16)
        return carry

    lax.fori_loop(0, preact.shape[0] // CHUNK, step, 0, unroll=2)


def third_kernel(
    core, grad_pre, w_in, normed, standard, inverse, vectors,
    kept, sent, grad_conv, low, high
):
    grad_std = matmul(w_in[...], grad_pre[...]).T * vectors[SIDE : SIDE + 1, :]
    half = grad_pre.shape[0] // 2
    other = pl.ds(pl.multiple_of((1 - core[0]) * half, half), half)
    own = pl.ds(pl.multiple_of(core[0] * half, half), half)
    sent[...] = matmul(grad_pre[other, :], normed[...]).astype(jnp.bfloat16)
    kept[...] = matmul(grad_pre[own, :], normed[...])
    norm = standard[...]
    mean = jnp.mean(grad_std, axis=-1, keepdims=True)
    along = jnp.mean(grad_std * norm, axis=-1, keepdims=True)
    result = inverse[:, :1] * (grad_std - mean - norm * along)
    grad_conv[...] = result
    edge = HALO * SIDE
    low[...] = result[:edge, :]
    high[...] = result[result.shape[0] - edge :, :]


def last_kernel(grad_conv, low, high, taps, cotangent, grad_features, wide):
    for k, lanes in enumerate(lane_blocks(grad_conv.shape[1])):
        for t in range(COLS // SIDE):
            columns = []
            for j in range(t * SIDE - HALO, (t + 1) * SIDE + HALO):
                if j < 0:
                    source, place = low, j + HALO
                elif j >= COLS:
                    source, place = high, j - COLS
                else:
                    source, place = grad_conv, j
                columns.append(source[place * SIDE : (place + 1) * SIDE, lanes])
            for j, total in enumerate(convolve(columns, taps, lanes, True)):
                wide[k, pl.ds(t * SIDE + j, SIDE, stride=COLS), :] = total
        result = cotangent[:, lanes].astype(jnp.float32) + wide[k]
        grad_features[:, lanes] = result.astype(jnp.bfloat16)


def pack_kernel(out_blocks, message, spread):
    members, places, _ = message.shape
    blocks = lane_blocks(out_blocks.shape[2])
    spread[...] = jnp.zeros_like(spread)
    for r in range(ROWS):
        part = slice(r * members, (r + 1) * members)
        for k, lanes in enumerate(blocks):
            summed = out_blocks[0, part, lanes].astype(jnp.float32)
            for i in range(1, out_blocks.shape[0]):
                summed += out_blocks[i, part, lanes].astype(jnp.float32)
            spread[pl.ds(r * len(blocks) + k, members, stride=places), :] = summed
    message[...] = spread[...].reshape(message.shape).astype(jnp.bfloat16)


def add_members(received):
    summed = received[0].astype(jnp.float32)
    for i in range(1, received.shape[0]):
        summed += received[i].astype(jnp.float32)
    return summed


def lines_kernel(place, kept, received, own, first, second, third):
    rows = own.shape[0]
    for d, block in enumerate((own, first, second, third)):
        part = pl.ds(pl.multiple_of((place[0] ^ d) * rows, rows), rows)
        block[...] = (kept[part, :] + received[part, :].astype(jnp.float32)).astype(block.dtype)


def turn_kernel(scale, received, own, first, second, third, message, spread, total):
    members, places, _ = message.shape
    blocks = lane_blocks(own.shape[1])
    finished = add_members(received) * scale
    spread[...] = jnp.zeros_like(spread)
    size = ROWS * len(blocks)
    for place in range(size):
        row = jnp.broadcast_to(finished[place : place + 1, :], (members, LANES))
        spread[pl.ds(place, members, stride=places), :] = row
    for k, lanes in enumerate(blocks):
        summed = own[:, lanes]
        for block in (first, second, third):
            summed = summed + block[:, lanes].astype(jnp.float32)
        total[k] = summed
        for r in range(ROWS):
            place = size + r * len(blocks) + k
            part = total[k, pl.ds(r, members, stride=ROWS), :]
            spread[pl.ds(place, members, stride=places), :] = part
    message[...] = spread[...].reshape(message.shape).astype(jnp.bfloat16)


def unpack_kernel(scale, received, message, grad_w_in, spread, sums):
    members, places, _ = received.shape
    blocks = lane_blocks(message.shape[2])
    spread[...] = received[...].astype(jnp.float32).reshape(spread.shape)
    for r in range(ROWS):
        for k, lanes in enumerate(blocks):
            part = spread[pl.ds(r * len(blocks) + k, members, stride=places), :]
            part = part.astype(jnp.bfloat16)
            for i in range(message.shape[0]):
                message[i, r * members : (r + 1) * members, lanes] = part
    sums[...] = add_members(received)
    size = ROWS * len(blocks)
    for k, lanes in enumerate(blocks):
        grad_w_in[:, lanes] = sums[pl.ds(size + k, ROWS, stride=len(blocks)), :] * scale


def join_kernel(core, own, other, in_rows, grad_w_out, grad_w_in):
    half = own.shape[0]
    grad_w_out[pl.ds(pl.multiple_of(core[0] * half, half), half), :] = own[...]
    grad_w_out[pl.ds(pl.multiple_of((1 - core[0]) * half, half), half), :] = other[...]
    grad_w_in[...] = in_rows[...]


def call(kernel, outs, scratch, scalars, arrays, flops, nbytes, space=pltpu.VMEM):
    if space == pltpu.HBM:
        arrays = [pltpu.with_memory_space_constraint(array, pltpu.HBM) for array in arrays]
    in_specs = [pl.BlockSpec(memory_space=pltpu.SMEM)] * len(scalars)
    in_specs += [pl.BlockSpec(memory_space=space)] * len(arrays)
    return pl.pallas_call(
        kernel,
        out_shape=[jax.ShapeDtypeStruct(shape, kind) for shape, kind in outs],
        in_specs=in_specs,
        out_specs=[pl.BlockSpec(memory_space=pltpu.VMEM)] * len(outs),
        scratch_shapes=scratch,
        compiler_params=pltpu.CompilerParams(vmem_limit_bytes=VMEM_LIMIT),
        cost_estimate=pl.CostEstimate(flops=flops, bytes_accessed=nbytes, transcendentals=0),
    )(*scalars, *arrays)


F32, B16 = jnp.float32, jnp.bfloat16


def edges(features):
    rows, width = features.shape
    return call(
        edge_kernel,
        [((EDGE, width), B16), ((EDGE, width), B16)],
        [pltpu.VMEM((rows, width), B16), pltpu.VMEM((width // LANES, rows, LANES), F32), pltpu.SemaphoreType.DMA],
        [],
        [features],
        features.size, 2 * features.size, pltpu.HBM,
    )


def before_halos(flags, features, cotangent, kernel, conv_bias, gain, bias, w_in, b_in, w_out, layer_scale):
    rows, width = features.shape
    hidden = w_out.shape[0]
    return call(
        first_kernel,
        [((rows, width), F32), ((rows, width), B16), ((hidden, rows), F32), ((hidden, width), B16),
         ((hidden, LANES), F32), (w_in.shape, B16), (kernel.shape, F32), ((3 * SIDE, width), F32)],
        [pltpu.VMEM((width // LANES, rows, LANES), F32), pltpu.SMEM(flags.shape, jnp.int32),
         pltpu.VMEM((rows, width), B16), pltpu.VMEM((rows, width), B16), pltpu.VMEM(w_out.shape, B16),
         pltpu.VMEM(b_in.shape, F32), pltpu.VMEM((width,), F32), pltpu.VMEM((width,), F32),
         pltpu.VMEM((width,), F32), pltpu.VMEM((width,), F32),
         pltpu.SemaphoreType.DMA((11,))],
        [],
        [flags, features, cotangent, w_out, w_in, b_in, kernel, layer_scale, conv_bias, gain, bias],
        2 * rows * width * hidden, 8 * 1024 * 1024, pltpu.HBM,
    )


def forward(core, conv, low, high, taps, vectors, w_in_t, b_cols, out_grad):
    rows, width = conv.shape
    hidden = w_in_t.shape[0]
    halo = pltpu.VMEM((EDGE, width), F32)
    return call(
        second_kernel,
        [((hidden // 2, width), F32), ((hidden // 2, width), B16), ((rows, width), F32), ((rows, LANES), F32),
         ((rows, width), B16), ((hidden, rows), F32), ((hidden, rows), F32)],
        [pltpu.VMEM((rows, width), F32), halo, halo, pltpu.VMEM((hidden, rows), B16)],
        [core],
        [conv, low, high, taps, vectors, w_in_t, b_cols, out_grad],
        4 * rows * width * hidden, 8 * 1024 * 1024,
    )


def slopes(back, preact, cdf):
    return call(slope_kernel, [(back.shape, B16)], [], [], [back, preact, cdf], 10 * back.size, 14 * back.size)[0]


def backward(core, grad_pre, w_in, normed, standard, inverse, vectors):
    rows, width = standard.shape
    hidden = grad_pre.shape[0]
    edge = (HALO * SIDE, width)
    return call(
        third_kernel,
        [((hidden // 2, width), F32), ((hidden // 2, width), B16), ((rows, width), F32), (edge, F32), (edge, F32)],
        [],
        [core],
        [grad_pre, w_in, normed, standard, inverse, vectors],
        4 * rows * width * hidden, 8 * 1024 * 1024,
    )


def to_features(grad_conv, low, high, taps, cotangent):
    rows, width = grad_conv.shape
    return call(
        last_kernel,
        [((rows, width), B16)],
        [pltpu.VMEM((width // LANES, rows, LANES), F32)],
        [],
        [grad_conv, low, high, taps, cotangent],
        2 * 49 * rows * width, 2 * 1024 * 1024,
    )[0]


def pack(out_blocks, members, places):
    return call(
        pack_kernel,
        [((members, places, LANES), B16)],
        [pltpu.VMEM((members * places, LANES), F32)],
        [],
        [out_blocks],
        out_blocks.size, 3 * out_blocks.size,
    )[0]


def split_lines(place, kept, received, lines):
    rows, width = kept.shape
    block = (rows // lines, width)
    return call(
        lines_kernel, [(block, F32)] + [(block, B16)] * 3, [], [place], [kept, received],
        kept.size, 4 * kept.size,
    )


def turn(scale, received, in_blocks, places):
    members = received.shape[0]
    rows, width = in_blocks[0].shape
    return call(
        functools.partial(turn_kernel, scale),
        [((members, places, LANES), B16)],
        [pltpu.VMEM((members * places, LANES), F32), pltpu.VMEM((width // LANES, rows, LANES), F32)],
        [],
        [received, *in_blocks],
        received.size, 6 * received.size,
    )[0]


def unpack(scale, received, lines, rows, width):
    return call(
        functools.partial(unpack_kernel, scale),
        [((lines, rows, width), B16), ((ROWS, width), F32)],
        [pltpu.VMEM((received.shape[0] * received.shape[1], LANES), F32), pltpu.VMEM(received.shape[1:], F32)],
        [],
        [received],
        received.size, 6 * received.size,
    )


def join(core, own, other, in_rows):
    rows, width = own.shape
    return call(
        join_kernel, [((2 * rows, width), B16), (in_rows.shape, F32)], [], [core], [own, other, in_rows],
        own.size, 8 * own.size,
    )


def from_left(block):
    count = lax.axis_size(TILE)
    return lax.ppermute(block, TILE, [(i, i + 1) for i in range(count - 1)])


def from_right(block):
    count = lax.axis_size(TILE)
    return lax.ppermute(block, TILE, [(i + 1, i) for i in range(count - 1)])


def exchange(blocks, axes):
    return lax.all_to_all(blocks, axes, split_axis=0, concat_axis=0, tiled=True)


def swap(block):
    return lax.ppermute(block, "c", SWAP)


def owners(sizes):
    zh_n, x_n, y_n, zl_n, c_n = sizes
    pairs = []
    for source in range(zh_n * x_n * y_n * zl_n * c_n):
        rest, c = divmod(source, c_n)
        rest, zl = divmod(rest, zl_n)
        rest, y = divmod(rest, y_n)
        zh, x = divmod(rest, x_n)
        pairs.append((source, (((c * x_n + x) * zh_n + zh) * y_n + y) * zl_n + zl))
    return pairs


def body(
    features, cotangent, kernel, conv_bias, ln_gain, ln_bias, w_in, b_in, w_out, layer_scale, tissue
):
    image = features[0]
    height, breadth, channels = image.shape
    rows = image.reshape(-1, channels)
    low, high = edges(rows)
    low, high = from_left(high), from_right(low)
    upstream = cotangent[0].reshape(-1, channels)
    core = lax.axis_index("c").astype(jnp.int32).reshape(1)
    sizes = [lax.axis_size(axis) for axis in EVERY]
    lines, ring = sizes[1], sizes[0] * sizes[2] * sizes[3]
    scale = 1.0 / math.sqrt(height * breadth * math.prod(sizes))

    conv, out_grad, back, w_in_t, b_cols, w_in_here, taps, vectors = before_halos(
        tissue, rows, upstream, kernel, conv_bias, ln_gain, ln_bias, w_in, b_in, w_out, layer_scale
    )
    kept, sent, standard, inverse, normed, preact, cdf = forward(
        core, conv, low, high, taps, vectors, w_in_t, b_cols, out_grad
    )
    grad_pre = slopes(back, preact, cdf)
    total = (kept + swap(sent).astype(F32)).astype(B16).reshape(lines, -1, channels)
    total, grad_pre = lax.optimization_barrier((total, grad_pre))
    out_blocks = exchange(total, "x")
    kept, sent, grad_conv, low, high = backward(
        core, grad_pre, w_in_here, normed, standard, inverse, vectors
    )
    line = lax.axis_index("x").astype(jnp.int32).reshape(1)
    own, *others = split_lines(line, kept, swap(sent), lines)
    low, high = from_left(high), from_right(low)

    out_blocks, *_ = lax.optimization_barrier((out_blocks, *others))
    pairs = [[(i, i ^ d) for i in range(lines)] for d in range(1, lines)]
    in_blocks = [own] + [lax.ppermute(block, "x", pair) for block, pair in zip(others, pairs)]
    received = exchange(pack(out_blocks, ring, 16), RING)
    received, low, high = lax.optimization_barrier((received, low, high))
    grad_image = to_features(grad_conv, low, high, taps, upstream)
    received = exchange(turn(scale, received, in_blocks, 24), RING)
    received, grad_image = lax.optimization_barrier((received, grad_image))
    message, in_rows = unpack(scale, received, lines, out_blocks.shape[1], channels)
    own = exchange(message, "x").reshape(-1, channels)
    own, in_rows = lax.optimization_barrier((own, in_rows))
    other = swap(own)
    in_rows = lax.ppermute(in_rows, EVERY, owners(sizes))
    grad_w_out, grad_w_in = join(core, own, other, in_rows)
    return (grad_image.reshape(1, height, breadth, channels), grad_w_in, grad_w_out)


def solution(mesh):
    fine = jax.sharding.Mesh(mesh.devices.reshape(4, 4, 8, 2, 2), EVERY)
    band = P(("zl", "c"), None, TILE, None)
    placed = (band, band) + (P(),) * 8 + (P(("zl", "c"), TILE),)
    return jax.shard_map(
        body,
        mesh=fine,
        in_specs=placed,
        out_specs=(band, P(EVERY, None), P()),
        check_vma=False,
    )
```

```python
import functools
import math

import jax
import jax.numpy as jnp
from jax import lax
from jax.experimental import pallas as pl
from jax.experimental.pallas import tpu as pltpu
from jax.sharding import PartitionSpec as P

SIDE = 8
HALO = 3
TAPS = 7
COLS = 32
LANES = 128
CHUNK = 32
ROWS = 3
EDGE = 4 * SIDE
EPSILON = 1e-06
VMEM_LIMIT = 16 * 1024 * 1024
NT = (((1,), (1,)), ((), ()))

TILE = ("zh", "xh", "xl", "yh", "yl")
CUBE = ("xl", "yl", "zl")
FAR = ("zh", "xh", "yh")
EVERY = ("zh", "xh", "xl", "yh", "yl", "zl", "c")
SWAP = [(0, 1), (1, 0)]


def matmul(left, right, dims=(((1,), (0,)), ((), ()))):
    return lax.dot_general(left, right, dims, preferred_element_type=jnp.float32)


def shifted(column, a):
    move = a - HALO
    if move == 0:
        return column
    row = lax.broadcasted_iota(jnp.int32, column.shape, 0)
    inside = (row + move >= 0) & (row + move < SIDE)
    return jnp.where(inside, pltpu.roll(column, (-move) % SIDE, 0), 0.0)


def convolve(columns, taps, lanes, flip):
    count = len(columns) - 2 * HALO
    totals = [None] * count
    for a in range(TAPS):
        sums = [None] * count
        for e in range(TAPS):
            row, place = (TAPS - 1 - a, TAPS - 1 - e) if flip else (a, e)
            tap = taps[row, place : place + 1, lanes]
            for j in range(count):
                if columns[j + e] is None:
                    continue
                term = columns[j + e] * tap
                sums[j] = term if sums[j] is None else sums[j] + term
        for j in range(count):
            if sums[j] is None:
                continue
            moved = shifted(sums[j], a)
            totals[j] = moved if totals[j] is None else totals[j] + moved
    return totals


def lane_blocks(width):
    return [slice(start, start + LANES) for start in range(0, width, LANES)]


def widen(source, wide):
    for k, lanes in enumerate(lane_blocks(source.shape[1])):
        wide[k] = source[:, lanes].astype(jnp.float32)


def edge_kernel(features, low, high, image, wide, sem):
    copy = pltpu.make_async_copy(features, image, sem)
    copy.start()
    copy.wait()
    widen(image, wide)
    count = EDGE // SIDE
    for k, lanes in enumerate(lane_blocks(features.shape[1])):
        for first, edge in ((0, low), (COLS - count, high)):
            columns = [wide[k, pl.ds(first + j, SIDE, stride=COLS), :] for j in range(count)]
            edge[:, lanes] = jnp.concatenate(columns, axis=0).astype(jnp.bfloat16)


def first_kernel(
    flags, features, cotangent, w_out, w_in, b_in, taps, scale, conv_bias, gain, bias,
    conv, out_grad, back, w_in_t, b_cols, w_in_here, taps_here, vectors,
    wide, flags_here, image, upstream, w_out_here, b_here, scale_here, conv_bias_here, gain_here, bias_here, sems
):
    width = features.shape[1]
    pairs = [
        (flags, flags_here), (cotangent, upstream), (scale, scale_here), (w_out, w_out_here),
        (features, image), (taps, taps_here), (w_in, w_in_here), (b_in, b_here),
        (conv_bias, conv_bias_here), (gain, gain_here), (bias, bias_here),
    ]
    copies = [pltpu.make_async_copy(src, dst, sems.at[i]) for i, (src, dst) in enumerate(pairs)]
    for copy in copies:
        copy.start()
    for copy in copies[:3]:
        copy.wait()
    widen(upstream, wide)
    rows = SIDE * SIDE
    by_lane = scale_here[...].reshape(1, width)
    for k, lanes in enumerate(lane_blocks(width)):
        for t in range(COLS // SIDE):
            gate = flags_here[0, t].astype(jnp.float32)
            tile = jnp.concatenate(
                [wide[k, pl.ds(t * SIDE + j, SIDE, stride=COLS), :] for j in range(SIDE)], axis=0
            )
            tile = (tile * by_lane[:, lanes] * gate).astype(jnp.bfloat16)
            out_grad[t * rows : (t + 1) * rows, lanes] = tile
    copies[3].wait()
    back[...] = matmul(w_out_here[...], out_grad[...], NT)
    copies[4].wait()
    copies[5].wait()
    widen(image, wide)
    for k, lanes in enumerate(lane_blocks(width)):
        for t in range(COLS // SIDE):
            columns = []
            for j in range(t * SIDE - HALO, (t + 1) * SIDE + HALO):
                inside = 0 <= j < COLS
                columns.append(wide[k, pl.ds(j, SIDE, stride=COLS), :] if inside else None)
            for j, total in enumerate(convolve(columns, taps_here, lanes, False)):
                start = (t * SIDE + j) * SIDE
                conv[start : start + SIDE, lanes] = total
    for copy in copies[6:]:
        copy.wait()
    hidden = w_in.shape[1]
    for start in range(0, hidden, LANES):
        w_in_t[start : start + LANES, :] = w_in_here[:, start : start + LANES].T
        b_cols[start : start + LANES, :] = jnp.broadcast_to(
            b_here[start : start + LANES].reshape(1, LANES), (LANES, LANES)
        ).T
    for i, vector in enumerate((conv_bias_here, gain_here, bias_here)):
        vectors[i * SIDE : (i + 1) * SIDE, :] = jnp.broadcast_to(
            vector[...].reshape(1, width), (SIDE, width)
        )


def middle_kernel(
    core, conv, low, high, taps, vectors, w_in_t, b_cols, out_grad, back, w_in,
    kept, sent, grad_conv, low_edge, high_edge,
    rows, low_wide, high_wide, standard, normed, preact, hidden, grad_pre
):
    width = conv.shape[1]
    rows[...] = conv[...]
    low_wide[...] = low[...].astype(jnp.float32)
    high_wide[...] = high[...].astype(jnp.float32)
    for lanes in lane_blocks(width):
        near = [low_wide[(j + 1) * SIDE : (j + 2) * SIDE, lanes] for j in range(HALO)]
        for j, total in enumerate(convolve(near + [None] * (2 * HALO), taps, lanes, False)):
            rows[j * SIDE : (j + 1) * SIDE, lanes] += total
        near = [high_wide[j * SIDE : (j + 1) * SIDE, lanes] for j in range(HALO)]
        for j, total in enumerate(convolve([None] * (2 * HALO) + near, taps, lanes, False)):
            start = (COLS - HALO + j) * SIDE
            rows[start : start + SIDE, lanes] += total
    gain, bias = vectors[SIDE : SIDE + 1, :], vectors[2 * SIDE : 2 * SIDE + 1, :]
    conv_out = rows[...] + vectors[:1, :]
    centre = conv_out - jnp.mean(conv_out, axis=-1, keepdims=True)
    inverse = lax.rsqrt(jnp.mean(centre * centre, axis=-1, keepdims=True) + EPSILON)
    standard[...] = centre * inverse
    normed[...] = (standard[...] * gain + bias).astype(jnp.bfloat16)
    preact[...] = matmul(w_in_t[...], normed[...], NT)

    def step(i, carry):
        part = pl.ds(pl.multiple_of(i * CHUNK, CHUNK), CHUNK)
        for lanes in lane_blocks(preact.shape[1]):
            z = preact[part, lanes] + b_cols[part, :]
            below = 0.5 * (1.0 + lax.erf(z * 0.7071067811865476))
            density = jnp.exp(-0.5 * z * z) * 0.3989422804014327
            hidden[part, lanes] = (z * below).astype(jnp.bfloat16)
            slope = below + z * density
            grad_pre[part, lanes] = (back[part, lanes] * slope).astype(jnp.bfloat16)
        return carry

    lax.fori_loop(0, preact.shape[0] // CHUNK, step, 0, unroll=2)
    half = hidden.shape[0] // 2
    other = pl.ds(pl.multiple_of((1 - core[0]) * half, half), half)
    own = pl.ds(pl.multiple_of(core[0] * half, half), half)
    sent[:half, :] = matmul(hidden[other, :], out_grad[...]).astype(jnp.bfloat16)
    sent[half:, :] = matmul(grad_pre[other, :], normed[...]).astype(jnp.bfloat16)
    kept[:half, :] = matmul(hidden[own, :], out_grad[...])
    kept[half:, :] = matmul(grad_pre[own, :], normed[...])
    grad_std = matmul(w_in[...], grad_pre[...]).T * gain
    norm = standard[...]
    mean = jnp.mean(grad_std, axis=-1, keepdims=True)
    along = jnp.mean(grad_std * norm, axis=-1, keepdims=True)
    result = inverse * (grad_std - mean - norm * along)
    grad_conv[...] = result
    edge = HALO * SIDE
    low_edge[...] = result[:edge, :]
    high_edge[...] = result[result.shape[0] - edge :, :]


def last_kernel(grad_conv, low, high, taps, cotangent, grad_features, wide):
    for k, lanes in enumerate(lane_blocks(grad_conv.shape[1])):
        for t in range(COLS // SIDE):
            columns = []
            for j in range(t * SIDE - HALO, (t + 1) * SIDE + HALO):
                if j < 0:
                    source, place = low, j + HALO
                elif j >= COLS:
                    source, place = high, j - COLS
                else:
                    source, place = grad_conv, j
                columns.append(source[place * SIDE : (place + 1) * SIDE, lanes])
            for j, total in enumerate(convolve(columns, taps, lanes, True)):
                wide[k, pl.ds(t * SIDE + j, SIDE, stride=COLS), :] = total
        result = cotangent[:, lanes].astype(jnp.float32) + wide[k]
        grad_features[:, lanes] = result.astype(jnp.bfloat16)


def cube_kernel(kept, received, message):
    members, rows, _ = message.shape
    rows //= 2
    for m in range(members):
        for i in range(2):
            start = (i * members + m) * rows
            part = slice(start, start + rows)
            total = kept[part, :] + received[part, :].astype(jnp.float32)
            message[m, i * rows : (i + 1) * rows, :] = total.astype(jnp.bfloat16)


def add_members(received):
    summed = received[0].astype(jnp.float32)
    for i in range(1, received.shape[0]):
        summed += received[i].astype(jnp.float32)
    return summed


def far_kernel(received, message, spread, total):
    members, places, _ = message.shape
    blocks = lane_blocks(received.shape[2])
    rows = ROWS * members
    size = ROWS * len(blocks)
    spread[...] = jnp.zeros_like(spread)
    for k, lanes in enumerate(blocks):
        summed = received[0, :, lanes].astype(jnp.float32)
        for i in range(1, received.shape[0]):
            summed += received[i, :, lanes].astype(jnp.float32)
        total[k] = summed
        for r in range(ROWS):
            place = r * len(blocks) + k
            part = total[k, r * members : (r + 1) * members, :]
            spread[pl.ds(place, members, stride=places), :] = part
            part = total[k, pl.ds(rows + r, members, stride=ROWS), :]
            spread[pl.ds(size + place, members, stride=places), :] = part
    message[...] = spread[...].reshape(message.shape).astype(jnp.bfloat16)


def turn_kernel(scale, received, message, grad_w_in, sums):
    sums[...] = add_members(received) * scale
    width = grad_w_in.shape[1]
    blocks = lane_blocks(width)
    size = ROWS * len(blocks)
    for k, lanes in enumerate(blocks):
        grad_w_in[:, lanes] = sums[pl.ds(size + k, ROWS, stride=len(blocks)), :]
    finished = sums[: message.shape[1], :].astype(jnp.bfloat16)
    for m in range(message.shape[0]):
        message[m] = finished


def unpack_kernel(received, message, spread):
    members, places, _ = received.shape
    blocks = lane_blocks(message.shape[2])
    spread[...] = received[...].astype(jnp.float32).reshape(spread.shape)
    for r in range(ROWS):
        for k, lanes in enumerate(blocks):
            part = spread[pl.ds(r * len(blocks) + k, members, stride=places), :]
            part = part.astype(jnp.bfloat16)
            for i in range(message.shape[0]):
                message[i, r * members : (r + 1) * members, lanes] = part


def join_kernel(core, own, other, in_rows, grad_w_out, grad_w_in):
    half = own.shape[0]
    grad_w_out[pl.ds(pl.multiple_of(core[0] * half, half), half), :] = own[...]
    grad_w_out[pl.ds(pl.multiple_of((1 - core[0]) * half, half), half), :] = other[...]
    grad_w_in[...] = in_rows[...]


def call(kernel, outs, scratch, scalars, arrays, flops, nbytes, space=pltpu.VMEM):
    if space == pltpu.HBM:
        arrays = [pltpu.with_memory_space_constraint(array, pltpu.HBM) for array in arrays]
    in_specs = [pl.BlockSpec(memory_space=pltpu.SMEM)] * len(scalars)
    in_specs += [pl.BlockSpec(memory_space=space)] * len(arrays)
    return pl.pallas_call(
        kernel,
        out_shape=[jax.ShapeDtypeStruct(shape, kind) for shape, kind in outs],
        in_specs=in_specs,
        out_specs=[pl.BlockSpec(memory_space=pltpu.VMEM)] * len(outs),
        scratch_shapes=scratch,
        compiler_params=pltpu.CompilerParams(vmem_limit_bytes=VMEM_LIMIT),
        cost_estimate=pl.CostEstimate(flops=flops, bytes_accessed=nbytes, transcendentals=0),
    )(*scalars, *arrays)


F32, B16 = jnp.float32, jnp.bfloat16


def edges(features):
    rows, width = features.shape
    return call(
        edge_kernel,
        [((EDGE, width), B16), ((EDGE, width), B16)],
        [pltpu.VMEM((rows, width), B16), pltpu.VMEM((width // LANES, rows, LANES), F32), pltpu.SemaphoreType.DMA],
        [],
        [features],
        features.size, 2 * features.size, pltpu.HBM,
    )


def before_halos(flags, features, cotangent, kernel, conv_bias, gain, bias, w_in, b_in, w_out, layer_scale):
    rows, width = features.shape
    hidden = w_out.shape[0]
    return call(
        first_kernel,
        [((rows, width), F32), ((rows, width), B16), ((hidden, rows), F32), ((hidden, width), B16),
         ((hidden, LANES), F32), (w_in.shape, B16), (kernel.shape, F32), ((3 * SIDE, width), F32)],
        [pltpu.VMEM((width // LANES, rows, LANES), F32), pltpu.SMEM(flags.shape, jnp.int32),
         pltpu.VMEM((rows, width), B16), pltpu.VMEM((rows, width), B16), pltpu.VMEM(w_out.shape, B16),
         pltpu.VMEM(b_in.shape, F32), pltpu.VMEM((width,), F32), pltpu.VMEM((width,), F32),
         pltpu.VMEM((width,), F32), pltpu.VMEM((width,), F32),
         pltpu.SemaphoreType.DMA((11,))],
        [],
        [flags, features, cotangent, w_out, w_in, b_in, kernel, layer_scale, conv_bias, gain, bias],
        2 * rows * width * hidden, 8 * 1024 * 1024, pltpu.HBM,
    )


def middle(core, conv, low, high, taps, vectors, w_in_t, b_cols, out_grad, back, w_in):
    rows, width = conv.shape
    hidden = w_in_t.shape[0]
    halo, edge = pltpu.VMEM((EDGE, width), F32), (HALO * SIDE, width)
    return call(
        middle_kernel,
        [((hidden, width), F32), ((hidden, width), B16), ((rows, width), F32), (edge, F32), (edge, F32)],
        [pltpu.VMEM((rows, width), F32), halo, halo, pltpu.VMEM((rows, width), F32), pltpu.VMEM((rows, width), B16),
         pltpu.VMEM((hidden, rows), F32), pltpu.VMEM((hidden, rows), B16), pltpu.VMEM((hidden, rows), B16)],
        [core],
        [conv, low, high, taps, vectors, w_in_t, b_cols, out_grad, back, w_in],
        8 * rows * width * hidden, 12 * 1024 * 1024,
    )


def to_features(grad_conv, low, high, taps, cotangent):
    rows, width = grad_conv.shape
    return call(
        last_kernel,
        [((rows, width), B16)],
        [pltpu.VMEM((width // LANES, rows, LANES), F32)],
        [],
        [grad_conv, low, high, taps, cotangent],
        2 * 49 * rows * width, 2 * 1024 * 1024,
    )[0]


def to_cube(members, kept, received):
    rows, width = kept.shape
    return call(
        cube_kernel, [((members, rows // members, width), B16)], [], [], [kept, received], 2 * kept.size, 8 * kept.size
    )[0]


def to_far(received, members):
    _, rows, width = received.shape
    return call(
        far_kernel,
        [((members, 24, LANES), B16)],
        [pltpu.VMEM((members * 24, LANES), F32), pltpu.VMEM((width // LANES, rows, LANES), F32)],
        [],
        [received],
        received.size, 3 * received.size,
    )[0]


def turn(scale, received, width):
    members, places, _ = received.shape
    return call(
        functools.partial(turn_kernel, scale),
        [((members, 16, LANES), B16), ((ROWS, width), F32)],
        [pltpu.VMEM((places, LANES), F32)],
        [],
        [received],
        received.size, 4 * received.size,
    )


def unpack(received, members, width):
    return call(
        unpack_kernel,
        [((members, ROWS * received.shape[0], width), B16)],
        [pltpu.VMEM((received.shape[0] * received.shape[1], LANES), F32)],
        [],
        [received],
        received.size, 6 * received.size,
    )[0]


def join(core, own, other, in_rows):
    rows, width = own.shape
    return call(
        join_kernel, [((2 * rows, width), B16), (in_rows.shape, F32)], [], [core], [own, other, in_rows],
        own.size, 8 * own.size,
    )


def from_left(block):
    count = lax.axis_size(TILE)
    return lax.ppermute(block, TILE, [(i, i + 1) for i in range(count - 1)])


def from_right(block):
    count = lax.axis_size(TILE)
    return lax.ppermute(block, TILE, [(i + 1, i) for i in range(count - 1)])


def exchange(blocks, axes):
    return lax.all_to_all(blocks, axes, split_axis=0, concat_axis=0, tiled=True)


def swap(block):
    return lax.ppermute(block, "c", SWAP)


def owners(sizes):
    count = math.prod(sizes.values())
    pairs = []
    for source in range(count):
        rest, at = source, {}
        for axis in reversed(EVERY):
            rest, at[axis] = divmod(rest, sizes[axis])
        target = 0
        for axis in ("c",) + CUBE + FAR:
            target = target * sizes[axis] + at[axis]
        pairs.append((source, target))
    return pairs


def body(
    features, cotangent, kernel, conv_bias, ln_gain, ln_bias, w_in, b_in, w_out, layer_scale, tissue
):
    image = features[0]
    height, breadth, channels = image.shape
    rows = image.reshape(-1, channels)
    low, high = edges(rows)
    low, high = from_left(high), from_right(low)
    upstream = cotangent[0].reshape(-1, channels)
    core = lax.axis_index("c").astype(jnp.int32).reshape(1)
    sizes = {axis: lax.axis_size(axis) for axis in EVERY}
    near = math.prod(sizes[axis] for axis in CUBE)
    far = math.prod(sizes[axis] for axis in FAR)
    scale = 1.0 / math.sqrt(height * breadth * math.prod(sizes.values()))

    conv, out_grad, back, w_in_t, b_cols, w_in_here, taps, vectors = before_halos(
        tissue, rows, upstream, kernel, conv_bias, ln_gain, ln_bias, w_in, b_in, w_out, layer_scale
    )
    kept, sent, grad_conv, low, high = middle(
        core, conv, low, high, taps, vectors, w_in_t, b_cols, out_grad, back, w_in_here
    )
    message = to_cube(near, kept, swap(sent))
    received = exchange(message, CUBE)
    low, high = from_left(high), from_right(low)
    received, low, high = lax.optimization_barrier((received, low, high))
    received = exchange(to_far(received, far), FAR)
    grad_image = to_features(grad_conv, low, high, taps, upstream)
    received, grad_image = lax.optimization_barrier((received, grad_image))
    message, in_rows = turn(scale, received, channels)
    received = exchange(message, FAR)
    in_rows = lax.ppermute(in_rows, EVERY, owners(sizes))
    received, in_rows = lax.optimization_barrier((received, in_rows))
    own = exchange(unpack(received, near, channels), CUBE).reshape(-1, channels)
    grad_w_out, grad_w_in = join(core, own, swap(own), in_rows)
    return (grad_image.reshape(1, height, breadth, channels), grad_w_in, grad_w_out)


def solution(mesh):
    fine = jax.sharding.Mesh(mesh.devices.reshape(4, 2, 2, 4, 2, 2, 2), EVERY)
    band = P(("zl", "c"), None, TILE, None)
    placed = (band, band) + (P(),) * 8 + (P(("zl", "c"), TILE),)
    return jax.shard_map(
        body,
        mesh=fine,
        in_specs=placed,
        out_specs=(band, P(EVERY, None), P()),
        check_vma=False,
    )
```

```python
import functools
import math

import jax
import jax.numpy as jnp
from jax import lax
from jax.experimental import pallas as pl
from jax.experimental.pallas import tpu as pltpu
from jax.sharding import PartitionSpec as P

SIDE = 8
HALO = 3
TAPS = 7
COLS = 32
LANES = 128
CHUNK = 32
ROWS = 3
EDGE = 4 * SIDE
EPSILON = 1e-06
VMEM_LIMIT = 16 * 1024 * 1024
NT = (((1,), (1,)), ((), ()))

TILE = ("zh", "xh", "xl", "yh", "yl")
CUBE = ("xl", "yl", "zl")
LINE = ("zh",)
PLANE = ("xh", "yh")
EVERY = ("zh", "xh", "xl", "yh", "yl", "zl", "c")
SWAP = [(0, 1), (1, 0)]


def matmul(left, right, dims=(((1,), (0,)), ((), ()))):
    return lax.dot_general(left, right, dims, preferred_element_type=jnp.float32)


def shifted(column, a):
    move = a - HALO
    if move == 0:
        return column
    row = lax.broadcasted_iota(jnp.int32, column.shape, 0)
    inside = (row + move >= 0) & (row + move < SIDE)
    return jnp.where(inside, pltpu.roll(column, (-move) % SIDE, 0), 0.0)


def convolve(columns, taps, lanes, flip):
    count = len(columns) - 2 * HALO
    totals = [None] * count
    for a in range(TAPS):
        sums = [None] * count
        for e in range(TAPS):
            row, place = (TAPS - 1 - a, TAPS - 1 - e) if flip else (a, e)
            tap = taps[row, place : place + 1, lanes]
            for j in range(count):
                if columns[j + e] is None:
                    continue
                term = columns[j + e] * tap
                sums[j] = term if sums[j] is None else sums[j] + term
        for j in range(count):
            if sums[j] is None:
                continue
            moved = shifted(sums[j], a)
            totals[j] = moved if totals[j] is None else totals[j] + moved
    return totals


def lane_blocks(width):
    return [slice(start, start + LANES) for start in range(0, width, LANES)]


def widen(source, wide):
    for k, lanes in enumerate(lane_blocks(source.shape[1])):
        wide[k] = source[:, lanes].astype(jnp.float32)


def edge_kernel(features, low, high, image, wide, sem):
    copy = pltpu.make_async_copy(features, image, sem)
    copy.start()
    copy.wait()
    widen(image, wide)
    count = EDGE // SIDE
    for k, lanes in enumerate(lane_blocks(features.shape[1])):
        for first, edge in ((0, low), (COLS - count, high)):
            columns = [wide[k, pl.ds(first + j, SIDE, stride=COLS), :] for j in range(count)]
            edge[:, lanes] = jnp.concatenate(columns, axis=0).astype(jnp.bfloat16)


def first_kernel(
    flags, features, cotangent, w_out, w_in, b_in, taps, scale, conv_bias, gain, bias,
    conv, out_grad, back, w_in_t, b_cols, w_in_here, taps_here, vectors,
    wide, flags_here, image, upstream, w_out_here, b_here, scale_here, conv_bias_here, gain_here, bias_here, sems
):
    width = features.shape[1]
    pairs = [
        (flags, flags_here), (cotangent, upstream), (scale, scale_here), (w_out, w_out_here),
        (features, image), (taps, taps_here), (w_in, w_in_here), (b_in, b_here),
        (conv_bias, conv_bias_here), (gain, gain_here), (bias, bias_here),
    ]
    copies = [pltpu.make_async_copy(src, dst, sems.at[i]) for i, (src, dst) in enumerate(pairs)]
    for copy in copies:
        copy.start()
    for copy in copies[:3]:
        copy.wait()
    widen(upstream, wide)
    rows = SIDE * SIDE
    by_lane = scale_here[...].reshape(1, width)
    for k, lanes in enumerate(lane_blocks(width)):
        for t in range(COLS // SIDE):
            gate = flags_here[0, t].astype(jnp.float32)
            tile = jnp.concatenate(
                [wide[k, pl.ds(t * SIDE + j, SIDE, stride=COLS), :] for j in range(SIDE)], axis=0
            )
            tile = (tile * by_lane[:, lanes] * gate).astype(jnp.bfloat16)
            out_grad[t * rows : (t + 1) * rows, lanes] = tile
    copies[3].wait()
    back[...] = matmul(w_out_here[...], out_grad[...], NT)
    copies[4].wait()
    copies[5].wait()
    widen(image, wide)
    for k, lanes in enumerate(lane_blocks(width)):
        for t in range(COLS // SIDE):
            columns = []
            for j in range(t * SIDE - HALO, (t + 1) * SIDE + HALO):
                inside = 0 <= j < COLS
                columns.append(wide[k, pl.ds(j, SIDE, stride=COLS), :] if inside else None)
            for j, total in enumerate(convolve(columns, taps_here, lanes, False)):
                start = (t * SIDE + j) * SIDE
                conv[start : start + SIDE, lanes] = total
    for copy in copies[6:]:
        copy.wait()
    hidden = w_in.shape[1]
    for start in range(0, hidden, LANES):
        w_in_t[start : start + LANES, :] = w_in_here[:, start : start + LANES].T
        b_cols[start : start + LANES, :] = jnp.broadcast_to(
            b_here[start : start + LANES].reshape(1, LANES), (LANES, LANES)
        ).T
    for i, vector in enumerate((conv_bias_here, gain_here, bias_here)):
        vectors[i * SIDE : (i + 1) * SIDE, :] = jnp.broadcast_to(
            vector[...].reshape(1, width), (SIDE, width)
        )


def middle_kernel(
    core, conv, low, high, taps, vectors, w_in_t, b_cols, out_grad, back, w_in,
    kept, sent, grad_conv, low_edge, high_edge,
    rows, low_wide, high_wide, standard, normed, preact, hidden, grad_pre
):
    width = conv.shape[1]
    rows[...] = conv[...]
    low_wide[...] = low[...].astype(jnp.float32)
    high_wide[...] = high[...].astype(jnp.float32)
    for lanes in lane_blocks(width):
        near = [low_wide[(j + 1) * SIDE : (j + 2) * SIDE, lanes] for j in range(HALO)]
        for j, total in enumerate(convolve(near + [None] * (2 * HALO), taps, lanes, False)):
            rows[j * SIDE : (j + 1) * SIDE, lanes] += total
        near = [high_wide[j * SIDE : (j + 1) * SIDE, lanes] for j in range(HALO)]
        for j, total in enumerate(convolve([None] * (2 * HALO) + near, taps, lanes, False)):
            start = (COLS - HALO + j) * SIDE
            rows[start : start + SIDE, lanes] += total
    gain, bias = vectors[SIDE : SIDE + 1, :], vectors[2 * SIDE : 2 * SIDE + 1, :]
    conv_out = rows[...] + vectors[:1, :]
    centre = conv_out - jnp.mean(conv_out, axis=-1, keepdims=True)
    inverse = lax.rsqrt(jnp.mean(centre * centre, axis=-1, keepdims=True) + EPSILON)
    standard[...] = centre * inverse
    normed[...] = (standard[...] * gain + bias).astype(jnp.bfloat16)
    preact[...] = matmul(w_in_t[...], normed[...], NT)

    def step(i, carry):
        part = pl.ds(pl.multiple_of(i * CHUNK, CHUNK), CHUNK)
        for lanes in lane_blocks(preact.shape[1]):
            z = preact[part, lanes] + b_cols[part, :]
            below = 0.5 * (1.0 + lax.erf(z * 0.7071067811865476))
            density = jnp.exp(-0.5 * z * z) * 0.3989422804014327
            hidden[part, lanes] = (z * below).astype(jnp.bfloat16)
            slope = below + z * density
            grad_pre[part, lanes] = (back[part, lanes] * slope).astype(jnp.bfloat16)
        return carry

    lax.fori_loop(0, preact.shape[0] // CHUNK, step, 0, unroll=2)
    half = hidden.shape[0] // 2
    other = pl.ds(pl.multiple_of((1 - core[0]) * half, half), half)
    own = pl.ds(pl.multiple_of(core[0] * half, half), half)
    sent[:half, :] = matmul(hidden[other, :], out_grad[...]).astype(jnp.bfloat16)
    sent[half:, :] = matmul(grad_pre[other, :], normed[...]).astype(jnp.bfloat16)
    kept[:half, :] = matmul(hidden[own, :], out_grad[...])
    kept[half:, :] = matmul(grad_pre[own, :], normed[...])
    grad_std = matmul(w_in[...], grad_pre[...]).T * gain
    norm = standard[...]
    mean = jnp.mean(grad_std, axis=-1, keepdims=True)
    along = jnp.mean(grad_std * norm, axis=-1, keepdims=True)
    result = inverse * (grad_std - mean - norm * along)
    grad_conv[...] = result
    edge = HALO * SIDE
    low_edge[...] = result[:edge, :]
    high_edge[...] = result[result.shape[0] - edge :, :]


def last_kernel(grad_conv, low, high, taps, cotangent, grad_features, wide):
    for k, lanes in enumerate(lane_blocks(grad_conv.shape[1])):
        for t in range(COLS // SIDE):
            columns = []
            for j in range(t * SIDE - HALO, (t + 1) * SIDE + HALO):
                if j < 0:
                    source, place = low, j + HALO
                elif j >= COLS:
                    source, place = high, j - COLS
                else:
                    source, place = grad_conv, j
                columns.append(source[place * SIDE : (place + 1) * SIDE, lanes])
            for j, total in enumerate(convolve(columns, taps, lanes, True)):
                wide[k, pl.ds(t * SIDE + j, SIDE, stride=COLS), :] = total
        result = cotangent[:, lanes].astype(jnp.float32) + wide[k]
        grad_features[:, lanes] = result.astype(jnp.bfloat16)


def cube_kernel(kept, received, message):
    members, rows, _ = message.shape
    rows //= 2
    for m in range(members):
        for i in range(2):
            start = (i * members + m) * rows
            part = slice(start, start + rows)
            total = kept[part, :] + received[part, :].astype(jnp.float32)
            message[m, i * rows : (i + 1) * rows, :] = total.astype(jnp.bfloat16)


def add_members(received):
    summed = received[0].astype(jnp.float32)
    for i in range(1, received.shape[0]):
        summed += received[i].astype(jnp.float32)
    return summed


def line_kernel(received, message, total):
    members, rows, _ = message.shape
    rows //= 2
    total[...] = add_members(received)
    for m in range(members):
        block = [total[start + m * rows : start + (m + 1) * rows, :] for start in (0, members * rows)]
        message[m] = jnp.concatenate(block, axis=0).astype(jnp.bfloat16)


def plane_kernel(received, message, total, block):
    rows = total.shape[0] // 2
    total[...] = add_members(received)
    block[...] = jnp.zeros_like(block)
    block[:rows, :] = total[:rows, :]
    for m in range(message.shape[0]):
        start = rows + m * ROWS
        block[rows : rows + ROWS, :] = total[start : start + ROWS, :]
        message[m] = block[...].astype(jnp.bfloat16)


def turn_kernel(scale, received, message, grad_w_in):
    rows = message.shape[1]
    total = add_members(received) * scale
    grad_w_in[...] = total[rows : rows + ROWS, :]
    finished = total[:rows, :].astype(jnp.bfloat16)
    for m in range(message.shape[0]):
        message[m] = finished


def unpack_kernel(received, message, total):
    members, rows, _ = received.shape
    for m in range(members):
        total[m * rows : (m + 1) * rows, :] = received[m].astype(jnp.float32)
    whole = total[...].astype(jnp.bfloat16)
    for m in range(message.shape[0]):
        message[m] = whole


def join_kernel(core, own, other, in_rows, grad_w_out, grad_w_in):
    half = own.shape[0]
    grad_w_out[pl.ds(pl.multiple_of(core[0] * half, half), half), :] = own[...]
    grad_w_out[pl.ds(pl.multiple_of((1 - core[0]) * half, half), half), :] = other[...]
    grad_w_in[...] = in_rows[...]


def call(kernel, outs, scratch, scalars, arrays, flops, nbytes, space=pltpu.VMEM):
    if space == pltpu.HBM:
        arrays = [pltpu.with_memory_space_constraint(array, pltpu.HBM) for array in arrays]
    in_specs = [pl.BlockSpec(memory_space=pltpu.SMEM)] * len(scalars)
    in_specs += [pl.BlockSpec(memory_space=space)] * len(arrays)
    return pl.pallas_call(
        kernel,
        out_shape=[jax.ShapeDtypeStruct(shape, kind) for shape, kind in outs],
        in_specs=in_specs,
        out_specs=[pl.BlockSpec(memory_space=pltpu.VMEM)] * len(outs),
        scratch_shapes=scratch,
        compiler_params=pltpu.CompilerParams(vmem_limit_bytes=VMEM_LIMIT),
        cost_estimate=pl.CostEstimate(flops=flops, bytes_accessed=nbytes, transcendentals=0),
    )(*scalars, *arrays)


F32, B16 = jnp.float32, jnp.bfloat16


def edges(features):
    rows, width = features.shape
    return call(
        edge_kernel,
        [((EDGE, width), B16), ((EDGE, width), B16)],
        [pltpu.VMEM((rows, width), B16), pltpu.VMEM((width // LANES, rows, LANES), F32), pltpu.SemaphoreType.DMA],
        [],
        [features],
        features.size, 2 * features.size, pltpu.HBM,
    )


def before_halos(flags, features, cotangent, kernel, conv_bias, gain, bias, w_in, b_in, w_out, layer_scale):
    rows, width = features.shape
    hidden = w_out.shape[0]
    return call(
        first_kernel,
        [((rows, width), F32), ((rows, width), B16), ((hidden, rows), F32), ((hidden, width), B16),
         ((hidden, LANES), F32), (w_in.shape, B16), (kernel.shape, F32), ((3 * SIDE, width), F32)],
        [pltpu.VMEM((width // LANES, rows, LANES), F32), pltpu.SMEM(flags.shape, jnp.int32),
         pltpu.VMEM((rows, width), B16), pltpu.VMEM((rows, width), B16), pltpu.VMEM(w_out.shape, B16),
         pltpu.VMEM(b_in.shape, F32), pltpu.VMEM((width,), F32), pltpu.VMEM((width,), F32),
         pltpu.VMEM((width,), F32), pltpu.VMEM((width,), F32),
         pltpu.SemaphoreType.DMA((11,))],
        [],
        [flags, features, cotangent, w_out, w_in, b_in, kernel, layer_scale, conv_bias, gain, bias],
        2 * rows * width * hidden, 8 * 1024 * 1024, pltpu.HBM,
    )


def middle(core, conv, low, high, taps, vectors, w_in_t, b_cols, out_grad, back, w_in):
    rows, width = conv.shape
    hidden = w_in_t.shape[0]
    halo, edge = pltpu.VMEM((EDGE, width), F32), (HALO * SIDE, width)
    return call(
        middle_kernel,
        [((hidden, width), F32), ((hidden, width), B16), ((rows, width), F32), (edge, F32), (edge, F32)],
        [pltpu.VMEM((rows, width), F32), halo, halo, pltpu.VMEM((rows, width), F32), pltpu.VMEM((rows, width), B16),
         pltpu.VMEM((hidden, rows), F32), pltpu.VMEM((hidden, rows), B16), pltpu.VMEM((hidden, rows), B16)],
        [core],
        [conv, low, high, taps, vectors, w_in_t, b_cols, out_grad, back, w_in],
        8 * rows * width * hidden, 12 * 1024 * 1024,
    )


def to_features(grad_conv, low, high, taps, cotangent):
    rows, width = grad_conv.shape
    return call(
        last_kernel,
        [((rows, width), B16)],
        [pltpu.VMEM((width // LANES, rows, LANES), F32)],
        [],
        [grad_conv, low, high, taps, cotangent],
        2 * 49 * rows * width, 2 * 1024 * 1024,
    )[0]


def to_cube(members, kept, received):
    rows, width = kept.shape
    return call(
        cube_kernel, [((members, rows // members, width), B16)], [], [], [kept, received], 2 * kept.size, 8 * kept.size
    )[0]


def to_line(received, members):
    _, rows, width = received.shape
    return call(
        line_kernel, [((members, rows // members, width), B16)], [pltpu.VMEM((rows, width), F32)], [], [received],
        received.size, 3 * received.size,
    )[0]


def to_plane(received, members):
    _, rows, width = received.shape
    return call(
        plane_kernel,
        [((members, rows // 2 + SIDE, width), B16)],
        [pltpu.VMEM((rows, width), F32), pltpu.VMEM((rows // 2 + SIDE, width), F32)],
        [],
        [received],
        received.size, 4 * received.size,
    )[0]


def turn(scale, received, members):
    _, rows, width = received.shape
    return call(
        functools.partial(turn_kernel, scale),
        [((members, rows - SIDE, width), B16), ((ROWS, width), F32)], [], [], [received],
        received.size, 4 * received.size,
    )


def unpack(received, members):
    count, rows, width = received.shape
    return call(
        unpack_kernel, [((members, count * rows, width), B16)], [pltpu.VMEM((count * rows, width), F32)], [], [received],
        received.size, 10 * received.size,
    )[0]


def join(core, own, other, in_rows):
    rows, width = own.shape
    return call(
        join_kernel, [((2 * rows, width), B16), (in_rows.shape, F32)], [], [core], [own, other, in_rows],
        own.size, 8 * own.size,
    )


def from_left(block):
    count = lax.axis_size(TILE)
    return lax.ppermute(block, TILE, [(i, i + 1) for i in range(count - 1)])


def from_right(block):
    count = lax.axis_size(TILE)
    return lax.ppermute(block, TILE, [(i + 1, i) for i in range(count - 1)])


def exchange(blocks, axes):
    return lax.all_to_all(blocks, axes, split_axis=0, concat_axis=0, tiled=True)


def swap(block):
    return lax.ppermute(block, "c", SWAP)


def owners(sizes):
    count = math.prod(sizes.values())
    pairs = []
    for source in range(count):
        rest, at = source, {}
        for axis in reversed(EVERY):
            rest, at[axis] = divmod(rest, sizes[axis])
        target = 0
        for axis in ("c",) + CUBE + LINE + PLANE:
            target = target * sizes[axis] + at[axis]
        pairs.append((source, target))
    return pairs


def body(
    features, cotangent, kernel, conv_bias, ln_gain, ln_bias, w_in, b_in, w_out, layer_scale, tissue
):
    image = features[0]
    height, breadth, channels = image.shape
    rows = image.reshape(-1, channels)
    low, high = edges(rows)
    low, high = from_left(high), from_right(low)
    upstream = cotangent[0].reshape(-1, channels)
    core = lax.axis_index("c").astype(jnp.int32).reshape(1)
    sizes = {axis: lax.axis_size(axis) for axis in EVERY}
    cube, line, plane = (math.prod(sizes[axis] for axis in axes) for axes in (CUBE, LINE, PLANE))
    scale = 1.0 / math.sqrt(height * breadth * math.prod(sizes.values()))

    conv, out_grad, back, w_in_t, b_cols, w_in_here, taps, vectors = before_halos(
        tissue, rows, upstream, kernel, conv_bias, ln_gain, ln_bias, w_in, b_in, w_out, layer_scale
    )
    kept, sent, grad_conv, low, high = middle(
        core, conv, low, high, taps, vectors, w_in_t, b_cols, out_grad, back, w_in_here
    )
    message = to_cube(cube, kept, swap(sent))
    received = exchange(message, CUBE)
    low, high = from_left(high), from_right(low)
    received, low, high = lax.optimization_barrier((received, low, high))
    received = exchange(to_line(received, line), LINE)
    received = exchange(to_plane(received, plane), PLANE)
    message, in_rows = turn(scale, received, line)
    received = exchange(message, LINE)
    received, in_rows, low, high = lax.optimization_barrier((received, in_rows, low, high))
    own = exchange(unpack(received, cube), CUBE).reshape(-1, channels)
    in_rows = lax.ppermute(in_rows, EVERY, owners(sizes))
    grad_image = to_features(grad_conv, low, high, taps, upstream)
    own, in_rows, grad_image = lax.optimization_barrier((own, in_rows, grad_image))
    grad_w_out, grad_w_in = join(core, own, swap(own), in_rows)
    return (grad_image.reshape(1, height, breadth, channels), grad_w_in, grad_w_out)


def solution(mesh):
    fine = jax.sharding.Mesh(mesh.devices.reshape(4, 2, 2, 4, 2, 2, 2), EVERY)
    band = P(("zl", "c"), None, TILE, None)
    placed = (band, band) + (P(),) * 8 + (P(("zl", "c"), TILE),)
    return jax.shard_map(
        body,
        mesh=fine,
        in_specs=placed,
        out_specs=(band, P(EVERY, None), P()),
        check_vma=False,
    )
```

```python
import functools
import itertools
import math

import jax
import jax.numpy as jnp
from jax import lax
from jax.experimental import pallas as pl
from jax.experimental.pallas import tpu as pltpu
from jax.sharding import PartitionSpec as P

SIDE = 8
HALO = 3
TAPS = 7
COLS = 32
LANES = 128
CHUNK = 32
ROWS = 3
EDGE = 4 * SIDE
TAIL = 16
EPSILON = 1e-06
VMEM_LIMIT = 16 * 1024 * 1024
NT = (((1,), (1,)), ((), ()))

TILE = ("zh", "xh", "xl", "yh", "yl")
CUBE = ("xl", "yl", "zl")
LINE = ("zh",)
PLANE = ("xh", "yh")
EVERY = ("zh", "xh", "xl", "yh", "yl", "zl", "c")
SWAP = [(0, 1), (1, 0)]


def matmul(left, right, dims=(((1,), (0,)), ((), ()))):
    return lax.dot_general(left, right, dims, preferred_element_type=jnp.float32)


def shifted(column, a):
    move = a - HALO
    if move == 0:
        return column
    row = lax.broadcasted_iota(jnp.int32, column.shape, 0)
    inside = (row + move >= 0) & (row + move < SIDE)
    return jnp.where(inside, pltpu.roll(column, (-move) % SIDE, 0), 0.0)


def convolve(columns, taps, lanes, flip):
    count = len(columns) - 2 * HALO
    totals = [None] * count
    for a in range(TAPS):
        sums = [None] * count
        for e in range(TAPS):
            row, place = (TAPS - 1 - a, TAPS - 1 - e) if flip else (a, e)
            tap = taps[row, place : place + 1, lanes]
            for j in range(count):
                if columns[j + e] is None:
                    continue
                term = columns[j + e] * tap
                sums[j] = term if sums[j] is None else sums[j] + term
        for j in range(count):
            if sums[j] is None:
                continue
            moved = shifted(sums[j], a)
            totals[j] = moved if totals[j] is None else totals[j] + moved
    return totals


def lane_blocks(width):
    return [slice(start, start + LANES) for start in range(0, width, LANES)]


def widen(source, wide):
    for k, lanes in enumerate(lane_blocks(source.shape[1])):
        wide[k] = source[:, lanes].astype(jnp.float32)


def edge_kernel(features, low, high, image, wide, sem):
    copy = pltpu.make_async_copy(features, image, sem)
    copy.start()
    copy.wait()
    widen(image, wide)
    count = EDGE // SIDE
    for k, lanes in enumerate(lane_blocks(features.shape[1])):
        for first, edge in ((0, low), (COLS - count, high)):
            columns = [wide[k, pl.ds(first + j, SIDE, stride=COLS), :] for j in range(count)]
            edge[:, lanes] = jnp.concatenate(columns, axis=0).astype(jnp.bfloat16)


def first_kernel(
    flags, features, cotangent, w_out, w_in, b_in, taps, scale, conv_bias, gain, bias,
    conv, out_grad, back, w_in_t, b_cols, w_in_here, taps_here, vectors,
    wide, flags_here, image, upstream, w_out_here, b_here, scale_here, conv_bias_here, gain_here, bias_here, sems
):
    width = features.shape[1]
    pairs = [
        (flags, flags_here), (cotangent, upstream), (scale, scale_here), (w_out, w_out_here),
        (features, image), (taps, taps_here), (w_in, w_in_here), (b_in, b_here),
        (conv_bias, conv_bias_here), (gain, gain_here), (bias, bias_here),
    ]
    copies = [pltpu.make_async_copy(src, dst, sems.at[i]) for i, (src, dst) in enumerate(pairs)]
    for copy in copies:
        copy.start()
    for copy in copies[:3]:
        copy.wait()
    widen(upstream, wide)
    rows = SIDE * SIDE
    by_lane = scale_here[...].reshape(1, width)
    for k, lanes in enumerate(lane_blocks(width)):
        for t in range(COLS // SIDE):
            gate = flags_here[0, t].astype(jnp.float32)
            tile = jnp.concatenate(
                [wide[k, pl.ds(t * SIDE + j, SIDE, stride=COLS), :] for j in range(SIDE)], axis=0
            )
            tile = (tile * by_lane[:, lanes] * gate).astype(jnp.bfloat16)
            out_grad[t * rows : (t + 1) * rows, lanes] = tile
    copies[3].wait()
    back[...] = matmul(w_out_here[...], out_grad[...], NT)
    copies[4].wait()
    copies[5].wait()
    widen(image, wide)
    for k, lanes in enumerate(lane_blocks(width)):
        for t in range(COLS // SIDE):
            columns = []
            for j in range(t * SIDE - HALO, (t + 1) * SIDE + HALO):
                inside = 0 <= j < COLS
                columns.append(wide[k, pl.ds(j, SIDE, stride=COLS), :] if inside else None)
            for j, total in enumerate(convolve(columns, taps_here, lanes, False)):
                start = (t * SIDE + j) * SIDE
                conv[start : start + SIDE, lanes] = total
    for copy in copies[6:]:
        copy.wait()
    hidden = w_in.shape[1]
    for start in range(0, hidden, LANES):
        w_in_t[start : start + LANES, :] = w_in_here[:, start : start + LANES].T
        b_cols[start : start + LANES, :] = jnp.broadcast_to(
            b_here[start : start + LANES].reshape(1, LANES), (LANES, LANES)
        ).T
    for i, vector in enumerate((conv_bias_here, gain_here, bias_here)):
        vectors[i * SIDE : (i + 1) * SIDE, :] = jnp.broadcast_to(
            vector[...].reshape(1, width), (SIDE, width)
        )


def middle_kernel(
    device, conv, low, high, taps, vectors, w_in_t, b_cols, out_grad, back, w_in,
    kept, sent, grad_conv, low_edge, high_edge,
    rows, low_wide, high_wide, standard, normed, preact, hidden, grad_pre
):
    width = conv.shape[1]
    rows[...] = conv[...]
    low_wide[...] = low[...].astype(jnp.float32)
    high_wide[...] = high[...].astype(jnp.float32)
    for lanes in lane_blocks(width):
        near = [low_wide[(j + 1) * SIDE : (j + 2) * SIDE, lanes] for j in range(HALO)]
        for j, total in enumerate(convolve(near + [None] * (2 * HALO), taps, lanes, False)):
            rows[j * SIDE : (j + 1) * SIDE, lanes] += total
        near = [high_wide[j * SIDE : (j + 1) * SIDE, lanes] for j in range(HALO)]
        for j, total in enumerate(convolve([None] * (2 * HALO) + near, taps, lanes, False)):
            start = (COLS - HALO + j) * SIDE
            rows[start : start + SIDE, lanes] += total
    gain, bias = vectors[SIDE : SIDE + 1, :], vectors[2 * SIDE : 2 * SIDE + 1, :]
    conv_out = rows[...] + vectors[:1, :]
    centre = conv_out - jnp.mean(conv_out, axis=-1, keepdims=True)
    inverse = lax.rsqrt(jnp.mean(centre * centre, axis=-1, keepdims=True) + EPSILON)
    standard[...] = centre * inverse
    normed[...] = (standard[...] * gain + bias).astype(jnp.bfloat16)
    preact[...] = matmul(w_in_t[...], normed[...], NT)

    def step(i, carry):
        part = pl.ds(pl.multiple_of(i * CHUNK, CHUNK), CHUNK)
        for lanes in lane_blocks(preact.shape[1]):
            z = preact[part, lanes] + b_cols[part, :]
            below = 0.5 * (1.0 + lax.erf(z * 0.7071067811865476))
            density = jnp.exp(-0.5 * z * z) * 0.3989422804014327
            hidden[part, lanes] = (z * below).astype(jnp.bfloat16)
            slope = below + z * density
            grad_pre[part, lanes] = (back[part, lanes] * slope).astype(jnp.bfloat16)
        return carry

    lax.fori_loop(0, preact.shape[0] // CHUNK, step, 0, unroll=2)
    half = hidden.shape[0] // 2
    core = device[0] & 1
    other = pl.ds(pl.multiple_of((1 - core) * half, half), half)
    own = pl.ds(pl.multiple_of(core * half, half), half)
    sent[:half, :] = matmul(hidden[other, :], out_grad[...]).astype(jnp.bfloat16)
    sent[half:, :] = matmul(grad_pre[other, :], normed[...]).astype(jnp.bfloat16)
    kept[:half, :] = matmul(hidden[own, :], out_grad[...])
    kept[half:, :] = matmul(grad_pre[own, :], normed[...])
    grad_std = matmul(w_in[...], grad_pre[...]).T * gain
    norm = standard[...]
    mean = jnp.mean(grad_std, axis=-1, keepdims=True)
    along = jnp.mean(grad_std * norm, axis=-1, keepdims=True)
    result = inverse * (grad_std - mean - norm * along)
    grad_conv[...] = result
    edge = HALO * SIDE
    low_edge[...] = result[:edge, :]
    high_edge[...] = result[result.shape[0] - edge :, :]


def last_kernel(grad_conv, low, high, taps, cotangent, grad_features, wide):
    for k, lanes in enumerate(lane_blocks(grad_conv.shape[1])):
        for t in range(COLS // SIDE):
            columns = []
            for j in range(t * SIDE - HALO, (t + 1) * SIDE + HALO):
                if j < 0:
                    source, place = low, j + HALO
                elif j >= COLS:
                    source, place = high, j - COLS
                else:
                    source, place = grad_conv, j
                columns.append(source[place * SIDE : (place + 1) * SIDE, lanes])
            for j, total in enumerate(convolve(columns, taps, lanes, True)):
                wide[k, pl.ds(t * SIDE + j, SIDE, stride=COLS), :] = total
        result = cotangent[:, lanes].astype(jnp.float32) + wide[k]
        grad_features[:, lanes] = result.astype(jnp.bfloat16)


def cube_kernel(kept, received, message):
    members, rows, _ = message.shape
    rows //= 2
    half = members * rows
    for m in range(members):
        part = slice(m * rows, (m + 1) * rows)
        total = kept[part, :] + received[part, :].astype(jnp.float32)
        message[m, :rows, :] = total.astype(jnp.bfloat16)
    run = 4 * ROWS
    for bit7, bit6, bit5 in itertools.product(range(2), repeat=3):
        start = half + (bit7 * 4 + bit6 * 2 + bit5) * rows
        total = kept[start : start + rows, :] + received[start : start + rows, :].astype(jnp.float32)
        for bit2 in range(2):
            runs = [total[(2 * i + bit2) * run : (2 * i + bit2 + 1) * run, :] for i in range(4)]
            place = rows + bit6 * 4 * run
            message[bit5 * 4 + bit2 * 2 + bit7, place : place + 4 * run, :] = jnp.concatenate(
                runs, axis=0
            ).astype(jnp.bfloat16)


def add_members(received):
    summed = received[0].astype(jnp.float32)
    for i in range(1, received.shape[0]):
        summed += received[i].astype(jnp.float32)
    return summed


def line_kernel(received, message, total):
    members, rows, width = message.shape
    rows //= 2
    summed = add_members(received)
    for k, lanes in enumerate(lane_blocks(width)):
        total[k] = summed[:, lanes]
        for m in range(members):
            parts = [total[k, m * rows : (m + 1) * rows, :]]
            for r in range(ROWS):
                start = members * rows + m * ROWS + r
                parts.append(total[k, pl.ds(start, SIDE, stride=members * ROWS), :])
            message[m, :, lanes] = jnp.concatenate(parts, axis=0).astype(jnp.bfloat16)


def plane_kernel(received, message, total, block):
    rows = received.shape[1] // 2
    members = message.shape[0]
    summed = add_members(received)
    for k, lanes in enumerate(lane_blocks(received.shape[2])):
        total[k] = summed[:, lanes]
    block[...] = jnp.zeros_like(block)
    for m in range(members):
        for k, lanes in enumerate(lane_blocks(received.shape[2])):
            block[:rows, lanes] = total[k, :rows, :]
            block[rows : rows + ROWS, lanes] = total[k, pl.ds(rows + m, ROWS, stride=members), :]
        message[m] = block[...].astype(jnp.bfloat16)


def turn_kernel(scale, received, message):
    finished = (add_members(received) * scale).astype(jnp.bfloat16)
    for m in range(message.shape[0]):
        message[m] = finished


def unpack_kernel(received, message, block):
    rows = received.shape[1] - SIDE
    count = received.shape[0] * rows
    parts = [received[m].astype(jnp.float32) for m in range(received.shape[0])]
    block[count:, :] = jnp.zeros_like(block[count:, :])
    for m, part in enumerate(parts):
        block[m * rows : (m + 1) * rows, :] = part[:rows, :]
    for bit1 in range(2):
        for bit0 in range(2):
            start = count + bit0 * ROWS
            block[start : start + ROWS, :] = parts[2 * bit1 + bit0][rows : rows + ROWS, :]
        whole = block[...].astype(jnp.bfloat16)
        for m in range(bit1, message.shape[0], 2):
            message[m] = whole


def join_kernel(device, own, other, grad_w_out, grad_w_in):
    number = device[0]
    here = number & 1
    source = ((number >> 5) & 1) * 4 + ((number >> 2) & 1) * 2 + ((number >> 7) & 1)
    members, rows, width = own.shape
    count = rows - TAIL
    half = members * count
    for core, blocks in ((here, own), (1 - here, other)):
        for m in range(members):
            start = pl.multiple_of(core * half + m * count, count)
            grad_w_out[pl.ds(start, count), :] = blocks[m, :count, :]
    tails = [blocks[source, count:, :].astype(jnp.float32) for blocks in (own, other)]
    tail = jnp.where(number >> 8 == here, tails[0], tails[1])
    grad_w_in[...] = jnp.where(here == 0, tail[:ROWS, :], tail[ROWS : 2 * ROWS, :])


def call(kernel, outs, scratch, scalars, arrays, flops, nbytes, space=pltpu.VMEM):
    if space == pltpu.HBM:
        arrays = [pltpu.with_memory_space_constraint(array, pltpu.HBM) for array in arrays]
    in_specs = [pl.BlockSpec(memory_space=pltpu.SMEM)] * len(scalars)
    in_specs += [pl.BlockSpec(memory_space=space)] * len(arrays)
    return pl.pallas_call(
        kernel,
        out_shape=[jax.ShapeDtypeStruct(shape, kind) for shape, kind in outs],
        in_specs=in_specs,
        out_specs=[pl.BlockSpec(memory_space=pltpu.VMEM)] * len(outs),
        scratch_shapes=scratch,
        compiler_params=pltpu.CompilerParams(vmem_limit_bytes=VMEM_LIMIT),
        cost_estimate=pl.CostEstimate(flops=flops, bytes_accessed=nbytes, transcendentals=0),
    )(*scalars, *arrays)


F32, B16 = jnp.float32, jnp.bfloat16


def edges(features):
    rows, width = features.shape
    return call(
        edge_kernel,
        [((EDGE, width), B16), ((EDGE, width), B16)],
        [pltpu.VMEM((rows, width), B16), pltpu.VMEM((width // LANES, rows, LANES), F32), pltpu.SemaphoreType.DMA],
        [],
        [features],
        features.size, 2 * features.size, pltpu.HBM,
    )


def before_halos(flags, features, cotangent, kernel, conv_bias, gain, bias, w_in, b_in, w_out, layer_scale):
    rows, width = features.shape
    hidden = w_out.shape[0]
    return call(
        first_kernel,
        [((rows, width), F32), ((rows, width), B16), ((hidden, rows), F32), ((hidden, width), B16),
         ((hidden, LANES), F32), (w_in.shape, B16), (kernel.shape, F32), ((3 * SIDE, width), F32)],
        [pltpu.VMEM((width // LANES, rows, LANES), F32), pltpu.SMEM(flags.shape, jnp.int32),
         pltpu.VMEM((rows, width), B16), pltpu.VMEM((rows, width), B16), pltpu.VMEM(w_out.shape, B16),
         pltpu.VMEM(b_in.shape, F32), pltpu.VMEM((width,), F32), pltpu.VMEM((width,), F32),
         pltpu.VMEM((width,), F32), pltpu.VMEM((width,), F32),
         pltpu.SemaphoreType.DMA((11,))],
        [],
        [flags, features, cotangent, w_out, w_in, b_in, kernel, layer_scale, conv_bias, gain, bias],
        2 * rows * width * hidden, 8 * 1024 * 1024, pltpu.HBM,
    )


def middle(device, conv, low, high, taps, vectors, w_in_t, b_cols, out_grad, back, w_in):
    rows, width = conv.shape
    hidden = w_in_t.shape[0]
    halo, edge = pltpu.VMEM((EDGE, width), F32), (HALO * SIDE, width)
    return call(
        middle_kernel,
        [((hidden, width), F32), ((hidden, width), B16), ((rows, width), F32), (edge, F32), (edge, F32)],
        [pltpu.VMEM((rows, width), F32), halo, halo, pltpu.VMEM((rows, width), F32), pltpu.VMEM((rows, width), B16),
         pltpu.VMEM((hidden, rows), F32), pltpu.VMEM((hidden, rows), B16), pltpu.VMEM((hidden, rows), B16)],
        [device],
        [conv, low, high, taps, vectors, w_in_t, b_cols, out_grad, back, w_in],
        8 * rows * width * hidden, 12 * 1024 * 1024,
    )


def to_features(grad_conv, low, high, taps, cotangent):
    rows, width = grad_conv.shape
    return call(
        last_kernel,
        [((rows, width), B16)],
        [pltpu.VMEM((width // LANES, rows, LANES), F32)],
        [],
        [grad_conv, low, high, taps, cotangent],
        2 * 49 * rows * width, 2 * 1024 * 1024,
    )[0]


def to_cube(members, kept, received):
    rows, width = kept.shape
    return call(
        cube_kernel, [((members, rows // members, width), B16)], [], [], [kept, received], 2 * kept.size, 8 * kept.size
    )[0]


def to_line(received, members):
    _, rows, width = received.shape
    return call(
        line_kernel, [((members, rows // members, width), B16)],
        [pltpu.VMEM((width // LANES, rows, LANES), F32)], [], [received],
        received.size, 3 * received.size,
    )[0]


def to_plane(received, members):
    _, rows, width = received.shape
    return call(
        plane_kernel,
        [((members, rows // 2 + SIDE, width), B16)],
        [pltpu.VMEM((width // LANES, rows, LANES), F32), pltpu.VMEM((rows // 2 + SIDE, width), F32)],
        [],
        [received],
        received.size, 4 * received.size,
    )[0]


def turn(scale, received, members):
    _, rows, width = received.shape
    return call(
        functools.partial(turn_kernel, scale), [((members, rows, width), B16)], [], [], [received],
        received.size, 4 * received.size,
    )[0]


def unpack(received, members):
    count, rows, width = received.shape
    rows = count * (rows - SIDE) + TAIL
    return call(
        unpack_kernel, [((members, rows, width), B16)], [pltpu.VMEM((rows, width), F32)], [], [received],
        received.size, 10 * received.size,
    )[0]


def join(device, own, other):
    members, rows, width = own.shape
    return call(
        join_kernel, [((2 * members * (rows - TAIL), width), B16), ((ROWS, width), F32)], [], [device], [own, other],
        own.size, 8 * own.size,
    )


def from_left(block):
    count = lax.axis_size(TILE)
    return lax.ppermute(block, TILE, [(i, i + 1) for i in range(count - 1)])


def from_right(block):
    count = lax.axis_size(TILE)
    return lax.ppermute(block, TILE, [(i + 1, i) for i in range(count - 1)])


def exchange(blocks, axes):
    return lax.all_to_all(blocks, axes, split_axis=0, concat_axis=0, tiled=True)


def swap(block):
    return lax.ppermute(block, "c", SWAP)


def body(
    features, cotangent, kernel, conv_bias, ln_gain, ln_bias, w_in, b_in, w_out, layer_scale, tissue
):
    image = features[0]
    height, breadth, channels = image.shape
    rows = image.reshape(-1, channels)
    low, high = edges(rows)
    low, high = from_left(high), from_right(low)
    upstream = cotangent[0].reshape(-1, channels)
    device = lax.axis_index(EVERY).astype(jnp.int32).reshape(1)
    sizes = {axis: lax.axis_size(axis) for axis in EVERY}
    cube, line, plane = (math.prod(sizes[axis] for axis in axes) for axes in (CUBE, LINE, PLANE))
    scale = 1.0 / math.sqrt(height * breadth * math.prod(sizes.values()))

    conv, out_grad, back, w_in_t, b_cols, w_in_here, taps, vectors = before_halos(
        tissue, rows, upstream, kernel, conv_bias, ln_gain, ln_bias, w_in, b_in, w_out, layer_scale
    )
    kept, sent, grad_conv, low, high = middle(
        device, conv, low, high, taps, vectors, w_in_t, b_cols, out_grad, back, w_in_here
    )
    message = to_cube(cube, kept, swap(sent))
    received = exchange(message, CUBE)
    low, high = from_left(high), from_right(low)
    received, low, high = lax.optimization_barrier((received, low, high))
    received = exchange(to_line(received, line), LINE)
    received = exchange(to_plane(received, plane), PLANE)
    received = exchange(turn(scale, received, line), LINE)
    received, low, high = lax.optimization_barrier((received, low, high))
    own = exchange(unpack(received, cube), CUBE)
    grad_image = to_features(grad_conv, low, high, taps, upstream)
    own, grad_image = lax.optimization_barrier((own, grad_image))
    grad_w_out, grad_w_in = join(device, own, swap(own))
    return (grad_image.reshape(1, height, breadth, channels), grad_w_in, grad_w_out)


def solution(mesh):
    fine = jax.sharding.Mesh(mesh.devices.reshape(4, 2, 2, 4, 2, 2, 2), EVERY)
    band = P(("zl", "c"), None, TILE, None)
    placed = (band, band) + (P(),) * 8 + (P(("zl", "c"), TILE),)
    return jax.shard_map(
        body,
        mesh=fine,
        in_specs=placed,
        out_specs=(band, P(EVERY, None), P()),
        check_vma=False,
    )
```

```python
import functools
import itertools
import math

import jax
import jax.numpy as jnp
from jax import lax
from jax.experimental import pallas as pl
from jax.experimental.pallas import tpu as pltpu
from jax.sharding import PartitionSpec as P

SIDE = 8
HALO = 3
TAPS = 7
COLS = 32
LANES = 128
CHUNK = 32
ROWS = 3
EDGE = 4 * SIDE
TAIL = 16
EPSILON = 1e-06
VMEM_LIMIT = 16 * 1024 * 1024
NT = (((1,), (1,)), ((), ()))

TILE = ("zh", "xh", "xl", "yh", "yl")
CUBE = ("xl", "yl", "zl")
LINE = ("zh",)
PLANE = ("xh", "yh")
EVERY = ("zh", "xh", "xl", "yh", "yl", "zl", "c")
SWAP = [(0, 1), (1, 0)]


def matmul(left, right, dims=(((1,), (0,)), ((), ()))):
    return lax.dot_general(left, right, dims, preferred_element_type=jnp.float32)


def shifted(column, a):
    move = a - HALO
    if move == 0:
        return column
    row = lax.broadcasted_iota(jnp.int32, column.shape, 0)
    inside = (row + move >= 0) & (row + move < SIDE)
    return jnp.where(inside, pltpu.roll(column, (-move) % SIDE, 0), 0.0)


def convolve(columns, taps, lanes, flip):
    count = len(columns) - 2 * HALO
    totals = [None] * count
    for a in range(TAPS):
        sums = [None] * count
        for e in range(TAPS):
            row, place = (TAPS - 1 - a, TAPS - 1 - e) if flip else (a, e)
            tap = taps[row, place : place + 1, lanes]
            for j in range(count):
                if columns[j + e] is None:
                    continue
                term = columns[j + e] * tap
                sums[j] = term if sums[j] is None else sums[j] + term
        for j in range(count):
            if sums[j] is None:
                continue
            moved = shifted(sums[j], a)
            totals[j] = moved if totals[j] is None else totals[j] + moved
    return totals


def lane_blocks(width):
    return [slice(start, start + LANES) for start in range(0, width, LANES)]


def widen(source, wide):
    for k, lanes in enumerate(lane_blocks(source.shape[1])):
        wide[k] = source[:, lanes].astype(jnp.float32)


def first_kernel(
    flags, features, cotangent, w_out, w_in, b_in, taps, scale, conv_bias, gain, bias,
    low_edge, high_edge, conv, out_grad, back, w_in_t, b_cols, w_in_here, taps_here, vectors,
    wide, flags_here, image, upstream, w_out_here, b_here, scale_here, conv_bias_here, gain_here, bias_here, sems
):
    width = features.shape[1]
    pairs = [
        (flags, flags_here), (cotangent, upstream), (scale, scale_here), (w_out, w_out_here),
        (features, image), (taps, taps_here), (w_in, w_in_here), (b_in, b_here),
        (conv_bias, conv_bias_here), (gain, gain_here), (bias, bias_here),
    ]
    copies = [pltpu.make_async_copy(src, dst, sems.at[i]) for i, (src, dst) in enumerate(pairs)]
    for copy in copies:
        copy.start()
    for copy in copies[:3]:
        copy.wait()
    widen(upstream, wide)
    rows = SIDE * SIDE
    by_lane = scale_here[...].reshape(1, width)
    for k, lanes in enumerate(lane_blocks(width)):
        for t in range(COLS // SIDE):
            gate = flags_here[0, t].astype(jnp.float32)
            tile = jnp.concatenate(
                [wide[k, pl.ds(t * SIDE + j, SIDE, stride=COLS), :] for j in range(SIDE)], axis=0
            )
            tile = (tile * by_lane[:, lanes] * gate).astype(jnp.bfloat16)
            out_grad[t * rows : (t + 1) * rows, lanes] = tile
    copies[3].wait()
    back[...] = matmul(w_out_here[...], out_grad[...], NT)
    copies[4].wait()
    copies[5].wait()
    widen(image, wide)
    count = EDGE // SIDE
    for k, lanes in enumerate(lane_blocks(width)):
        for first, edge in ((0, low_edge), (COLS - count, high_edge)):
            columns = [wide[k, pl.ds(first + j, SIDE, stride=COLS), :] for j in range(count)]
            edge[:, lanes] = jnp.concatenate(columns, axis=0).astype(jnp.bfloat16)
        for t in range(COLS // SIDE):
            columns = []
            for j in range(t * SIDE - HALO, (t + 1) * SIDE + HALO):
                inside = 0 <= j < COLS
                columns.append(wide[k, pl.ds(j, SIDE, stride=COLS), :] if inside else None)
            for j, total in enumerate(convolve(columns, taps_here, lanes, False)):
                start = (t * SIDE + j) * SIDE
                conv[start : start + SIDE, lanes] = total
    for copy in copies[6:]:
        copy.wait()
    hidden = w_in.shape[1]
    for start in range(0, hidden, LANES):
        w_in_t[start : start + LANES, :] = w_in_here[:, start : start + LANES].T
        b_cols[start : start + LANES, :] = jnp.broadcast_to(
            b_here[start : start + LANES].reshape(1, LANES), (LANES, LANES)
        ).T
    for i, vector in enumerate((conv_bias_here, gain_here, bias_here)):
        vectors[i * SIDE : (i + 1) * SIDE, :] = jnp.broadcast_to(
            vector[...].reshape(1, width), (SIDE, width)
        )


def middle_kernel(
    device, conv, low, high, taps, vectors, w_in_t, b_cols, out_grad, back,
    kept, sent, standard, inverse, grad_pre,
    rows, low_wide, high_wide, normed, preact, hidden
):
    width = conv.shape[1]
    rows[...] = conv[...]
    low_wide[...] = low[...].astype(jnp.float32)
    high_wide[...] = high[...].astype(jnp.float32)
    for lanes in lane_blocks(width):
        near = [low_wide[(j + 1) * SIDE : (j + 2) * SIDE, lanes] for j in range(HALO)]
        for j, total in enumerate(convolve(near + [None] * (2 * HALO), taps, lanes, False)):
            rows[j * SIDE : (j + 1) * SIDE, lanes] += total
        near = [high_wide[j * SIDE : (j + 1) * SIDE, lanes] for j in range(HALO)]
        for j, total in enumerate(convolve([None] * (2 * HALO) + near, taps, lanes, False)):
            start = (COLS - HALO + j) * SIDE
            rows[start : start + SIDE, lanes] += total
    gain, bias = vectors[SIDE : SIDE + 1, :], vectors[2 * SIDE : 2 * SIDE + 1, :]
    conv_out = rows[...] + vectors[:1, :]
    centre = conv_out - jnp.mean(conv_out, axis=-1, keepdims=True)
    scale = lax.rsqrt(jnp.mean(centre * centre, axis=-1, keepdims=True) + EPSILON)
    inverse[...] = jnp.broadcast_to(scale, inverse.shape)
    standard[...] = centre * scale
    normed[...] = (standard[...] * gain + bias).astype(jnp.bfloat16)
    preact[...] = matmul(w_in_t[...], normed[...], NT)

    def step(i, carry):
        part = pl.ds(pl.multiple_of(i * CHUNK, CHUNK), CHUNK)
        for lanes in lane_blocks(preact.shape[1]):
            z = preact[part, lanes] + b_cols[part, :]
            below = 0.5 * (1.0 + lax.erf(z * 0.7071067811865476))
            density = jnp.exp(-0.5 * z * z) * 0.3989422804014327
            hidden[part, lanes] = (z * below).astype(jnp.bfloat16)
            slope = below + z * density
            grad_pre[part, lanes] = (back[part, lanes] * slope).astype(jnp.bfloat16)
        return carry

    lax.fori_loop(0, preact.shape[0] // CHUNK, step, 0, unroll=2)
    half = hidden.shape[0] // 2
    core = device[0] & 1
    other = pl.ds(pl.multiple_of((1 - core) * half, half), half)
    own = pl.ds(pl.multiple_of(core * half, half), half)
    sent[:half, :] = matmul(hidden[other, :], out_grad[...]).astype(jnp.bfloat16)
    sent[half:, :] = matmul(grad_pre[other, :], normed[...]).astype(jnp.bfloat16)
    kept[:half, :] = matmul(hidden[own, :], out_grad[...])
    kept[half:, :] = matmul(grad_pre[own, :], normed[...])


def back_kernel(grad_pre, w_in, standard, inverse, vectors, grad_conv, low_edge, high_edge):
    grad_std = matmul(w_in[...], grad_pre[...]).T * vectors[SIDE : SIDE + 1, :]
    norm = standard[...]
    mean = jnp.mean(grad_std, axis=-1, keepdims=True)
    along = jnp.mean(grad_std * norm, axis=-1, keepdims=True)
    result = inverse[:, :1] * (grad_std - mean - norm * along)
    grad_conv[...] = result
    edge = HALO * SIDE
    low_edge[...] = result[:edge, :]
    high_edge[...] = result[result.shape[0] - edge :, :]


def last_kernel(grad_conv, low, high, taps, cotangent, grad_features, wide):
    for k, lanes in enumerate(lane_blocks(grad_conv.shape[1])):
        for t in range(COLS // SIDE):
            columns = []
            for j in range(t * SIDE - HALO, (t + 1) * SIDE + HALO):
                if j < 0:
                    source, place = low, j + HALO
                elif j >= COLS:
                    source, place = high, j - COLS
                else:
                    source, place = grad_conv, j
                columns.append(source[place * SIDE : (place + 1) * SIDE, lanes])
            for j, total in enumerate(convolve(columns, taps, lanes, True)):
                wide[k, pl.ds(t * SIDE + j, SIDE, stride=COLS), :] = total
        result = cotangent[:, lanes].astype(jnp.float32) + wide[k]
        grad_features[:, lanes] = result.astype(jnp.bfloat16)


def cube_kernel(kept, received, message):
    members, rows, _ = message.shape
    rows //= 2
    half = members * rows
    for m in range(members):
        part = slice(m * rows, (m + 1) * rows)
        total = kept[part, :] + received[part, :].astype(jnp.float32)
        message[m, :rows, :] = total.astype(jnp.bfloat16)
    run = 4 * ROWS
    for bit7, bit6, bit5 in itertools.product(range(2), repeat=3):
        start = half + (bit7 * 4 + bit6 * 2 + bit5) * rows
        total = kept[start : start + rows, :] + received[start : start + rows, :].astype(jnp.float32)
        for bit2 in range(2):
            runs = [total[(2 * i + bit2) * run : (2 * i + bit2 + 1) * run, :] for i in range(4)]
            place = rows + bit6 * 4 * run
            message[bit5 * 4 + bit2 * 2 + bit7, place : place + 4 * run, :] = jnp.concatenate(
                runs, axis=0
            ).astype(jnp.bfloat16)


def add_members(received):
    summed = received[0].astype(jnp.float32)
    for i in range(1, received.shape[0]):
        summed += received[i].astype(jnp.float32)
    return summed


def plane_kernel(received, message, total):
    members, rows, width = message.shape
    rows //= 2
    summed = add_members(received)
    for k, lanes in enumerate(lane_blocks(width)):
        total[k] = summed[:, lanes]
        for m in range(members):
            start = (members + m) * rows
            parts = [total[k, pl.ds(m, rows, stride=members), :], total[k, start : start + rows, :]]
            message[m, :, lanes] = jnp.concatenate(parts, axis=0).astype(jnp.bfloat16)


def line_kernel(received, message):
    summed = add_members(received).astype(jnp.bfloat16)
    for m in range(message.shape[0]):
        message[m] = summed


def turn_kernel(scale, received, message, in_rows, block):
    finished = add_members(received) * scale
    rows = finished.shape[0] // 2
    block[...] = jnp.zeros_like(block)
    block[:rows, :] = finished[:rows, :]
    in_rows[...] = jnp.zeros_like(in_rows)
    in_rows[:rows, :] = finished[rows:, :]
    whole = block[...].astype(jnp.bfloat16)
    for m in range(message.shape[0]):
        message[m] = whole


def unpack_kernel(received, in_rows, message, spread, block):
    members, _, width = received.shape
    rows = 4 * ROWS
    count = members * rows
    block[count:, :] = jnp.zeros_like(block[count:, :])
    for m in range(members):
        part = received[m].astype(jnp.float32)
        for k, lanes in enumerate(lane_blocks(width)):
            spread[k, pl.ds(m, rows, stride=members), :] = part[:rows, lanes]
    for k, lanes in enumerate(lane_blocks(width)):
        block[:count, lanes] = spread[k]
    for bit1 in range(2):
        block[count : count + 2 * ROWS, :] = in_rows[bit1 * 2 * ROWS : (bit1 + 1) * 2 * ROWS, :]
        whole = block[...].astype(jnp.bfloat16)
        for m in range(bit1, message.shape[0], 2):
            message[m] = whole


def join_kernel(device, own, other, grad_w_out, grad_w_in):
    number = device[0]
    here = number & 1
    source = ((number >> 5) & 1) * 4 + ((number >> 2) & 1) * 2 + ((number >> 7) & 1)
    members, rows, width = own.shape
    count = rows - TAIL
    half = members * count
    for core, blocks in ((here, own), (1 - here, other)):
        for m in range(members):
            start = pl.multiple_of(core * half + m * count, count)
            grad_w_out[pl.ds(start, count), :] = blocks[m, :count, :]
    tails = [blocks[source, count:, :].astype(jnp.float32) for blocks in (own, other)]
    tail = jnp.where(number >> 8 == here, tails[0], tails[1])
    grad_w_in[...] = jnp.where(here == 0, tail[:ROWS, :], tail[ROWS : 2 * ROWS, :])


def call(kernel, outs, scratch, scalars, arrays, flops, nbytes, space=pltpu.VMEM):
    if space == pltpu.HBM:
        arrays = [pltpu.with_memory_space_constraint(array, pltpu.HBM) for array in arrays]
    in_specs = [pl.BlockSpec(memory_space=pltpu.SMEM)] * len(scalars)
    in_specs += [pl.BlockSpec(memory_space=space)] * len(arrays)
    return pl.pallas_call(
        kernel,
        out_shape=[jax.ShapeDtypeStruct(shape, kind) for shape, kind in outs],
        in_specs=in_specs,
        out_specs=[pl.BlockSpec(memory_space=pltpu.VMEM)] * len(outs),
        scratch_shapes=scratch,
        compiler_params=pltpu.CompilerParams(vmem_limit_bytes=VMEM_LIMIT),
        cost_estimate=pl.CostEstimate(flops=flops, bytes_accessed=nbytes, transcendentals=0),
    )(*scalars, *arrays)


F32, B16 = jnp.float32, jnp.bfloat16


def before_halos(flags, features, cotangent, kernel, conv_bias, gain, bias, w_in, b_in, w_out, layer_scale):
    rows, width = features.shape
    hidden = w_out.shape[0]
    return call(
        first_kernel,
        [((EDGE, width), B16), ((EDGE, width), B16), ((rows, width), F32), ((rows, width), B16), ((hidden, rows), F32), ((hidden, width), B16),
         ((hidden, LANES), F32), (w_in.shape, B16), (kernel.shape, F32), ((3 * SIDE, width), F32)],
        [pltpu.VMEM((width // LANES, rows, LANES), F32), pltpu.SMEM(flags.shape, jnp.int32),
         pltpu.VMEM((rows, width), B16), pltpu.VMEM((rows, width), B16), pltpu.VMEM(w_out.shape, B16),
         pltpu.VMEM(b_in.shape, F32), pltpu.VMEM((width,), F32), pltpu.VMEM((width,), F32),
         pltpu.VMEM((width,), F32), pltpu.VMEM((width,), F32),
         pltpu.SemaphoreType.DMA((11,))],
        [],
        [flags, features, cotangent, w_out, w_in, b_in, kernel, layer_scale, conv_bias, gain, bias],
        2 * rows * width * hidden, 8 * 1024 * 1024, pltpu.HBM,
    )


def middle(device, conv, low, high, taps, vectors, w_in_t, b_cols, out_grad, back):
    rows, width = conv.shape
    hidden = w_in_t.shape[0]
    halo = pltpu.VMEM((EDGE, width), F32)
    return call(
        middle_kernel,
        [((hidden, width), F32), ((hidden, width), B16), ((rows, width), F32), ((rows, LANES), F32), ((hidden, rows), B16)],
        [pltpu.VMEM((rows, width), F32), halo, halo, pltpu.VMEM((rows, width), B16),
         pltpu.VMEM((hidden, rows), F32), pltpu.VMEM((hidden, rows), B16)],
        [device],
        [conv, low, high, taps, vectors, w_in_t, b_cols, out_grad, back],
        6 * rows * width * hidden, 12 * 1024 * 1024,
    )


def to_conv(grad_pre, w_in, standard, inverse, vectors):
    rows, width = standard.shape
    edge = (HALO * SIDE, width)
    return call(
        back_kernel, [((rows, width), F32), (edge, F32), (edge, F32)], [], [],
        [grad_pre, w_in, standard, inverse, vectors],
        2 * grad_pre.size * width, 4 * grad_pre.size,
    )


def to_features(grad_conv, low, high, taps, cotangent):
    rows, width = grad_conv.shape
    return call(
        last_kernel,
        [((rows, width), B16)],
        [pltpu.VMEM((width // LANES, rows, LANES), F32)],
        [],
        [grad_conv, low, high, taps, cotangent],
        2 * 49 * rows * width, 2 * 1024 * 1024,
    )[0]


def to_cube(members, kept, received):
    rows, width = kept.shape
    return call(
        cube_kernel, [((members, rows // members, width), B16)], [], [], [kept, received], 2 * kept.size, 8 * kept.size
    )[0]


def to_plane(received, members):
    _, rows, width = received.shape
    return call(
        plane_kernel, [((members, rows // members, width), B16)],
        [pltpu.VMEM((width // LANES, rows, LANES), F32)], [], [received],
        received.size, 3 * received.size,
    )[0]


def to_line(received, members):
    _, rows, width = received.shape
    return call(
        line_kernel, [((members, rows, width), B16)], [], [], [received], received.size, 4 * received.size
    )[0]


def turn(scale, received, members):
    width = received.shape[2]
    return call(
        functools.partial(turn_kernel, scale),
        [((members, 16, width), B16), ((16, width), F32)], [pltpu.VMEM((16, width), F32)], [], [received],
        received.size, 6 * received.size,
    )


def unpack(received, in_rows, members):
    count, _, width = received.shape
    count *= 4 * ROWS
    return call(
        unpack_kernel, [((members, count + TAIL, width), B16)],
        [pltpu.VMEM((width // LANES, count, LANES), F32), pltpu.VMEM((count + TAIL, width), F32)], [], [received, in_rows],
        received.size, 10 * received.size,
    )[0]


def join(device, own, other):
    members, rows, width = own.shape
    return call(
        join_kernel, [((2 * members * (rows - TAIL), width), B16), ((ROWS, width), F32)], [], [device], [own, other],
        own.size, 8 * own.size,
    )


def from_left(block):
    count = lax.axis_size(TILE)
    return lax.ppermute(block, TILE, [(i, i + 1) for i in range(count - 1)])


def from_right(block):
    count = lax.axis_size(TILE)
    return lax.ppermute(block, TILE, [(i + 1, i) for i in range(count - 1)])


def exchange(blocks, axes):
    return lax.all_to_all(blocks, axes, split_axis=0, concat_axis=0, tiled=True)


def swap(block):
    return lax.ppermute(block, "c", SWAP)


def body(
    features, cotangent, kernel, conv_bias, ln_gain, ln_bias, w_in, b_in, w_out, layer_scale, tissue
):
    image = features[0]
    height, breadth, channels = image.shape
    rows = image.reshape(-1, channels)
    upstream = cotangent[0].reshape(-1, channels)
    device = lax.axis_index(EVERY).astype(jnp.int32).reshape(1)
    sizes = {axis: lax.axis_size(axis) for axis in EVERY}
    cube, line, plane = (math.prod(sizes[axis] for axis in axes) for axes in (CUBE, LINE, PLANE))
    scale = 1.0 / math.sqrt(height * breadth * math.prod(sizes.values()))

    device, rows = lax.optimization_barrier((device, rows))
    low, high, conv, out_grad, back, w_in_t, b_cols, w_in_here, taps, vectors = before_halos(
        tissue, rows, upstream, kernel, conv_bias, ln_gain, ln_bias, w_in, b_in, w_out, layer_scale
    )
    low, high = from_left(high), from_right(low)
    kept, sent, standard, inverse, grad_pre = middle(
        device, conv, low, high, taps, vectors, w_in_t, b_cols, out_grad, back
    )
    grad_conv, low, high = to_conv(grad_pre, w_in_here, standard, inverse, vectors)
    kept, low, high = lax.optimization_barrier((kept, low, high))
    received = exchange(to_cube(cube, kept, swap(sent)), CUBE)
    low, high = from_left(high), from_right(low)
    received, low, high = lax.optimization_barrier((received, low, high))
    received = exchange(to_plane(received, plane), PLANE)
    received = exchange(to_line(received, line), LINE)
    message, in_rows = turn(scale, received, plane)
    received = exchange(message, PLANE)
    received, low, high = lax.optimization_barrier((received, low, high))
    own = exchange(unpack(received, in_rows, cube), CUBE)
    grad_image = to_features(grad_conv, low, high, taps, upstream)
    own, grad_image = lax.optimization_barrier((own, grad_image))
    grad_w_out, grad_w_in = join(device, own, swap(own))
    return (grad_image.reshape(1, height, breadth, channels), grad_w_in, grad_w_out)


def solution(mesh):
    fine = jax.sharding.Mesh(mesh.devices.reshape(4, 2, 2, 4, 2, 2, 2), EVERY)
    band = P(("zl", "c"), None, TILE, None)
    placed = (band, band) + (P(),) * 8 + (P(("zl", "c"), TILE),)
    return jax.shard_map(
        body,
        mesh=fine,
        in_specs=placed,
        out_specs=(band, P(EVERY, None), P()),
        check_vma=False,
    )
```

```python
import functools
import itertools
import math

import jax
import jax.numpy as jnp
from jax import lax
from jax.experimental import pallas as pl
from jax.experimental.pallas import tpu as pltpu
from jax.sharding import PartitionSpec as P

SIDE = 8
HALO = 3
TAPS = 7
COLS = 32
LANES = 128
CHUNK = 32
ROWS = 3
EDGE = 4 * SIDE
TAIL = 16
EPSILON = 1e-06
VMEM_LIMIT = 16 * 1024 * 1024
NT = (((1,), (1,)), ((), ()))

TILE = ("zh", "xh", "xl", "yh", "yl")
CUBE = ("xl", "yl", "zl")
LINE = ("zh",)
PLANE = ("xh", "yh")
EVERY = ("zh", "xh", "xl", "yh", "yl", "zl", "c")
SWAP = [(0, 1), (1, 0)]


def matmul(left, right, dims=(((1,), (0,)), ((), ()))):
    return lax.dot_general(left, right, dims, preferred_element_type=jnp.float32)


def shifted(column, a):
    move = a - HALO
    if move == 0:
        return column
    row = lax.broadcasted_iota(jnp.int32, column.shape, 0)
    inside = (row + move >= 0) & (row + move < SIDE)
    return jnp.where(inside, pltpu.roll(column, (-move) % SIDE, 0), 0.0)


def convolve(columns, taps, lanes, flip):
    count = len(columns) - 2 * HALO
    totals = [None] * count
    for a in range(TAPS):
        sums = [None] * count
        for e in range(TAPS):
            row, place = (TAPS - 1 - a, TAPS - 1 - e) if flip else (a, e)
            tap = taps[row, place : place + 1, lanes]
            for j in range(count):
                if columns[j + e] is None:
                    continue
                term = columns[j + e] * tap
                sums[j] = term if sums[j] is None else sums[j] + term
        for j in range(count):
            if sums[j] is None:
                continue
            moved = shifted(sums[j], a)
            totals[j] = moved if totals[j] is None else totals[j] + moved
    return totals


def lane_blocks(width):
    return [slice(start, start + LANES) for start in range(0, width, LANES)]


def widen(source, wide):
    for k, lanes in enumerate(lane_blocks(source.shape[1])):
        wide[k] = source[:, lanes].astype(jnp.float32)


def edge_kernel(features, low, high, image, wide, sem):
    copy = pltpu.make_async_copy(features, image, sem)
    copy.start()
    copy.wait()
    widen(image, wide)
    count = EDGE // SIDE
    for k, lanes in enumerate(lane_blocks(features.shape[1])):
        for first, edge in ((0, low), (COLS - count, high)):
            columns = [wide[k, pl.ds(first + j, SIDE, stride=COLS), :] for j in range(count)]
            edge[:, lanes] = jnp.concatenate(columns, axis=0).astype(jnp.bfloat16)


def first_kernel(
    flags, features, cotangent, w_out, w_in, b_in, taps, scale, conv_bias, gain, bias,
    conv, out_grad, back, w_in_t, b_cols, w_in_here, taps_here, vectors,
    wide, flags_here, image, upstream, w_out_here, b_here, scale_here, conv_bias_here, gain_here, bias_here, sems
):
    width = features.shape[1]
    pairs = [
        (flags, flags_here), (cotangent, upstream), (scale, scale_here), (w_out, w_out_here),
        (features, image), (taps, taps_here), (w_in, w_in_here), (b_in, b_here),
        (conv_bias, conv_bias_here), (gain, gain_here), (bias, bias_here),
    ]
    copies = [pltpu.make_async_copy(src, dst, sems.at[i]) for i, (src, dst) in enumerate(pairs)]
    for copy in copies:
        copy.start()
    for copy in copies[:3]:
        copy.wait()
    widen(upstream, wide)
    rows = SIDE * SIDE
    by_lane = scale_here[...].reshape(1, width)
    for k, lanes in enumerate(lane_blocks(width)):
        for t in range(COLS // SIDE):
            gate = flags_here[0, t].astype(jnp.float32)
            tile = jnp.concatenate(
                [wide[k, pl.ds(t * SIDE + j, SIDE, stride=COLS), :] for j in range(SIDE)], axis=0
            )
            tile = (tile * by_lane[:, lanes] * gate).astype(jnp.bfloat16)
            out_grad[t * rows : (t + 1) * rows, lanes] = tile
    copies[3].wait()
    back[...] = matmul(w_out_here[...], out_grad[...], NT)
    copies[4].wait()
    copies[5].wait()
    widen(image, wide)
    for k, lanes in enumerate(lane_blocks(width)):
        for t in range(COLS // SIDE):
            columns = []
            for j in range(t * SIDE - HALO, (t + 1) * SIDE + HALO):
                inside = 0 <= j < COLS
                columns.append(wide[k, pl.ds(j, SIDE, stride=COLS), :] if inside else None)
            for j, total in enumerate(convolve(columns, taps_here, lanes, False)):
                start = (t * SIDE + j) * SIDE
                conv[start : start + SIDE, lanes] = total
    for copy in copies[6:]:
        copy.wait()
    hidden = w_in.shape[1]
    for start in range(0, hidden, LANES):
        w_in_t[start : start + LANES, :] = w_in_here[:, start : start + LANES].T
        b_cols[start : start + LANES, :] = jnp.broadcast_to(
            b_here[start : start + LANES].reshape(1, LANES), (LANES, LANES)
        ).T
    for i, vector in enumerate((conv_bias_here, gain_here, bias_here)):
        vectors[i * SIDE : (i + 1) * SIDE, :] = jnp.broadcast_to(
            vector[...].reshape(1, width), (SIDE, width)
        )


def middle_kernel(
    device, conv, low, high, taps, vectors, w_in_t, b_cols, out_grad, back,
    kept, sent, standard, inverse, grad_pre,
    rows, low_wide, high_wide, normed, preact, hidden
):
    width = conv.shape[1]
    rows[...] = conv[...]
    low_wide[...] = low[...].astype(jnp.float32)
    high_wide[...] = high[...].astype(jnp.float32)
    for lanes in lane_blocks(width):
        near = [low_wide[(j + 1) * SIDE : (j + 2) * SIDE, lanes] for j in range(HALO)]
        for j, total in enumerate(convolve(near + [None] * (2 * HALO), taps, lanes, False)):
            rows[j * SIDE : (j + 1) * SIDE, lanes] += total
        near = [high_wide[j * SIDE : (j + 1) * SIDE, lanes] for j in range(HALO)]
        for j, total in enumerate(convolve([None] * (2 * HALO) + near, taps, lanes, False)):
            start = (COLS - HALO + j) * SIDE
            rows[start : start + SIDE, lanes] += total
    gain, bias = vectors[SIDE : SIDE + 1, :], vectors[2 * SIDE : 2 * SIDE + 1, :]
    conv_out = rows[...] + vectors[:1, :]
    centre = conv_out - jnp.mean(conv_out, axis=-1, keepdims=True)
    scale = lax.rsqrt(jnp.mean(centre * centre, axis=-1, keepdims=True) + EPSILON)
    inverse[...] = jnp.broadcast_to(scale, inverse.shape)
    standard[...] = centre * scale
    normed[...] = (standard[...] * gain + bias).astype(jnp.bfloat16)
    preact[...] = matmul(w_in_t[...], normed[...], NT)

    def step(i, carry):
        part = pl.ds(pl.multiple_of(i * CHUNK, CHUNK), CHUNK)
        for lanes in lane_blocks(preact.shape[1]):
            z = preact[part, lanes] + b_cols[part, :]
            below = 0.5 * (1.0 + lax.erf(z * 0.7071067811865476))
            density = jnp.exp(-0.5 * z * z) * 0.3989422804014327
            hidden[part, lanes] = (z * below).astype(jnp.bfloat16)
            slope = below + z * density
            grad_pre[part, lanes] = (back[part, lanes] * slope).astype(jnp.bfloat16)
        return carry

    lax.fori_loop(0, preact.shape[0] // CHUNK, step, 0, unroll=2)
    half = hidden.shape[0] // 2
    core = device[0] & 1
    other = pl.ds(pl.multiple_of((1 - core) * half, half), half)
    own = pl.ds(pl.multiple_of(core * half, half), half)
    sent[:half, :] = matmul(hidden[other, :], out_grad[...]).astype(jnp.bfloat16)
    sent[half:, :] = matmul(grad_pre[other, :], normed[...]).astype(jnp.bfloat16)
    kept[:half, :] = matmul(hidden[own, :], out_grad[...])
    kept[half:, :] = matmul(grad_pre[own, :], normed[...])


def back_kernel(grad_pre, w_in, standard, inverse, vectors, grad_conv, low_edge, high_edge):
    grad_std = matmul(w_in[...], grad_pre[...]).T * vectors[SIDE : SIDE + 1, :]
    norm = standard[...]
    mean = jnp.mean(grad_std, axis=-1, keepdims=True)
    along = jnp.mean(grad_std * norm, axis=-1, keepdims=True)
    result = inverse[:, :1] * (grad_std - mean - norm * along)
    grad_conv[...] = result
    edge = HALO * SIDE
    low_edge[...] = result[:edge, :]
    high_edge[...] = result[result.shape[0] - edge :, :]


def last_kernel(grad_conv, low, high, taps, cotangent, grad_features, wide):
    for k, lanes in enumerate(lane_blocks(grad_conv.shape[1])):
        for t in range(COLS // SIDE):
            columns = []
            for j in range(t * SIDE - HALO, (t + 1) * SIDE + HALO):
                if j < 0:
                    source, place = low, j + HALO
                elif j >= COLS:
                    source, place = high, j - COLS
                else:
                    source, place = grad_conv, j
                columns.append(source[place * SIDE : (place + 1) * SIDE, lanes])
            for j, total in enumerate(convolve(columns, taps, lanes, True)):
                wide[k, pl.ds(t * SIDE + j, SIDE, stride=COLS), :] = total
        result = cotangent[:, lanes].astype(jnp.float32) + wide[k]
        grad_features[:, lanes] = result.astype(jnp.bfloat16)


def cube_kernel(kept, received, message):
    members, rows, _ = message.shape
    rows //= 2
    half = members * rows
    for m in range(members):
        part = slice(m * rows, (m + 1) * rows)
        total = kept[part, :] + received[part, :].astype(jnp.float32)
        message[m, :rows, :] = total.astype(jnp.bfloat16)
    run = 4 * ROWS
    for bit7, bit6, bit5 in itertools.product(range(2), repeat=3):
        start = half + (bit7 * 4 + bit6 * 2 + bit5) * rows
        total = kept[start : start + rows, :] + received[start : start + rows, :].astype(jnp.float32)
        for bit2 in range(2):
            runs = [total[(2 * i + bit2) * run : (2 * i + bit2 + 1) * run, :] for i in range(4)]
            place = rows + bit6 * 4 * run
            message[bit5 * 4 + bit2 * 2 + bit7, place : place + 4 * run, :] = jnp.concatenate(
                runs, axis=0
            ).astype(jnp.bfloat16)


def add_members(received):
    summed = received[0].astype(jnp.float32)
    for i in range(1, received.shape[0]):
        summed += received[i].astype(jnp.float32)
    return summed


def line_kernel(received, message, total):
    members, rows, width = message.shape
    rows //= 2
    summed = add_members(received)
    for k, lanes in enumerate(lane_blocks(width)):
        total[k] = summed[:, lanes]
        for m in range(members):
            parts = [total[k, m * rows : (m + 1) * rows, :]]
            for r in range(ROWS):
                start = members * rows + m * ROWS + r
                parts.append(total[k, pl.ds(start, SIDE, stride=members * ROWS), :])
            message[m, :, lanes] = jnp.concatenate(parts, axis=0).astype(jnp.bfloat16)


def plane_kernel(received, message, total, block):
    rows = received.shape[1] // 2
    members = message.shape[0]
    summed = add_members(received)
    for k, lanes in enumerate(lane_blocks(received.shape[2])):
        total[k] = summed[:, lanes]
    block[...] = jnp.zeros_like(block)
    for m in range(members):
        for k, lanes in enumerate(lane_blocks(received.shape[2])):
            block[:rows, lanes] = total[k, :rows, :]
            block[rows : rows + ROWS, lanes] = total[k, pl.ds(rows + m, ROWS, stride=members), :]
        message[m] = block[...].astype(jnp.bfloat16)


def turn_kernel(scale, received, message):
    finished = (add_members(received) * scale).astype(jnp.bfloat16)
    for m in range(message.shape[0]):
        message[m] = finished


def unpack_kernel(received, message, block):
    rows = received.shape[1] - SIDE
    count = received.shape[0] * rows
    parts = [received[m].astype(jnp.float32) for m in range(received.shape[0])]
    block[count:, :] = jnp.zeros_like(block[count:, :])
    for m, part in enumerate(parts):
        block[m * rows : (m + 1) * rows, :] = part[:rows, :]
    for bit1 in range(2):
        for bit0 in range(2):
            start = count + bit0 * ROWS
            block[start : start + ROWS, :] = parts[2 * bit1 + bit0][rows : rows + ROWS, :]
        whole = block[...].astype(jnp.bfloat16)
        for m in range(bit1, message.shape[0], 2):
            message[m] = whole


def join_kernel(device, own, other, grad_w_out, grad_w_in):
    number = device[0]
    here = number & 1
    source = ((number >> 5) & 1) * 4 + ((number >> 2) & 1) * 2 + ((number >> 7) & 1)
    members, rows, width = own.shape
    count = rows - TAIL
    half = members * count
    for core, blocks in ((here, own), (1 - here, other)):
        for m in range(members):
            start = pl.multiple_of(core * half + m * count, count)
            grad_w_out[pl.ds(start, count), :] = blocks[m, :count, :]
    tails = [blocks[source, count:, :].astype(jnp.float32) for blocks in (own, other)]
    tail = jnp.where(number >> 8 == here, tails[0], tails[1])
    grad_w_in[...] = jnp.where(here == 0, tail[:ROWS, :], tail[ROWS : 2 * ROWS, :])


def call(kernel, outs, scratch, scalars, arrays, flops, nbytes, space=pltpu.VMEM):
    if space == pltpu.HBM:
        arrays = [pltpu.with_memory_space_constraint(array, pltpu.HBM) for array in arrays]
    in_specs = [pl.BlockSpec(memory_space=pltpu.SMEM)] * len(scalars)
    in_specs += [pl.BlockSpec(memory_space=space)] * len(arrays)
    return pl.pallas_call(
        kernel,
        out_shape=[jax.ShapeDtypeStruct(shape, kind) for shape, kind in outs],
        in_specs=in_specs,
        out_specs=[pl.BlockSpec(memory_space=pltpu.VMEM)] * len(outs),
        scratch_shapes=scratch,
        compiler_params=pltpu.CompilerParams(vmem_limit_bytes=VMEM_LIMIT),
        cost_estimate=pl.CostEstimate(flops=flops, bytes_accessed=nbytes, transcendentals=0),
    )(*scalars, *arrays)


F32, B16 = jnp.float32, jnp.bfloat16


def edges(features):
    rows, width = features.shape
    return call(
        edge_kernel,
        [((EDGE, width), B16), ((EDGE, width), B16)],
        [pltpu.VMEM((rows, width), B16), pltpu.VMEM((width // LANES, rows, LANES), F32), pltpu.SemaphoreType.DMA],
        [],
        [features],
        features.size, 2 * features.size, pltpu.HBM,
    )


def before_halos(flags, features, cotangent, kernel, conv_bias, gain, bias, w_in, b_in, w_out, layer_scale):
    rows, width = features.shape
    hidden = w_out.shape[0]
    return call(
        first_kernel,
        [((rows, width), F32), ((rows, width), B16), ((hidden, rows), F32), ((hidden, width), B16),
         ((hidden, LANES), F32), (w_in.shape, B16), (kernel.shape, F32), ((3 * SIDE, width), F32)],
        [pltpu.VMEM((width // LANES, rows, LANES), F32), pltpu.SMEM(flags.shape, jnp.int32),
         pltpu.VMEM((rows, width), B16), pltpu.VMEM((rows, width), B16), pltpu.VMEM(w_out.shape, B16),
         pltpu.VMEM(b_in.shape, F32), pltpu.VMEM((width,), F32), pltpu.VMEM((width,), F32),
         pltpu.VMEM((width,), F32), pltpu.VMEM((width,), F32),
         pltpu.SemaphoreType.DMA((11,))],
        [],
        [flags, features, cotangent, w_out, w_in, b_in, kernel, layer_scale, conv_bias, gain, bias],
        2 * rows * width * hidden, 8 * 1024 * 1024, pltpu.HBM,
    )


def middle(device, conv, low, high, taps, vectors, w_in_t, b_cols, out_grad, back):
    rows, width = conv.shape
    hidden = w_in_t.shape[0]
    halo = pltpu.VMEM((EDGE, width), F32)
    return call(
        middle_kernel,
        [((hidden, width), F32), ((hidden, width), B16), ((rows, width), F32), ((rows, LANES), F32), ((hidden, rows), B16)],
        [pltpu.VMEM((rows, width), F32), halo, halo, pltpu.VMEM((rows, width), B16),
         pltpu.VMEM((hidden, rows), F32), pltpu.VMEM((hidden, rows), B16)],
        [device],
        [conv, low, high, taps, vectors, w_in_t, b_cols, out_grad, back],
        6 * rows * width * hidden, 12 * 1024 * 1024,
    )


def to_conv(grad_pre, w_in, standard, inverse, vectors):
    rows, width = standard.shape
    edge = (HALO * SIDE, width)
    return call(
        back_kernel, [((rows, width), F32), (edge, F32), (edge, F32)], [], [],
        [grad_pre, w_in, standard, inverse, vectors],
        2 * grad_pre.size * width, 4 * grad_pre.size,
    )


def to_features(grad_conv, low, high, taps, cotangent):
    rows, width = grad_conv.shape
    return call(
        last_kernel,
        [((rows, width), B16)],
        [pltpu.VMEM((width // LANES, rows, LANES), F32)],
        [],
        [grad_conv, low, high, taps, cotangent],
        2 * 49 * rows * width, 2 * 1024 * 1024,
    )[0]


def to_cube(members, kept, received):
    rows, width = kept.shape
    return call(
        cube_kernel, [((members, rows // members, width), B16)], [], [], [kept, received], 2 * kept.size, 8 * kept.size
    )[0]


def to_line(received, members):
    _, rows, width = received.shape
    return call(
        line_kernel, [((members, rows // members, width), B16)],
        [pltpu.VMEM((width // LANES, rows, LANES), F32)], [], [received],
        received.size, 3 * received.size,
    )[0]


def to_plane(received, members):
    _, rows, width = received.shape
    return call(
        plane_kernel,
        [((members, rows // 2 + SIDE, width), B16)],
        [pltpu.VMEM((width // LANES, rows, LANES), F32), pltpu.VMEM((rows // 2 + SIDE, width), F32)],
        [],
        [received],
        received.size, 4 * received.size,
    )[0]


def turn(scale, received, members):
    _, rows, width = received.shape
    return call(
        functools.partial(turn_kernel, scale), [((members, rows, width), B16)], [], [], [received],
        received.size, 4 * received.size,
    )[0]


def unpack(received, members):
    count, rows, width = received.shape
    rows = count * (rows - SIDE) + TAIL
    return call(
        unpack_kernel, [((members, rows, width), B16)], [pltpu.VMEM((rows, width), F32)], [], [received],
        received.size, 10 * received.size,
    )[0]


def join(device, own, other):
    members, rows, width = own.shape
    return call(
        join_kernel, [((2 * members * (rows - TAIL), width), B16), ((ROWS, width), F32)], [], [device], [own, other],
        own.size, 8 * own.size,
    )


def from_left(block):
    count = lax.axis_size(TILE)
    return lax.ppermute(block, TILE, [(i, i + 1) for i in range(count - 1)])


def from_right(block):
    count = lax.axis_size(TILE)
    return lax.ppermute(block, TILE, [(i + 1, i) for i in range(count - 1)])


def exchange(blocks, axes):
    return lax.all_to_all(blocks, axes, split_axis=0, concat_axis=0, tiled=True)


def swap(block):
    return lax.ppermute(block, "c", SWAP)


def body(
    features, cotangent, kernel, conv_bias, ln_gain, ln_bias, w_in, b_in, w_out, layer_scale, tissue
):
    image = features[0]
    height, breadth, channels = image.shape
    rows = image.reshape(-1, channels)
    low, high = edges(rows)
    low, high = from_left(high), from_right(low)
    upstream = cotangent[0].reshape(-1, channels)
    device = lax.axis_index(EVERY).astype(jnp.int32).reshape(1)
    sizes = {axis: lax.axis_size(axis) for axis in EVERY}
    cube, line, plane = (math.prod(sizes[axis] for axis in axes) for axes in (CUBE, LINE, PLANE))
    scale = 1.0 / math.sqrt(height * breadth * math.prod(sizes.values()))

    conv, out_grad, back, w_in_t, b_cols, w_in_here, taps, vectors = before_halos(
        tissue, rows, upstream, kernel, conv_bias, ln_gain, ln_bias, w_in, b_in, w_out, layer_scale
    )
    kept, sent, standard, inverse, grad_pre = middle(
        device, conv, low, high, taps, vectors, w_in_t, b_cols, out_grad, back
    )
    grad_conv, low, high = to_conv(grad_pre, w_in_here, standard, inverse, vectors)
    kept, low, high = lax.optimization_barrier((kept, low, high))
    received = exchange(to_cube(cube, kept, swap(sent)), CUBE)
    received = exchange(to_line(received, line), LINE)
    received = exchange(to_plane(received, plane), PLANE)
    received = exchange(turn(scale, received, line), LINE)
    received, low, high = lax.optimization_barrier((received, low, high))
    low, high = from_left(high), from_right(low)
    own = exchange(unpack(received, cube), CUBE)
    grad_image = to_features(grad_conv, low, high, taps, upstream)
    own, grad_image = lax.optimization_barrier((own, grad_image))
    grad_w_out, grad_w_in = join(device, own, swap(own))
    return (grad_image.reshape(1, height, breadth, channels), grad_w_in, grad_w_out)


def solution(mesh):
    fine = jax.sharding.Mesh(mesh.devices.reshape(4, 2, 2, 4, 2, 2, 2), EVERY)
    band = P(("zl", "c"), None, TILE, None)
    placed = (band, band) + (P(),) * 8 + (P(("zl", "c"), TILE),)
    return jax.shard_map(
        body,
        mesh=fine,
        in_specs=placed,
        out_specs=(band, P(EVERY, None), P()),
        check_vma=False,
    )
```

```python
import functools
import itertools
import math

import jax
import jax.numpy as jnp
from jax import lax
from jax.experimental import pallas as pl
from jax.experimental.pallas import tpu as pltpu
from jax.sharding import PartitionSpec as P

SIDE = 8
HALO = 3
TAPS = 7
COLS = 32
LANES = 128
CHUNK = 32
ROWS = 3
EDGE = 4 * SIDE
EPSILON = 1e-06
VMEM_LIMIT = 16 * 1024 * 1024
NT = (((1,), (1,)), ((), ()))

TILE = ("zh", "xh", "xl", "y2", "y1", "yl")
CUBE = ("xl", "yl", "zl")
FOUR = ("xh", "y1")
EIGHT = ("zh", "y2")
EVERY = ("zh", "xh", "xl", "y2", "y1", "yl", "zl", "c")
SWAP = [(0, 1), (1, 0)]


def matmul(left, right, dims=(((1,), (0,)), ((), ()))):
    return lax.dot_general(left, right, dims, preferred_element_type=jnp.float32)


def shifted(column, a):
    move = a - HALO
    if move == 0:
        return column
    row = lax.broadcasted_iota(jnp.int32, column.shape, 0)
    inside = (row + move >= 0) & (row + move < SIDE)
    return jnp.where(inside, pltpu.roll(column, (-move) % SIDE, 0), 0.0)


def convolve(columns, taps, lanes, flip):
    count = len(columns) - 2 * HALO
    totals = [None] * count
    for a in range(TAPS):
        sums = [None] * count
        for e in range(TAPS):
            row, place = (TAPS - 1 - a, TAPS - 1 - e) if flip else (a, e)
            tap = taps[row, place : place + 1, lanes]
            for j in range(count):
                if columns[j + e] is None:
                    continue
                term = columns[j + e] * tap
                sums[j] = term if sums[j] is None else sums[j] + term
        for j in range(count):
            if sums[j] is None:
                continue
            moved = shifted(sums[j], a)
            totals[j] = moved if totals[j] is None else totals[j] + moved
    return totals


def lane_blocks(width):
    return [slice(start, start + LANES) for start in range(0, width, LANES)]


def widen(source, wide):
    for k, lanes in enumerate(lane_blocks(source.shape[1])):
        wide[k] = source[:, lanes].astype(jnp.float32)


def edge_kernel(features, low, high, image, wide, sem):
    copy = pltpu.make_async_copy(features, image, sem)
    copy.start()
    copy.wait()
    widen(image, wide)
    count = EDGE // SIDE
    for k, lanes in enumerate(lane_blocks(features.shape[1])):
        for first, edge in ((0, low), (COLS - count, high)):
            columns = [wide[k, pl.ds(first + j, SIDE, stride=COLS), :] for j in range(count)]
            edge[:, lanes] = jnp.concatenate(columns, axis=0).astype(jnp.bfloat16)


def first_kernel(
    flags, features, cotangent, w_out, w_in, b_in, taps, scale, conv_bias, gain, bias,
    conv, out_grad, back, w_in_t, b_cols, w_in_here, taps_here, vectors,
    wide, flags_here, image, upstream, w_out_here, b_here, scale_here, conv_bias_here, gain_here, bias_here, sems
):
    width = features.shape[1]
    pairs = [
        (flags, flags_here), (cotangent, upstream), (scale, scale_here), (w_out, w_out_here),
        (features, image), (taps, taps_here), (w_in, w_in_here), (b_in, b_here),
        (conv_bias, conv_bias_here), (gain, gain_here), (bias, bias_here),
    ]
    copies = [pltpu.make_async_copy(src, dst, sems.at[i]) for i, (src, dst) in enumerate(pairs)]
    for copy in copies:
        copy.start()
    for copy in copies[:3]:
        copy.wait()
    widen(upstream, wide)
    rows = SIDE * SIDE
    by_lane = scale_here[...].reshape(1, width)
    for k, lanes in enumerate(lane_blocks(width)):
        for t in range(COLS // SIDE):
            gate = flags_here[0, t].astype(jnp.float32)
            tile = jnp.concatenate(
                [wide[k, pl.ds(t * SIDE + j, SIDE, stride=COLS), :] for j in range(SIDE)], axis=0
            )
            tile = (tile * by_lane[:, lanes] * gate).astype(jnp.bfloat16)
            out_grad[t * rows : (t + 1) * rows, lanes] = tile
    copies[3].wait()
    back[...] = matmul(w_out_here[...], out_grad[...], NT)
    copies[4].wait()
    copies[5].wait()
    widen(image, wide)
    for k, lanes in enumerate(lane_blocks(width)):
        for t in range(COLS // SIDE):
            columns = []
            for j in range(t * SIDE - HALO, (t + 1) * SIDE + HALO):
                inside = 0 <= j < COLS
                columns.append(wide[k, pl.ds(j, SIDE, stride=COLS), :] if inside else None)
            for j, total in enumerate(convolve(columns, taps_here, lanes, False)):
                start = (t * SIDE + j) * SIDE
                conv[start : start + SIDE, lanes] = total
    for copy in copies[6:]:
        copy.wait()
    hidden = w_in.shape[1]
    for start in range(0, hidden, LANES):
        w_in_t[start : start + LANES, :] = w_in_here[:, start : start + LANES].T
        b_cols[start : start + LANES, :] = jnp.broadcast_to(
            b_here[start : start + LANES].reshape(1, LANES), (LANES, LANES)
        ).T
    for i, vector in enumerate((conv_bias_here, gain_here, bias_here)):
        vectors[i * SIDE : (i + 1) * SIDE, :] = jnp.broadcast_to(
            vector[...].reshape(1, width), (SIDE, width)
        )


def middle_kernel(
    device, conv, low, high, taps, vectors, w_in_t, b_cols, out_grad, back,
    kept, sent, standard, inverse, grad_pre,
    rows, low_wide, high_wide, normed, preact, hidden
):
    width = conv.shape[1]
    rows[...] = conv[...]
    low_wide[...] = low[...].astype(jnp.float32)
    high_wide[...] = high[...].astype(jnp.float32)
    for lanes in lane_blocks(width):
        near = [low_wide[(j + 1) * SIDE : (j + 2) * SIDE, lanes] for j in range(HALO)]
        for j, total in enumerate(convolve(near + [None] * (2 * HALO), taps, lanes, False)):
            rows[j * SIDE : (j + 1) * SIDE, lanes] += total
        near = [high_wide[j * SIDE : (j + 1) * SIDE, lanes] for j in range(HALO)]
        for j, total in enumerate(convolve([None] * (2 * HALO) + near, taps, lanes, False)):
            start = (COLS - HALO + j) * SIDE
            rows[start : start + SIDE, lanes] += total
    gain, bias = vectors[SIDE : SIDE + 1, :], vectors[2 * SIDE : 2 * SIDE + 1, :]
    conv_out = rows[...] + vectors[:1, :]
    centre = conv_out - jnp.mean(conv_out, axis=-1, keepdims=True)
    scale = lax.rsqrt(jnp.mean(centre * centre, axis=-1, keepdims=True) + EPSILON)
    inverse[...] = jnp.broadcast_to(scale, inverse.shape)
    standard[...] = centre * scale
    normed[...] = (standard[...] * gain + bias).astype(jnp.bfloat16)
    preact[...] = matmul(w_in_t[...], normed[...], NT)

    def step(i, carry):
        part = pl.ds(pl.multiple_of(i * CHUNK, CHUNK), CHUNK)
        for lanes in lane_blocks(preact.shape[1]):
            z = preact[part, lanes] + b_cols[part, :]
            below = 0.5 * (1.0 + lax.erf(z * 0.7071067811865476))
            density = jnp.exp(-0.5 * z * z) * 0.3989422804014327
            hidden[part, lanes] = (z * below).astype(jnp.bfloat16)
            slope = below + z * density
            grad_pre[part, lanes] = (back[part, lanes] * slope).astype(jnp.bfloat16)
        return carry

    lax.fori_loop(0, preact.shape[0] // CHUNK, step, 0, unroll=2)
    half = hidden.shape[0] // 2
    core = device[0] & 1
    other = pl.ds(pl.multiple_of((1 - core) * half, half), half)
    own = pl.ds(pl.multiple_of(core * half, half), half)
    sent[:half, :] = matmul(hidden[other, :], out_grad[...]).astype(jnp.bfloat16)
    kept[:half, :] = matmul(hidden[own, :], out_grad[...])
    run = 64 * ROWS
    for i in range(half // run):
        place = half + i * run
        start = pl.multiple_of((2 * i + 1 - core) * run, run)
        sent[place : place + run, :] = matmul(grad_pre[pl.ds(start, run), :], normed[...]).astype(jnp.bfloat16)
        start = pl.multiple_of((2 * i + core) * run, run)
        kept[place : place + run, :] = matmul(grad_pre[pl.ds(start, run), :], normed[...])


def back_kernel(grad_pre, w_in, standard, inverse, vectors, grad_conv, low_edge, high_edge):
    grad_std = matmul(w_in[...], grad_pre[...]).T * vectors[SIDE : SIDE + 1, :]
    norm = standard[...]
    mean = jnp.mean(grad_std, axis=-1, keepdims=True)
    along = jnp.mean(grad_std * norm, axis=-1, keepdims=True)
    result = inverse[:, :1] * (grad_std - mean - norm * along)
    grad_conv[...] = result
    edge = HALO * SIDE
    low_edge[...] = result[:edge, :]
    high_edge[...] = result[result.shape[0] - edge :, :]


def last_kernel(grad_conv, low, high, taps, cotangent, grad_features, wide):
    for k, lanes in enumerate(lane_blocks(grad_conv.shape[1])):
        for t in range(COLS // SIDE):
            columns = []
            for j in range(t * SIDE - HALO, (t + 1) * SIDE + HALO):
                if j < 0:
                    source, place = low, j + HALO
                elif j >= COLS:
                    source, place = high, j - COLS
                else:
                    source, place = grad_conv, j
                columns.append(source[place * SIDE : (place + 1) * SIDE, lanes])
            for j, total in enumerate(convolve(columns, taps, lanes, True)):
                wide[k, pl.ds(t * SIDE + j, SIDE, stride=COLS), :] = total
        result = cotangent[:, lanes].astype(jnp.float32) + wide[k]
        grad_features[:, lanes] = result.astype(jnp.bfloat16)


def cube_kernel(kept, received, message):
    members, rows, _ = message.shape
    rows //= 2
    half = members * rows
    for m in range(members):
        part = slice(m * rows, (m + 1) * rows)
        total = kept[part, :] + received[part, :].astype(jnp.float32)
        message[m, :rows, :] = total.astype(jnp.bfloat16)
    run = 2 * ROWS
    for top, bit5 in itertools.product(range(2), repeat=2):
        totals = []
        for i in (2 * top, 2 * top + 1):
            start = half + (2 * i + bit5) * rows
            totals.append(kept[start : start + rows, :] + received[start : start + rows, :].astype(jnp.float32))
        for low in range(4):
            runs = [
                total[(4 * i + low) * run : (4 * i + low + 1) * run, :] for total in totals for i in range(4)
            ]
            place = rows + top * 8 * run
            message[bit5 * 4 + low, place : place + 8 * run, :] = jnp.concatenate(runs, axis=0).astype(jnp.bfloat16)


def add_members(received):
    summed = received[0].astype(jnp.float32)
    for i in range(1, received.shape[0]):
        summed += received[i].astype(jnp.float32)
    return summed


def four_kernel(received, message, total):
    members, rows, width = message.shape
    rows //= 2
    summed = add_members(received)
    for k, lanes in enumerate(lane_blocks(width)):
        total[k] = summed[:, lanes]
        for m in range(members):
            parts = [total[k, m * rows : (m + 1) * rows, :]]
            for r in range(ROWS):
                start = members * rows + (m % 2) * 2 * ROWS + (m // 2) * ROWS + r
                parts.append(total[k, pl.ds(start, SIDE, stride=members * ROWS), :])
            message[m, :, lanes] = jnp.concatenate(parts, axis=0).astype(jnp.bfloat16)


def eight_kernel(received, message, total, block):
    rows = received.shape[1] // 2
    members = message.shape[0]
    summed = add_members(received)
    for k, lanes in enumerate(lane_blocks(received.shape[2])):
        total[k] = summed[:, lanes]
    block[...] = jnp.zeros_like(block)
    block[:rows, :] = summed[:rows, :]
    for m in range(members):
        for k, lanes in enumerate(lane_blocks(received.shape[2])):
            block[rows : rows + ROWS, lanes] = total[k, pl.ds(rows + m, ROWS, stride=members), :]
        message[m] = block[...].astype(jnp.bfloat16)


def turn_kernel(scale, received, message, grad_w_in):
    finished = add_members(received) * scale
    rows = message.shape[1]
    grad_w_in[...] = finished[rows : rows + ROWS, :]
    whole = finished[:rows, :].astype(jnp.bfloat16)
    for m in range(message.shape[0]):
        message[m] = whole


def join_kernel(device, own, other, in_rows, grad_w_out, grad_w_in):
    core = device[0] & 1
    grad_w_in[...] = in_rows[...]
    members, rows, _ = own.shape
    for place, blocks in ((core, own), (1 - core, other)):
        for m in range(0, members, 2):
            pair = [blocks[i].astype(jnp.float32) for i in (m, m + 1)]
            start = pl.multiple_of((place * members + m) * rows, 2 * rows)
            grad_w_out[pl.ds(start, 2 * rows), :] = jnp.concatenate(pair, axis=0).astype(jnp.bfloat16)


def call(kernel, outs, scratch, scalars, arrays, flops, nbytes, space=pltpu.VMEM):
    if space == pltpu.HBM:
        arrays = [pltpu.with_memory_space_constraint(array, pltpu.HBM) for array in arrays]
    in_specs = [pl.BlockSpec(memory_space=pltpu.SMEM)] * len(scalars)
    in_specs += [pl.BlockSpec(memory_space=space)] * len(arrays)
    return pl.pallas_call(
        kernel,
        out_shape=[jax.ShapeDtypeStruct(shape, kind) for shape, kind in outs],
        in_specs=in_specs,
        out_specs=[pl.BlockSpec(memory_space=pltpu.VMEM)] * len(outs),
        scratch_shapes=scratch,
        compiler_params=pltpu.CompilerParams(vmem_limit_bytes=VMEM_LIMIT),
        cost_estimate=pl.CostEstimate(flops=flops, bytes_accessed=nbytes, transcendentals=0),
    )(*scalars, *arrays)


F32, B16 = jnp.float32, jnp.bfloat16


def edges(features):
    rows, width = features.shape
    return call(
        edge_kernel,
        [((EDGE, width), B16), ((EDGE, width), B16)],
        [pltpu.VMEM((rows, width), B16), pltpu.VMEM((width // LANES, rows, LANES), F32), pltpu.SemaphoreType.DMA],
        [],
        [features],
        features.size, 2 * features.size, pltpu.HBM,
    )


def before_halos(flags, features, cotangent, kernel, conv_bias, gain, bias, w_in, b_in, w_out, layer_scale):
    rows, width = features.shape
    hidden = w_out.shape[0]
    return call(
        first_kernel,
        [((rows, width), F32), ((rows, width), B16), ((hidden, rows), F32), ((hidden, width), B16),
         ((hidden, LANES), F32), (w_in.shape, B16), (kernel.shape, F32), ((3 * SIDE, width), F32)],
        [pltpu.VMEM((width // LANES, rows, LANES), F32), pltpu.SMEM(flags.shape, jnp.int32),
         pltpu.VMEM((rows, width), B16), pltpu.VMEM((rows, width), B16), pltpu.VMEM(w_out.shape, B16),
         pltpu.VMEM(b_in.shape, F32), pltpu.VMEM((width,), F32), pltpu.VMEM((width,), F32),
         pltpu.VMEM((width,), F32), pltpu.VMEM((width,), F32),
         pltpu.SemaphoreType.DMA((11,))],
        [],
        [flags, features, cotangent, w_out, w_in, b_in, kernel, layer_scale, conv_bias, gain, bias],
        2 * rows * width * hidden, 8 * 1024 * 1024, pltpu.HBM,
    )


def middle(device, conv, low, high, taps, vectors, w_in_t, b_cols, out_grad, back):
    rows, width = conv.shape
    hidden = w_in_t.shape[0]
    halo = pltpu.VMEM((EDGE, width), F32)
    return call(
        middle_kernel,
        [((hidden, width), F32), ((hidden, width), B16), ((rows, width), F32), ((rows, LANES), F32), ((hidden, rows), B16)],
        [pltpu.VMEM((rows, width), F32), halo, halo, pltpu.VMEM((rows, width), B16),
         pltpu.VMEM((hidden, rows), F32), pltpu.VMEM((hidden, rows), B16)],
        [device],
        [conv, low, high, taps, vectors, w_in_t, b_cols, out_grad, back],
        6 * rows * width * hidden, 12 * 1024 * 1024,
    )


def to_conv(grad_pre, w_in, standard, inverse, vectors):
    rows, width = standard.shape
    edge = (HALO * SIDE, width)
    return call(
        back_kernel, [((rows, width), F32), (edge, F32), (edge, F32)], [], [],
        [grad_pre, w_in, standard, inverse, vectors],
        2 * grad_pre.size * width, 4 * grad_pre.size,
    )


def to_features(grad_conv, low, high, taps, cotangent):
    rows, width = grad_conv.shape
    return call(
        last_kernel,
        [((rows, width), B16)],
        [pltpu.VMEM((width // LANES, rows, LANES), F32)],
        [],
        [grad_conv, low, high, taps, cotangent],
        2 * 49 * rows * width, 2 * 1024 * 1024,
    )[0]


def to_cube(members, kept, received):
    rows, width = kept.shape
    return call(
        cube_kernel, [((members, rows // members, width), B16)], [], [], [kept, received], 2 * kept.size, 8 * kept.size
    )[0]


def to_four(received, members):
    _, rows, width = received.shape
    return call(
        four_kernel, [((members, rows // members, width), B16)],
        [pltpu.VMEM((width // LANES, rows, LANES), F32)], [], [received],
        received.size, 3 * received.size,
    )[0]


def to_eight(received, members):
    _, rows, width = received.shape
    return call(
        eight_kernel,
        [((members, rows // 2 + SIDE, width), B16)],
        [pltpu.VMEM((width // LANES, rows, LANES), F32), pltpu.VMEM((rows // 2 + SIDE, width), F32)],
        [],
        [received],
        received.size, 4 * received.size,
    )[0]


def turn(scale, received, members):
    _, rows, width = received.shape
    return call(
        functools.partial(turn_kernel, scale),
        [((members, rows - SIDE, width), B16), ((ROWS, width), F32)], [], [], [received],
        received.size, 4 * received.size,
    )


def join(device, own, other, in_rows):
    members, rows, width = own.shape
    return call(
        join_kernel, [((2 * members * rows, width), B16), (in_rows.shape, F32)], [], [device], [own, other, in_rows],
        own.size, 8 * own.size,
    )


def from_left(block):
    count = lax.axis_size(TILE)
    return lax.ppermute(block, TILE, [(i, i + 1) for i in range(count - 1)])


def from_right(block):
    count = lax.axis_size(TILE)
    return lax.ppermute(block, TILE, [(i + 1, i) for i in range(count - 1)])


def exchange(blocks, axes):
    return lax.all_to_all(blocks, axes, split_axis=0, concat_axis=0, tiled=True)


def swap(block):
    return lax.ppermute(block, "c", SWAP)


def body(
    features, cotangent, kernel, conv_bias, ln_gain, ln_bias, w_in, b_in, w_out, layer_scale, tissue
):
    image = features[0]
    height, breadth, channels = image.shape
    rows = image.reshape(-1, channels)
    low, high = edges(rows)
    low, high = from_left(high), from_right(low)
    upstream = cotangent[0].reshape(-1, channels)
    device = lax.axis_index(EVERY).astype(jnp.int32).reshape(1)
    sizes = {axis: lax.axis_size(axis) for axis in EVERY}
    cube, four, eight = (math.prod(sizes[axis] for axis in axes) for axes in (CUBE, FOUR, EIGHT))
    scale = 1.0 / math.sqrt(height * breadth * math.prod(sizes.values()))

    conv, out_grad, back, w_in_t, b_cols, w_in_here, taps, vectors = before_halos(
        tissue, rows, upstream, kernel, conv_bias, ln_gain, ln_bias, w_in, b_in, w_out, layer_scale
    )
    kept, sent, standard, inverse, grad_pre = middle(
        device, conv, low, high, taps, vectors, w_in_t, b_cols, out_grad, back
    )
    grad_conv, low, high = to_conv(grad_pre, w_in_here, standard, inverse, vectors)
    kept, low, high = lax.optimization_barrier((kept, low, high))
    received = exchange(to_cube(cube, kept, swap(sent)), CUBE)
    low, high = from_left(high), from_right(low)
    received, low, high = lax.optimization_barrier((received, low, high))
    received = exchange(to_four(received, four), FOUR)
    received = exchange(to_eight(received, eight), EIGHT)
    message, in_rows = turn(scale, received, cube * four)
    own = exchange(message, CUBE + FOUR)
    pairs = [(2 * xh + c, 2 * c + xh) for xh in range(2) for c in range(2)]
    in_rows = lax.ppermute(in_rows, ("xh", "c"), pairs)
    message, low, high = lax.optimization_barrier((message, low, high))
    grad_image = to_features(grad_conv, low, high, taps, upstream)
    own, in_rows, grad_image = lax.optimization_barrier((own, in_rows, grad_image))
    grad_w_out, grad_w_in = join(device, own, swap(own), in_rows)
    return (grad_image.reshape(1, height, breadth, channels), grad_w_in, grad_w_out)


def solution(mesh):
    fine = jax.sharding.Mesh(mesh.devices.reshape(4, 2, 2, 2, 2, 2, 2, 2), EVERY)
    band = P(("zl", "c"), None, TILE, None)
    placed = (band, band) + (P(),) * 8 + (P(("zl", "c"), TILE),)
    return jax.shard_map(
        body,
        mesh=fine,
        in_specs=placed,
        out_specs=(band, P(EVERY, None), P()),
        check_vma=False,
    )
```

```python
import functools
import itertools
import math

import jax
import jax.numpy as jnp
from jax import lax
from jax.experimental import pallas as pl
from jax.experimental.pallas import tpu as pltpu
from jax.sharding import PartitionSpec as P

SIDE = 8
HALO = 3
TAPS = 7
COLS = 32
LANES = 128
CHUNK = 32
ROWS = 3
EDGE = 4 * SIDE
EPSILON = 1e-06
VMEM_LIMIT = 16 * 1024 * 1024
NT = (((1,), (1,)), ((), ()))

TILE = ("zh", "xh", "xl", "y2", "y1", "yl")
CUBE = ("xl", "yl", "zl")
FOUR = ("xh", "y1")
EIGHT = ("zh", "y2")
EVERY = ("zh", "xh", "xl", "y2", "y1", "yl", "zl", "c")
SWAP = [(0, 1), (1, 0)]


def matmul(left, right, dims=(((1,), (0,)), ((), ()))):
    return lax.dot_general(left, right, dims, preferred_element_type=jnp.float32)


def shifted(column, a):
    move = a - HALO
    if move == 0:
        return column
    row = lax.broadcasted_iota(jnp.int32, column.shape, 0)
    inside = (row + move >= 0) & (row + move < SIDE)
    return jnp.where(inside, pltpu.roll(column, (-move) % SIDE, 0), 0.0)


def convolve(columns, taps, lanes, flip):
    count = len(columns) - 2 * HALO
    totals = [None] * count
    for a in range(TAPS):
        sums = [None] * count
        for e in range(TAPS):
            row, place = (TAPS - 1 - a, TAPS - 1 - e) if flip else (a, e)
            tap = taps[row, place : place + 1, lanes]
            for j in range(count):
                if columns[j + e] is None:
                    continue
                term = columns[j + e] * tap
                sums[j] = term if sums[j] is None else sums[j] + term
        for j in range(count):
            if sums[j] is None:
                continue
            moved = shifted(sums[j], a)
            totals[j] = moved if totals[j] is None else totals[j] + moved
    return totals


def lane_blocks(width):
    return [slice(start, start + LANES) for start in range(0, width, LANES)]


def widen(source, wide):
    for k, lanes in enumerate(lane_blocks(source.shape[1])):
        wide[k] = source[:, lanes].astype(jnp.float32)


def edge_kernel(features, low, high, image, wide, sem):
    copy = pltpu.make_async_copy(features, image, sem)
    copy.start()
    copy.wait()
    widen(image, wide)
    count = EDGE // SIDE
    for k, lanes in enumerate(lane_blocks(features.shape[1])):
        for first, edge in ((0, low), (COLS - count, high)):
            columns = [wide[k, pl.ds(first + j, SIDE, stride=COLS), :] for j in range(count)]
            edge[:, lanes] = jnp.concatenate(columns, axis=0).astype(jnp.bfloat16)


def first_kernel(
    flags, features, cotangent, w_out, w_in, b_in, taps, scale, conv_bias, gain, bias,
    conv, out_grad, back, w_in_t, b_cols, w_in_here, taps_here, vectors,
    wide, flags_here, image, upstream, w_out_here, b_here, scale_here, conv_bias_here, gain_here, bias_here, sems
):
    width = features.shape[1]
    pairs = [
        (flags, flags_here), (cotangent, upstream), (scale, scale_here), (w_out, w_out_here),
        (features, image), (taps, taps_here), (w_in, w_in_here), (b_in, b_here),
        (conv_bias, conv_bias_here), (gain, gain_here), (bias, bias_here),
    ]
    copies = [pltpu.make_async_copy(src, dst, sems.at[i]) for i, (src, dst) in enumerate(pairs)]
    for copy in copies:
        copy.start()
    for copy in copies[:3]:
        copy.wait()
    widen(upstream, wide)
    rows = SIDE * SIDE
    by_lane = scale_here[...].reshape(1, width)
    for k, lanes in enumerate(lane_blocks(width)):
        for t in range(COLS // SIDE):
            gate = flags_here[0, t].astype(jnp.float32)
            tile = jnp.concatenate(
                [wide[k, pl.ds(t * SIDE + j, SIDE, stride=COLS), :] for j in range(SIDE)], axis=0
            )
            tile = (tile * by_lane[:, lanes] * gate).astype(jnp.bfloat16)
            out_grad[t * rows : (t + 1) * rows, lanes] = tile
    copies[3].wait()
    back[...] = matmul(w_out_here[...], out_grad[...], NT)
    copies[4].wait()
    copies[5].wait()
    widen(image, wide)
    def convolve_tile(t):
        for k, lanes in enumerate(lane_blocks(width)):
            columns = []
            for j in range(t * SIDE - HALO, (t + 1) * SIDE + HALO):
                inside = 0 <= j < COLS
                columns.append(wide[k, pl.ds(j, SIDE, stride=COLS), :] if inside else None)
            for j, total in enumerate(convolve(columns, taps_here, lanes, False)):
                start = (t * SIDE + j) * SIDE
                conv[start : start + SIDE, lanes] = total

    for t in range(COLS // SIDE):
        tissue = flags_here[0, t] != 0
        pl.when(tissue)(functools.partial(convolve_tile, t))

        @pl.when(jnp.logical_not(tissue))
        def _(t=t):
            conv[t * rows : (t + 1) * rows, :] = jnp.zeros((rows, width), jnp.float32)

    for copy in copies[6:]:
        copy.wait()
    hidden = w_in.shape[1]
    for start in range(0, hidden, LANES):
        w_in_t[start : start + LANES, :] = w_in_here[:, start : start + LANES].T
        b_cols[start : start + LANES, :] = jnp.broadcast_to(
            b_here[start : start + LANES].reshape(1, LANES), (LANES, LANES)
        ).T
    for i, vector in enumerate((conv_bias_here, gain_here, bias_here)):
        vectors[i * SIDE : (i + 1) * SIDE, :] = jnp.broadcast_to(
            vector[...].reshape(1, width), (SIDE, width)
        )


def middle_kernel(
    device, conv, low, high, taps, vectors, w_in_t, b_cols, out_grad, back,
    kept, sent, standard, inverse, grad_pre,
    rows, low_wide, high_wide, normed, preact, hidden
):
    width = conv.shape[1]
    rows[...] = conv[...]
    low_wide[...] = low[...].astype(jnp.float32)
    high_wide[...] = high[...].astype(jnp.float32)
    for lanes in lane_blocks(width):
        near = [low_wide[(j + 1) * SIDE : (j + 2) * SIDE, lanes] for j in range(HALO)]
        for j, total in enumerate(convolve(near + [None] * (2 * HALO), taps, lanes, False)):
            rows[j * SIDE : (j + 1) * SIDE, lanes] += total
        near = [high_wide[j * SIDE : (j + 1) * SIDE, lanes] for j in range(HALO)]
        for j, total in enumerate(convolve([None] * (2 * HALO) + near, taps, lanes, False)):
            start = (COLS - HALO + j) * SIDE
            rows[start : start + SIDE, lanes] += total
    gain, bias = vectors[SIDE : SIDE + 1, :], vectors[2 * SIDE : 2 * SIDE + 1, :]
    conv_out = rows[...] + vectors[:1, :]
    centre = conv_out - jnp.mean(conv_out, axis=-1, keepdims=True)
    scale = lax.rsqrt(jnp.mean(centre * centre, axis=-1, keepdims=True) + EPSILON)
    inverse[...] = jnp.broadcast_to(scale, inverse.shape)
    standard[...] = centre * scale
    normed[...] = (standard[...] * gain + bias).astype(jnp.bfloat16)
    preact[...] = matmul(w_in_t[...], normed[...], NT)

    def step(i, carry):
        part = pl.ds(pl.multiple_of(i * CHUNK, CHUNK), CHUNK)
        for lanes in lane_blocks(preact.shape[1]):
            z = preact[part, lanes] + b_cols[part, :]
            below = 0.5 * (1.0 + lax.erf(z * 0.7071067811865476))
            density = jnp.exp(-0.5 * z * z) * 0.3989422804014327
            hidden[part, lanes] = (z * below).astype(jnp.bfloat16)
            slope = below + z * density
            grad_pre[part, lanes] = (back[part, lanes] * slope).astype(jnp.bfloat16)
        return carry

    lax.fori_loop(0, preact.shape[0] // CHUNK, step, 0, unroll=2)
    half = hidden.shape[0] // 2
    core = device[0] & 1
    other = pl.ds(pl.multiple_of((1 - core) * half, half), half)
    own = pl.ds(pl.multiple_of(core * half, half), half)
    sent[:half, :] = matmul(hidden[other, :], out_grad[...]).astype(jnp.bfloat16)
    kept[:half, :] = matmul(hidden[own, :], out_grad[...])
    run = 64 * ROWS
    for i in range(half // run):
        place = half + i * run
        start = pl.multiple_of((2 * i + 1 - core) * run, run)
        sent[place : place + run, :] = matmul(grad_pre[pl.ds(start, run), :], normed[...]).astype(jnp.bfloat16)
        start = pl.multiple_of((2 * i + core) * run, run)
        kept[place : place + run, :] = matmul(grad_pre[pl.ds(start, run), :], normed[...])


def back_kernel(grad_pre, w_in, standard, inverse, vectors, grad_conv, low_edge, high_edge):
    grad_std = matmul(w_in[...], grad_pre[...]).T * vectors[SIDE : SIDE + 1, :]
    norm = standard[...]
    mean = jnp.mean(grad_std, axis=-1, keepdims=True)
    along = jnp.mean(grad_std * norm, axis=-1, keepdims=True)
    result = inverse[:, :1] * (grad_std - mean - norm * along)
    grad_conv[...] = result
    edge = HALO * SIDE
    low_edge[...] = result[:edge, :]
    high_edge[...] = result[result.shape[0] - edge :, :]


def last_kernel(grad_conv, low, high, taps, cotangent, grad_features, wide):
    for k, lanes in enumerate(lane_blocks(grad_conv.shape[1])):
        for t in range(COLS // SIDE):
            columns = []
            for j in range(t * SIDE - HALO, (t + 1) * SIDE + HALO):
                if j < 0:
                    source, place = low, j + HALO
                elif j >= COLS:
                    source, place = high, j - COLS
                else:
                    source, place = grad_conv, j
                columns.append(source[place * SIDE : (place + 1) * SIDE, lanes])
            for j, total in enumerate(convolve(columns, taps, lanes, True)):
                wide[k, pl.ds(t * SIDE + j, SIDE, stride=COLS), :] = total
        result = cotangent[:, lanes].astype(jnp.float32) + wide[k]
        grad_features[:, lanes] = result.astype(jnp.bfloat16)


def cube_kernel(kept, received, message):
    members, rows, _ = message.shape
    rows //= 2
    half = members * rows
    for m in range(members):
        part = slice(m * rows, (m + 1) * rows)
        total = kept[part, :] + received[part, :].astype(jnp.float32)
        message[m, :rows, :] = total.astype(jnp.bfloat16)
    run = 2 * ROWS
    for top, bit5 in itertools.product(range(2), repeat=2):
        totals = []
        for i in (2 * top, 2 * top + 1):
            start = half + (2 * i + bit5) * rows
            totals.append(kept[start : start + rows, :] + received[start : start + rows, :].astype(jnp.float32))
        for low in range(4):
            runs = [
                total[(4 * i + low) * run : (4 * i + low + 1) * run, :] for total in totals for i in range(4)
            ]
            place = rows + top * 8 * run
            message[bit5 * 4 + low, place : place + 8 * run, :] = jnp.concatenate(runs, axis=0).astype(jnp.bfloat16)


def add_members(received):
    summed = received[0].astype(jnp.float32)
    for i in range(1, received.shape[0]):
        summed += received[i].astype(jnp.float32)
    return summed


def four_kernel(received, message, total):
    members, rows, width = message.shape
    rows //= 2
    summed = add_members(received)
    for k, lanes in enumerate(lane_blocks(width)):
        total[k] = summed[:, lanes]
        for m in range(members):
            parts = [total[k, m * rows : (m + 1) * rows, :]]
            for r in range(ROWS):
                start = members * rows + (m % 2) * 2 * ROWS + (m // 2) * ROWS + r
                parts.append(total[k, pl.ds(start, SIDE, stride=members * ROWS), :])
            message[m, :, lanes] = jnp.concatenate(parts, axis=0).astype(jnp.bfloat16)


def eight_kernel(received, message, total, block):
    rows = received.shape[1] // 2
    members = message.shape[0]
    summed = add_members(received)
    for k, lanes in enumerate(lane_blocks(received.shape[2])):
        total[k] = summed[:, lanes]
    block[...] = jnp.zeros_like(block)
    block[:rows, :] = summed[:rows, :]
    for m in range(members):
        for k, lanes in enumerate(lane_blocks(received.shape[2])):
            block[rows : rows + ROWS, lanes] = total[k, pl.ds(rows + m, ROWS, stride=members), :]
        message[m] = block[...].astype(jnp.bfloat16)


def turn_kernel(scale, received, message, grad_w_in):
    finished = add_members(received) * scale
    rows = message.shape[1]
    grad_w_in[...] = finished[rows : rows + ROWS, :]
    whole = finished[:rows, :].astype(jnp.bfloat16)
    for m in range(message.shape[0]):
        message[m] = whole


def join_kernel(device, own, other, in_rows, grad_w_out, grad_w_in):
    core = device[0] & 1
    grad_w_in[...] = in_rows[...]
    members, rows, _ = own.shape
    for place, blocks in ((core, own), (1 - core, other)):
        for m in range(0, members, 2):
            pair = [blocks[i].astype(jnp.float32) for i in (m, m + 1)]
            start = pl.multiple_of((place * members + m) * rows, 2 * rows)
            grad_w_out[pl.ds(start, 2 * rows), :] = jnp.concatenate(pair, axis=0).astype(jnp.bfloat16)


def call(kernel, outs, scratch, scalars, arrays, flops, nbytes, space=pltpu.VMEM):
    if space == pltpu.HBM:
        arrays = [pltpu.with_memory_space_constraint(array, pltpu.HBM) for array in arrays]
    in_specs = [pl.BlockSpec(memory_space=pltpu.SMEM)] * len(scalars)
    in_specs += [pl.BlockSpec(memory_space=space)] * len(arrays)
    return pl.pallas_call(
        kernel,
        out_shape=[jax.ShapeDtypeStruct(shape, kind) for shape, kind in outs],
        in_specs=in_specs,
        out_specs=[pl.BlockSpec(memory_space=pltpu.VMEM)] * len(outs),
        scratch_shapes=scratch,
        compiler_params=pltpu.CompilerParams(vmem_limit_bytes=VMEM_LIMIT),
        cost_estimate=pl.CostEstimate(flops=flops, bytes_accessed=nbytes, transcendentals=0),
    )(*scalars, *arrays)


F32, B16 = jnp.float32, jnp.bfloat16


def edges(features):
    rows, width = features.shape
    return call(
        edge_kernel,
        [((EDGE, width), B16), ((EDGE, width), B16)],
        [pltpu.VMEM((rows, width), B16), pltpu.VMEM((width // LANES, rows, LANES), F32), pltpu.SemaphoreType.DMA],
        [],
        [features],
        features.size, 2 * features.size, pltpu.HBM,
    )


def before_halos(flags, features, cotangent, kernel, conv_bias, gain, bias, w_in, b_in, w_out, layer_scale):
    rows, width = features.shape
    hidden = w_out.shape[0]
    return call(
        first_kernel,
        [((rows, width), F32), ((rows, width), B16), ((hidden, rows), F32), ((hidden, width), B16),
         ((hidden, LANES), F32), (w_in.shape, B16), (kernel.shape, F32), ((3 * SIDE, width), F32)],
        [pltpu.VMEM((width // LANES, rows, LANES), F32), pltpu.SMEM(flags.shape, jnp.int32),
         pltpu.VMEM((rows, width), B16), pltpu.VMEM((rows, width), B16), pltpu.VMEM(w_out.shape, B16),
         pltpu.VMEM(b_in.shape, F32), pltpu.VMEM((width,), F32), pltpu.VMEM((width,), F32),
         pltpu.VMEM((width,), F32), pltpu.VMEM((width,), F32),
         pltpu.SemaphoreType.DMA((11,))],
        [],
        [flags, features, cotangent, w_out, w_in, b_in, kernel, layer_scale, conv_bias, gain, bias],
        2 * rows * width * hidden, 8 * 1024 * 1024, pltpu.HBM,
    )


def middle(device, conv, low, high, taps, vectors, w_in_t, b_cols, out_grad, back):
    rows, width = conv.shape
    hidden = w_in_t.shape[0]
    halo = pltpu.VMEM((EDGE, width), F32)
    return call(
        middle_kernel,
        [((hidden, width), F32), ((hidden, width), B16), ((rows, width), F32), ((rows, LANES), F32), ((hidden, rows), B16)],
        [pltpu.VMEM((rows, width), F32), halo, halo, pltpu.VMEM((rows, width), B16),
         pltpu.VMEM((hidden, rows), F32), pltpu.VMEM((hidden, rows), B16)],
        [device],
        [conv, low, high, taps, vectors, w_in_t, b_cols, out_grad, back],
        6 * rows * width * hidden, 12 * 1024 * 1024,
    )


def to_conv(grad_pre, w_in, standard, inverse, vectors):
    rows, width = standard.shape
    edge = (HALO * SIDE, width)
    return call(
        back_kernel, [((rows, width), F32), (edge, F32), (edge, F32)], [], [],
        [grad_pre, w_in, standard, inverse, vectors],
        2 * grad_pre.size * width, 4 * grad_pre.size,
    )


def to_features(grad_conv, low, high, taps, cotangent):
    rows, width = grad_conv.shape
    return call(
        last_kernel,
        [((rows, width), B16)],
        [pltpu.VMEM((width // LANES, rows, LANES), F32)],
        [],
        [grad_conv, low, high, taps, cotangent],
        2 * 49 * rows * width, 2 * 1024 * 1024,
    )[0]


def to_cube(members, kept, received):
    rows, width = kept.shape
    return call(
        cube_kernel, [((members, rows // members, width), B16)], [], [], [kept, received], 2 * kept.size, 8 * kept.size
    )[0]


def to_four(received, members):
    _, rows, width = received.shape
    return call(
        four_kernel, [((members, rows // members, width), B16)],
        [pltpu.VMEM((width // LANES, rows, LANES), F32)], [], [received],
        received.size, 3 * received.size,
    )[0]


def to_eight(received, members):
    _, rows, width = received.shape
    return call(
        eight_kernel,
        [((members, rows // 2 + SIDE, width), B16)],
        [pltpu.VMEM((width // LANES, rows, LANES), F32), pltpu.VMEM((rows // 2 + SIDE, width), F32)],
        [],
        [received],
        received.size, 4 * received.size,
    )[0]


def turn(scale, received, members):
    _, rows, width = received.shape
    return call(
        functools.partial(turn_kernel, scale),
        [((members, rows - SIDE, width), B16), ((ROWS, width), F32)], [], [], [received],
        received.size, 4 * received.size,
    )


def join(device, own, other, in_rows):
    members, rows, width = own.shape
    return call(
        join_kernel, [((2 * members * rows, width), B16), (in_rows.shape, F32)], [], [device], [own, other, in_rows],
        own.size, 8 * own.size,
    )


def from_left(block):
    count = lax.axis_size(TILE)
    return lax.ppermute(block, TILE, [(i, i + 1) for i in range(count - 1)])


def from_right(block):
    count = lax.axis_size(TILE)
    return lax.ppermute(block, TILE, [(i + 1, i) for i in range(count - 1)])


def exchange(blocks, axes):
    return lax.all_to_all(blocks, axes, split_axis=0, concat_axis=0, tiled=True)


def swap(block):
    return lax.ppermute(block, "c", SWAP)


def body(
    features, cotangent, kernel, conv_bias, ln_gain, ln_bias, w_in, b_in, w_out, layer_scale, tissue
):
    image = features[0]
    height, breadth, channels = image.shape
    rows = image.reshape(-1, channels)
    low, high = edges(rows)
    low, high = from_left(high), from_right(low)
    upstream = cotangent[0].reshape(-1, channels)
    device = lax.axis_index(EVERY).astype(jnp.int32).reshape(1)
    sizes = {axis: lax.axis_size(axis) for axis in EVERY}
    cube, four, eight = (math.prod(sizes[axis] for axis in axes) for axes in (CUBE, FOUR, EIGHT))
    scale = 1.0 / math.sqrt(height * breadth * math.prod(sizes.values()))

    conv, out_grad, back, w_in_t, b_cols, w_in_here, taps, vectors = before_halos(
        tissue, rows, upstream, kernel, conv_bias, ln_gain, ln_bias, w_in, b_in, w_out, layer_scale
    )
    kept, sent, standard, inverse, grad_pre = middle(
        device, conv, low, high, taps, vectors, w_in_t, b_cols, out_grad, back
    )
    grad_conv, low, high = to_conv(grad_pre, w_in_here, standard, inverse, vectors)
    kept, low, high = lax.optimization_barrier((kept, low, high))
    received = exchange(to_cube(cube, kept, swap(sent)), CUBE)
    received = exchange(to_four(received, four), FOUR)
    received, low, high = lax.optimization_barrier((received, low, high))
    received = exchange(to_eight(received, eight), EIGHT)
    low, high = from_left(high), from_right(low)
    received, low, high = lax.optimization_barrier((received, low, high))
    message, in_rows = turn(scale, received, cube * four)
    own = exchange(message, CUBE + FOUR)
    pairs = [(2 * xh + c, 2 * c + xh) for xh in range(2) for c in range(2)]
    in_rows = lax.ppermute(in_rows, ("xh", "c"), pairs)
    message, low, high = lax.optimization_barrier((message, low, high))
    grad_image = to_features(grad_conv, low, high, taps, upstream)
    own, in_rows, grad_image = lax.optimization_barrier((own, in_rows, grad_image))
    grad_w_out, grad_w_in = join(device, own, swap(own), in_rows)
    return (grad_image.reshape(1, height, breadth, channels), grad_w_in, grad_w_out)


def solution(mesh):
    fine = jax.sharding.Mesh(mesh.devices.reshape(4, 2, 2, 2, 2, 2, 2, 2), EVERY)
    band = P(("zl", "c"), None, TILE, None)
    placed = (band, band) + (P(),) * 8 + (P(("zl", "c"), TILE),)
    return jax.shard_map(
        body,
        mesh=fine,
        in_specs=placed,
        out_specs=(band, P(EVERY, None), P()),
        check_vma=False,
    )
```

```python
import functools
import itertools
import math

import jax
import jax.numpy as jnp
from jax import lax
from jax.experimental import pallas as pl
from jax.experimental.pallas import tpu as pltpu
from jax.sharding import PartitionSpec as P

SIDE = 8
HALO = 3
TAPS = 7
COLS = 32
LANES = 128
CHUNK = 32
ROWS = 3
EDGE = 10 * SIDE
EPSILON = 1e-06
VMEM_LIMIT = 16 * 1024 * 1024
NT = (((1,), (1,)), ((), ()))

TILE = ("zh", "xh", "xl", "y2", "y1", "yl")
CUBE = ("xl", "yl", "zl")
FOUR = ("xh", "y1")
EIGHT = ("zh", "y2")
EVERY = ("zh", "xh", "xl", "y2", "y1", "yl", "zl", "c")
SWAP = [(0, 1), (1, 0)]


def matmul(left, right, dims=(((1,), (0,)), ((), ()))):
    return lax.dot_general(left, right, dims, preferred_element_type=jnp.float32)


def shifted(column, a):
    move = a - HALO
    if move == 0:
        return column
    row = lax.broadcasted_iota(jnp.int32, column.shape, 0)
    inside = (row + move >= 0) & (row + move < SIDE)
    return jnp.where(inside, pltpu.roll(column, (-move) % SIDE, 0), 0.0)


def convolve(columns, taps, lanes, flip):
    count = len(columns) - 2 * HALO
    totals = [None] * count
    for a in range(TAPS):
        sums = [None] * count
        for e in range(TAPS):
            row, place = (TAPS - 1 - a, TAPS - 1 - e) if flip else (a, e)
            tap = taps[row, place : place + 1, lanes]
            for j in range(count):
                if columns[j + e] is None:
                    continue
                term = columns[j + e] * tap
                sums[j] = term if sums[j] is None else sums[j] + term
        for j in range(count):
            if sums[j] is None:
                continue
            moved = shifted(sums[j], a)
            totals[j] = moved if totals[j] is None else totals[j] + moved
    return totals


def lane_blocks(width):
    return [slice(start, start + LANES) for start in range(0, width, LANES)]


def widen(source, wide):
    for k, lanes in enumerate(lane_blocks(source.shape[1])):
        wide[k] = source[:, lanes].astype(jnp.float32)


def edge_kernel(
    flags, features, cotangent, scale, low, high, flags_here, image, upstream, scale_here, wide, wide_grad, sems
):
    pairs = [(features, image), (cotangent, upstream), (scale, scale_here), (flags, flags_here)]
    copies = [pltpu.make_async_copy(src, dst, sems.at[i]) for i, (src, dst) in enumerate(pairs)]
    for copy in copies:
        copy.start()
    for copy in copies:
        copy.wait()
    widen(image, wide)
    widen(upstream, wide_grad)
    by_lane = scale_here[...].reshape(1, features.shape[1])
    for k, lanes in enumerate(lane_blocks(features.shape[1])):
        for first, first_grad, edge in ((0, 0, low), (COLS - 2 * HALO, COLS - HALO, high)):
            columns = [wide[k, pl.ds(first + j, SIDE, stride=COLS), :] for j in range(2 * HALO)]
            gate = flags_here[0, first_grad // SIDE].astype(jnp.float32)
            for j in range(HALO):
                column = wide_grad[k, pl.ds(first_grad + j, SIDE, stride=COLS), :]
                columns.append(column * by_lane[:, lanes] * gate)
            columns.append(jnp.zeros((SIDE, LANES), jnp.float32))
            edge[:, lanes] = jnp.concatenate(columns, axis=0).astype(jnp.bfloat16)


def first_kernel(
    flags, features, cotangent, w_out, w_in, b_in, taps, scale, conv_bias, gain, bias,
    conv, out_grad, back, w_in_t, b_cols, w_in_here, w_out_here, taps_here, vectors,
    wide, flags_here, image, upstream, b_here, scale_here, conv_bias_here, gain_here, bias_here, sems
):
    width = features.shape[1]
    pairs = [
        (flags, flags_here), (cotangent, upstream), (scale, scale_here), (w_out, w_out_here),
        (features, image), (taps, taps_here), (w_in, w_in_here), (b_in, b_here),
        (conv_bias, conv_bias_here), (gain, gain_here), (bias, bias_here),
    ]
    copies = [pltpu.make_async_copy(src, dst, sems.at[i]) for i, (src, dst) in enumerate(pairs)]
    for copy in copies:
        copy.start()
    for copy in copies[:3]:
        copy.wait()
    widen(upstream, wide)
    rows = SIDE * SIDE
    by_lane = scale_here[...].reshape(1, width)
    for k, lanes in enumerate(lane_blocks(width)):
        for t in range(COLS // SIDE):
            gate = flags_here[0, t].astype(jnp.float32)
            tile = jnp.concatenate(
                [wide[k, pl.ds(t * SIDE + j, SIDE, stride=COLS), :] for j in range(SIDE)], axis=0
            )
            tile = (tile * by_lane[:, lanes] * gate).astype(jnp.bfloat16)
            out_grad[t * rows : (t + 1) * rows, lanes] = tile
    copies[3].wait()
    back[...] = matmul(w_out_here[...], out_grad[...], NT)
    copies[4].wait()
    copies[5].wait()
    widen(image, wide)
    def convolve_tile(t):
        for k, lanes in enumerate(lane_blocks(width)):
            columns = []
            for j in range(t * SIDE - HALO, (t + 1) * SIDE + HALO):
                inside = 0 <= j < COLS
                columns.append(wide[k, pl.ds(j, SIDE, stride=COLS), :] if inside else None)
            for j, total in enumerate(convolve(columns, taps_here, lanes, False)):
                start = (t * SIDE + j) * SIDE
                conv[start : start + SIDE, lanes] = total

    for t in range(COLS // SIDE):
        tissue = flags_here[0, t] != 0
        pl.when(tissue)(functools.partial(convolve_tile, t))

        @pl.when(jnp.logical_not(tissue))
        def _(t=t):
            conv[t * rows : (t + 1) * rows, :] = jnp.zeros((rows, width), jnp.float32)

    for copy in copies[6:]:
        copy.wait()
    hidden = w_in.shape[1]
    for start in range(0, hidden, LANES):
        w_in_t[start : start + LANES, :] = w_in_here[:, start : start + LANES].T
        b_cols[start : start + LANES, :] = jnp.broadcast_to(
            b_here[start : start + LANES].reshape(1, LANES), (LANES, LANES)
        ).T
    for i, vector in enumerate((conv_bias_here, gain_here, bias_here)):
        vectors[i * SIDE : (i + 1) * SIDE, :] = jnp.broadcast_to(
            vector[...].reshape(1, width), (SIDE, width)
        )


def middle_kernel(
    device, conv, low, high, taps, vectors, w_in_t, b_cols, out_grad, back,
    kept, sent, standard, inverse, grad_pre,
    rows, low_wide, high_wide, normed, preact, hidden
):
    width = conv.shape[1]
    rows[...] = conv[...]
    low_wide[...] = low[...].astype(jnp.float32)
    high_wide[...] = high[...].astype(jnp.float32)
    for lanes in lane_blocks(width):
        near = [low_wide[(HALO + j) * SIDE : (HALO + j + 1) * SIDE, lanes] for j in range(HALO)]
        for j, total in enumerate(convolve(near + [None] * (2 * HALO), taps, lanes, False)):
            rows[j * SIDE : (j + 1) * SIDE, lanes] += total
        near = [high_wide[j * SIDE : (j + 1) * SIDE, lanes] for j in range(HALO)]
        for j, total in enumerate(convolve([None] * (2 * HALO) + near, taps, lanes, False)):
            start = (COLS - HALO + j) * SIDE
            rows[start : start + SIDE, lanes] += total
    gain, bias = vectors[SIDE : SIDE + 1, :], vectors[2 * SIDE : 2 * SIDE + 1, :]
    conv_out = rows[...] + vectors[:1, :]
    centre = conv_out - jnp.mean(conv_out, axis=-1, keepdims=True)
    scale = lax.rsqrt(jnp.mean(centre * centre, axis=-1, keepdims=True) + EPSILON)
    inverse[...] = jnp.broadcast_to(scale, inverse.shape)
    standard[...] = centre * scale
    normed[...] = (standard[...] * gain + bias).astype(jnp.bfloat16)
    preact[...] = matmul(w_in_t[...], normed[...], NT)

    def step(i, carry):
        part = pl.ds(pl.multiple_of(i * CHUNK, CHUNK), CHUNK)
        for lanes in lane_blocks(preact.shape[1]):
            z = preact[part, lanes] + b_cols[part, :]
            below = 0.5 * (1.0 + lax.erf(z * 0.7071067811865476))
            density = jnp.exp(-0.5 * z * z) * 0.3989422804014327
            hidden[part, lanes] = (z * below).astype(jnp.bfloat16)
            slope = below + z * density
            grad_pre[part, lanes] = (back[part, lanes] * slope).astype(jnp.bfloat16)
        return carry

    lax.fori_loop(0, preact.shape[0] // CHUNK, step, 0, unroll=2)
    half = hidden.shape[0] // 2
    core = device[0] & 1
    other = pl.ds(pl.multiple_of((1 - core) * half, half), half)
    own = pl.ds(pl.multiple_of(core * half, half), half)
    sent[:half, :] = matmul(hidden[other, :], out_grad[...]).astype(jnp.bfloat16)
    kept[:half, :] = matmul(hidden[own, :], out_grad[...])
    run = 64 * ROWS
    for i in range(half // run):
        place = half + i * run
        start = pl.multiple_of((2 * i + 1 - core) * run, run)
        sent[place : place + run, :] = matmul(grad_pre[pl.ds(start, run), :], normed[...]).astype(jnp.bfloat16)
        start = pl.multiple_of((2 * i + core) * run, run)
        kept[place : place + run, :] = matmul(grad_pre[pl.ds(start, run), :], normed[...])


def through_norm(grad_std, standard, inverse):
    mean = jnp.mean(grad_std, axis=-1, keepdims=True)
    along = jnp.mean(grad_std * standard, axis=-1, keepdims=True)
    return inverse * (grad_std - mean - standard * along)


def back_kernel(
    grad_pre, w_in, standard, inverse, vectors, w_out, w_in_t, b_cols, taps, own_low, own_high, low, high,
    grad_conv, low_conv, high_conv,
    rows, out_grad, preact, back, halo_pre
):
    conv_bias, gain, bias = (vectors[i * SIDE : i * SIDE + 1, :] for i in range(3))
    grad_std = matmul(w_in[...], grad_pre[...]).T * gain
    grad_conv[...] = through_norm(grad_std, standard[...], inverse[:, :1])

    edge = HALO * SIDE
    rows[...] = jnp.zeros_like(rows)
    for lanes in lane_blocks(rows.shape[1]):
        near, far = ([x[:, lanes].astype(jnp.float32) for x in pair] for pair in ((own_low, own_high), (low, high)))
        for i in range(2):
            column = lambda block, j: block[j * SIDE : (j + 1) * SIDE, :]
            beyond = [column(far[i], j) for j in range(2 * HALO)]
            inside = [column(near[i], j + i * HALO) for j in range(HALO)]
            columns = inside + beyond if i else beyond + inside
            for j, total in enumerate(convolve(columns, taps, lanes, False)):
                start = i * edge + j * SIDE
                rows[start : start + SIDE, lanes] = total
        grads = [block[2 * edge : 3 * edge, :] for block in far]
        grads.append(jnp.zeros((rows.shape[0] - 2 * edge, LANES), jnp.float32))
        out_grad[:, lanes] = jnp.concatenate(grads, axis=0).astype(jnp.bfloat16)
    conv_out = rows[...] + conv_bias
    centre = conv_out - jnp.mean(conv_out, axis=-1, keepdims=True)
    scale = lax.rsqrt(jnp.mean(centre * centre, axis=-1, keepdims=True) + EPSILON)
    norm = centre * scale
    preact[...] = matmul(w_in_t[...], (norm * gain + bias).astype(jnp.bfloat16), NT)
    back[...] = matmul(w_out[...], out_grad[...], NT)

    def step(i, carry):
        part = pl.ds(pl.multiple_of(i * CHUNK, CHUNK), CHUNK)
        z = preact[part, :] + b_cols[part, :]
        below = 0.5 * (1.0 + lax.erf(z * 0.7071067811865476))
        density = jnp.exp(-0.5 * z * z) * 0.3989422804014327
        halo_pre[part, :] = (back[part, :] * (below + z * density)).astype(jnp.bfloat16)
        return carry

    lax.fori_loop(0, preact.shape[0] // CHUNK, step, 0, unroll=4)
    grad_std = matmul(w_in[...], halo_pre[...]).T * gain
    result = through_norm(grad_std, norm, scale)
    low_conv[...] = result[:edge, :]
    high_conv[...] = result[edge : 2 * edge, :]


def last_kernel(grad_conv, low, high, taps, cotangent, grad_features, wide):
    for k, lanes in enumerate(lane_blocks(grad_conv.shape[1])):
        for t in range(COLS // SIDE):
            columns = []
            for j in range(t * SIDE - HALO, (t + 1) * SIDE + HALO):
                if j < 0:
                    source, place = low, j + HALO
                elif j >= COLS:
                    source, place = high, j - COLS
                else:
                    source, place = grad_conv, j
                columns.append(source[place * SIDE : (place + 1) * SIDE, lanes])
            for j, total in enumerate(convolve(columns, taps, lanes, True)):
                wide[k, pl.ds(t * SIDE + j, SIDE, stride=COLS), :] = total
        result = cotangent[:, lanes].astype(jnp.float32) + wide[k]
        grad_features[:, lanes] = result.astype(jnp.bfloat16)


def cube_kernel(kept, received, message):
    members, rows, _ = message.shape
    rows //= 2
    half = members * rows
    for m in range(members):
        part = slice(m * rows, (m + 1) * rows)
        total = kept[part, :] + received[part, :].astype(jnp.float32)
        message[m, :rows, :] = total.astype(jnp.bfloat16)
    run = 2 * ROWS
    for top, bit5 in itertools.product(range(2), repeat=2):
        totals = []
        for i in (2 * top, 2 * top + 1):
            start = half + (2 * i + bit5) * rows
            totals.append(kept[start : start + rows, :] + received[start : start + rows, :].astype(jnp.float32))
        for low in range(4):
            runs = [
                total[(4 * i + low) * run : (4 * i + low + 1) * run, :] for total in totals for i in range(4)
            ]
            place = rows + top * 8 * run
            message[bit5 * 4 + low, place : place + 8 * run, :] = jnp.concatenate(runs, axis=0).astype(jnp.bfloat16)


def add_members(received):
    summed = received[0].astype(jnp.float32)
    for i in range(1, received.shape[0]):
        summed += received[i].astype(jnp.float32)
    return summed


def four_kernel(received, message, total):
    members, rows, width = message.shape
    rows //= 2
    summed = add_members(received)
    for k, lanes in enumerate(lane_blocks(width)):
        total[k] = summed[:, lanes]
        for m in range(members):
            parts = [total[k, m * rows : (m + 1) * rows, :]]
            for r in range(ROWS):
                start = members * rows + (m % 2) * 2 * ROWS + (m // 2) * ROWS + r
                parts.append(total[k, pl.ds(start, SIDE, stride=members * ROWS), :])
            message[m, :, lanes] = jnp.concatenate(parts, axis=0).astype(jnp.bfloat16)


def eight_kernel(received, message, total, block):
    rows = received.shape[1] // 2
    members = message.shape[0]
    summed = add_members(received)
    for k, lanes in enumerate(lane_blocks(received.shape[2])):
        total[k] = summed[:, lanes]
    block[...] = jnp.zeros_like(block)
    block[:rows, :] = summed[:rows, :]
    for m in range(members):
        for k, lanes in enumerate(lane_blocks(received.shape[2])):
            block[rows : rows + ROWS, lanes] = total[k, pl.ds(rows + m, ROWS, stride=members), :]
        message[m] = block[...].astype(jnp.bfloat16)


def turn_kernel(scale, received, message, grad_w_in):
    finished = add_members(received) * scale
    rows = message.shape[1]
    grad_w_in[...] = finished[rows : rows + ROWS, :]
    whole = finished[:rows, :].astype(jnp.bfloat16)
    for m in range(message.shape[0]):
        message[m] = whole


def join_kernel(device, own, other, in_rows, grad_w_out, grad_w_in):
    core = device[0] & 1
    grad_w_in[...] = in_rows[...]
    members, rows, _ = own.shape
    for place, blocks in ((core, own), (1 - core, other)):
        for m in range(0, members, 2):
            pair = [blocks[i].astype(jnp.float32) for i in (m, m + 1)]
            start = pl.multiple_of((place * members + m) * rows, 2 * rows)
            grad_w_out[pl.ds(start, 2 * rows), :] = jnp.concatenate(pair, axis=0).astype(jnp.bfloat16)


def call(kernel, outs, scratch, scalars, arrays, flops, nbytes, space=pltpu.VMEM):
    if space == pltpu.HBM:
        arrays = [pltpu.with_memory_space_constraint(array, pltpu.HBM) for array in arrays]
    in_specs = [pl.BlockSpec(memory_space=pltpu.SMEM)] * len(scalars)
    in_specs += [pl.BlockSpec(memory_space=space)] * len(arrays)
    return pl.pallas_call(
        kernel,
        out_shape=[jax.ShapeDtypeStruct(shape, kind) for shape, kind in outs],
        in_specs=in_specs,
        out_specs=[pl.BlockSpec(memory_space=pltpu.VMEM)] * len(outs),
        scratch_shapes=scratch,
        compiler_params=pltpu.CompilerParams(vmem_limit_bytes=VMEM_LIMIT),
        cost_estimate=pl.CostEstimate(flops=flops, bytes_accessed=nbytes, transcendentals=0),
    )(*scalars, *arrays)


F32, B16 = jnp.float32, jnp.bfloat16


def edges(flags, features, cotangent, layer_scale):
    rows, width = features.shape
    wide = pltpu.VMEM((width // LANES, rows, LANES), F32)
    return call(
        edge_kernel,
        [((EDGE, width), B16), ((EDGE, width), B16)],
        [pltpu.SMEM(flags.shape, jnp.int32), pltpu.VMEM((rows, width), B16), pltpu.VMEM((rows, width), B16),
         pltpu.VMEM((width,), F32), wide, wide, pltpu.SemaphoreType.DMA((4,))],
        [],
        [flags, features, cotangent, layer_scale],
        features.size, 4 * features.size, pltpu.HBM,
    )


def before_halos(flags, features, cotangent, kernel, conv_bias, gain, bias, w_in, b_in, w_out, layer_scale):
    rows, width = features.shape
    hidden = w_out.shape[0]
    return call(
        first_kernel,
        [((rows, width), F32), ((rows, width), B16), ((hidden, rows), F32), ((hidden, width), B16),
         ((hidden, LANES), F32), (w_in.shape, B16), (w_out.shape, B16), (kernel.shape, F32), ((3 * SIDE, width), F32)],
        [pltpu.VMEM((width // LANES, rows, LANES), F32), pltpu.SMEM(flags.shape, jnp.int32),
         pltpu.VMEM((rows, width), B16), pltpu.VMEM((rows, width), B16),
         pltpu.VMEM(b_in.shape, F32), pltpu.VMEM((width,), F32), pltpu.VMEM((width,), F32),
         pltpu.VMEM((width,), F32), pltpu.VMEM((width,), F32),
         pltpu.SemaphoreType.DMA((11,))],
        [],
        [flags, features, cotangent, w_out, w_in, b_in, kernel, layer_scale, conv_bias, gain, bias],
        2 * rows * width * hidden, 8 * 1024 * 1024, pltpu.HBM,
    )


def middle(device, conv, low, high, taps, vectors, w_in_t, b_cols, out_grad, back):
    rows, width = conv.shape
    hidden = w_in_t.shape[0]
    halo = pltpu.VMEM((EDGE, width), F32)
    return call(
        middle_kernel,
        [((hidden, width), F32), ((hidden, width), B16), ((rows, width), F32), ((rows, LANES), F32), ((hidden, rows), B16)],
        [pltpu.VMEM((rows, width), F32), halo, halo, pltpu.VMEM((rows, width), B16),
         pltpu.VMEM((hidden, rows), F32), pltpu.VMEM((hidden, rows), B16)],
        [device],
        [conv, low, high, taps, vectors, w_in_t, b_cols, out_grad, back],
        6 * rows * width * hidden, 12 * 1024 * 1024,
    )


def to_conv(grad_pre, w_in, standard, inverse, vectors, *more):
    rows, width = standard.shape
    hidden = grad_pre.shape[0]
    edge = (HALO * SIDE, width)
    return call(
        back_kernel, [((rows, width), F32), (edge, F32), (edge, F32)],
        [pltpu.VMEM((LANES, width), F32), pltpu.VMEM((LANES, width), B16), pltpu.VMEM((hidden, LANES), F32),
         pltpu.VMEM((hidden, LANES), F32), pltpu.VMEM((hidden, LANES), B16)],
        [],
        [grad_pre, w_in, standard, inverse, vectors, *more],
        2 * grad_pre.size * width, 4 * grad_pre.size,
    )


def to_features(grad_conv, low, high, taps, cotangent):
    rows, width = grad_conv.shape
    return call(
        last_kernel,
        [((rows, width), B16)],
        [pltpu.VMEM((width // LANES, rows, LANES), F32)],
        [],
        [grad_conv, low, high, taps, cotangent],
        2 * 49 * rows * width, 2 * 1024 * 1024,
    )[0]


def to_cube(members, kept, received):
    rows, width = kept.shape
    return call(
        cube_kernel, [((members, rows // members, width), B16)], [], [], [kept, received], 2 * kept.size, 8 * kept.size
    )[0]


def to_four(received, members):
    _, rows, width = received.shape
    return call(
        four_kernel, [((members, rows // members, width), B16)],
        [pltpu.VMEM((width // LANES, rows, LANES), F32)], [], [received],
        received.size, 3 * received.size,
    )[0]


def to_eight(received, members):
    _, rows, width = received.shape
    return call(
        eight_kernel,
        [((members, rows // 2 + SIDE, width), B16)],
        [pltpu.VMEM((width // LANES, rows, LANES), F32), pltpu.VMEM((rows // 2 + SIDE, width), F32)],
        [],
        [received],
        received.size, 4 * received.size,
    )[0]


def turn(scale, received, members):
    _, rows, width = received.shape
    return call(
        functools.partial(turn_kernel, scale),
        [((members, rows - SIDE, width), B16), ((ROWS, width), F32)], [], [], [received],
        received.size, 4 * received.size,
    )


def join(device, own, other, in_rows):
    members, rows, width = own.shape
    return call(
        join_kernel, [((2 * members * rows, width), B16), (in_rows.shape, F32)], [], [device], [own, other, in_rows],
        own.size, 8 * own.size,
    )


def from_left(block):
    count = lax.axis_size(TILE)
    return lax.ppermute(block, TILE, [(i, i + 1) for i in range(count - 1)])


def from_right(block):
    count = lax.axis_size(TILE)
    return lax.ppermute(block, TILE, [(i + 1, i) for i in range(count - 1)])


def exchange(blocks, axes):
    return lax.all_to_all(blocks, axes, split_axis=0, concat_axis=0, tiled=True)


def swap(block):
    return lax.ppermute(block, "c", SWAP)


def body(
    features, cotangent, kernel, conv_bias, ln_gain, ln_bias, w_in, b_in, w_out, layer_scale, tissue
):
    image = features[0]
    height, breadth, channels = image.shape
    rows = image.reshape(-1, channels)
    upstream = cotangent[0].reshape(-1, channels)
    own_low, own_high = edges(tissue, rows, upstream, layer_scale)
    low, high = from_left(own_high), from_right(own_low)
    device = lax.axis_index(EVERY).astype(jnp.int32).reshape(1)
    sizes = {axis: lax.axis_size(axis) for axis in EVERY}
    cube, four, eight = (math.prod(sizes[axis] for axis in axes) for axes in (CUBE, FOUR, EIGHT))
    scale = 1.0 / math.sqrt(height * breadth * math.prod(sizes.values()))

    conv, out_grad, back, w_in_t, b_cols, w_in_here, w_out_here, taps, vectors = before_halos(
        tissue, rows, upstream, kernel, conv_bias, ln_gain, ln_bias, w_in, b_in, w_out, layer_scale
    )
    kept, sent, standard, inverse, grad_pre = middle(
        device, conv, low, high, taps, vectors, w_in_t, b_cols, out_grad, back
    )
    grad_conv, low, high = to_conv(
        grad_pre, w_in_here, standard, inverse, vectors,
        w_out_here, w_in_t, b_cols, taps, own_low, own_high, low, high,
    )
    kept, low, high = lax.optimization_barrier((kept, low, high))
    received = exchange(to_cube(cube, kept, swap(sent)), CUBE)
    received = exchange(to_four(received, four), FOUR)
    received = exchange(to_eight(received, eight), EIGHT)
    message, in_rows = turn(scale, received, cube * four)
    own = exchange(message, CUBE + FOUR)
    pairs = [(2 * xh + c, 2 * c + xh) for xh in range(2) for c in range(2)]
    in_rows = lax.ppermute(in_rows, ("xh", "c"), pairs)
    message, low, high = lax.optimization_barrier((message, low, high))
    grad_image = to_features(grad_conv, low, high, taps, upstream)
    own, in_rows, grad_image = lax.optimization_barrier((own, in_rows, grad_image))
    grad_w_out, grad_w_in = join(device, own, swap(own), in_rows)
    return (grad_image.reshape(1, height, breadth, channels), grad_w_in, grad_w_out)


def solution(mesh):
    fine = jax.sharding.Mesh(mesh.devices.reshape(4, 2, 2, 2, 2, 2, 2, 2), EVERY)
    band = P(("zl", "c"), None, TILE, None)
    placed = (band, band) + (P(),) * 8 + (P(("zl", "c"), TILE),)
    return jax.shard_map(
        body,
        mesh=fine,
        in_specs=placed,
        out_specs=(band, P(EVERY, None), P()),
        check_vma=False,
    )
```

```python
import functools
import itertools
import math

import jax
import jax.numpy as jnp
from jax import lax
from jax.experimental import pallas as pl
from jax.experimental.pallas import tpu as pltpu
from jax.sharding import PartitionSpec as P

SIDE = 8
HALO = 3
TAPS = 7
COLS = 32
LANES = 128
CHUNK = 32
ROWS = 3
EDGE = 10 * SIDE
EPSILON = 1e-06
VMEM_LIMIT = 16 * 1024 * 1024
NT = (((1,), (1,)), ((), ()))

TILE = ("zh", "xh", "xl", "y2", "y1", "yl")
CUBE = ("xl", "yl", "zl")
FOUR = ("xh", "y1")
EIGHT = ("zh", "y2")
EVERY = ("zh", "xh", "xl", "y2", "y1", "yl", "zl", "c")
SWAP = [(0, 1), (1, 0)]


def matmul(left, right, dims=(((1,), (0,)), ((), ()))):
    return lax.dot_general(left, right, dims, preferred_element_type=jnp.float32)


def shifted(column, a):
    move = a - HALO
    if move == 0:
        return column
    row = lax.broadcasted_iota(jnp.int32, column.shape, 0)
    inside = (row + move >= 0) & (row + move < SIDE)
    return jnp.where(inside, pltpu.roll(column, (-move) % SIDE, 0), 0.0)


def convolve(columns, taps, lanes, flip):
    count = len(columns) - 2 * HALO
    totals = [None] * count
    for a in range(TAPS):
        sums = [None] * count
        for e in range(TAPS):
            row, place = (TAPS - 1 - a, TAPS - 1 - e) if flip else (a, e)
            tap = taps[row, place : place + 1, lanes]
            for j in range(count):
                if columns[j + e] is None:
                    continue
                term = columns[j + e] * tap
                sums[j] = term if sums[j] is None else sums[j] + term
        for j in range(count):
            if sums[j] is None:
                continue
            moved = shifted(sums[j], a)
            totals[j] = moved if totals[j] is None else totals[j] + moved
    return totals


def lane_blocks(width):
    return [slice(start, start + LANES) for start in range(0, width, LANES)]


def widen(source, wide):
    for k, lanes in enumerate(lane_blocks(source.shape[1])):
        wide[k] = source[:, lanes].astype(jnp.float32)


def edge_kernel(
    flags, features, cotangent, scale, low, high, flags_here, image, upstream, scale_here, wide, wide_grad, sems
):
    pairs = [(features, image), (cotangent, upstream), (scale, scale_here), (flags, flags_here)]
    copies = [pltpu.make_async_copy(src, dst, sems.at[i]) for i, (src, dst) in enumerate(pairs)]
    for copy in copies:
        copy.start()
    for copy in copies:
        copy.wait()
    widen(image, wide)
    widen(upstream, wide_grad)
    by_lane = scale_here[...].reshape(1, features.shape[1])
    for k, lanes in enumerate(lane_blocks(features.shape[1])):
        for first, first_grad, edge in ((0, 0, low), (COLS - 2 * HALO, COLS - HALO, high)):
            columns = [wide[k, pl.ds(first + j, SIDE, stride=COLS), :] for j in range(2 * HALO)]
            gate = flags_here[0, first_grad // SIDE].astype(jnp.float32)
            for j in range(HALO):
                column = wide_grad[k, pl.ds(first_grad + j, SIDE, stride=COLS), :]
                columns.append(column * by_lane[:, lanes] * gate)
            columns.append(jnp.zeros((SIDE, LANES), jnp.float32))
            edge[:, lanes] = jnp.concatenate(columns, axis=0).astype(jnp.bfloat16)


def first_kernel(
    flags, features, cotangent, w_out, w_in, b_in, taps, scale, conv_bias, gain, bias,
    conv, out_grad, back, w_in_t, b_cols, w_in_here, w_out_here, taps_here, vectors,
    wide, flags_here, image, upstream, b_here, scale_here, conv_bias_here, gain_here, bias_here, sems
):
    width = features.shape[1]
    pairs = [
        (flags, flags_here), (cotangent, upstream), (scale, scale_here), (w_out, w_out_here),
        (features, image), (taps, taps_here), (w_in, w_in_here), (b_in, b_here),
        (conv_bias, conv_bias_here), (gain, gain_here), (bias, bias_here),
    ]
    copies = [pltpu.make_async_copy(src, dst, sems.at[i]) for i, (src, dst) in enumerate(pairs)]
    for copy in copies:
        copy.start()
    for copy in copies[:3]:
        copy.wait()
    widen(upstream, wide)
    rows = SIDE * SIDE
    by_lane = scale_here[...].reshape(1, width)
    for k, lanes in enumerate(lane_blocks(width)):
        for t in range(COLS // SIDE):
            gate = flags_here[0, t].astype(jnp.float32)
            tile = jnp.concatenate(
                [wide[k, pl.ds(t * SIDE + j, SIDE, stride=COLS), :] for j in range(SIDE)], axis=0
            )
            tile = (tile * by_lane[:, lanes] * gate).astype(jnp.bfloat16)
            out_grad[t * rows : (t + 1) * rows, lanes] = tile
    copies[3].wait()
    back[...] = matmul(w_out_here[...], out_grad[...], NT)
    copies[4].wait()
    copies[5].wait()
    widen(image, wide)
    def convolve_tile(t):
        for k, lanes in enumerate(lane_blocks(width)):
            columns = []
            for j in range(t * SIDE - HALO, (t + 1) * SIDE + HALO):
                inside = 0 <= j < COLS
                columns.append(wide[k, pl.ds(j, SIDE, stride=COLS), :] if inside else None)
            for j, total in enumerate(convolve(columns, taps_here, lanes, False)):
                start = (t * SIDE + j) * SIDE
                conv[start : start + SIDE, lanes] = total

    for t in range(COLS // SIDE):
        tissue = flags_here[0, t] != 0
        pl.when(tissue)(functools.partial(convolve_tile, t))

        @pl.when(jnp.logical_not(tissue))
        def _(t=t):
            conv[t * rows : (t + 1) * rows, :] = jnp.zeros((rows, width), jnp.float32)

    for copy in copies[6:]:
        copy.wait()
    hidden = w_in.shape[1]
    for start in range(0, hidden, LANES):
        w_in_t[start : start + LANES, :] = w_in_here[:, start : start + LANES].T
        b_cols[start : start + LANES, :] = jnp.broadcast_to(
            b_here[start : start + LANES].reshape(1, LANES), (LANES, LANES)
        ).T
    for i, vector in enumerate((conv_bias_here, gain_here, bias_here)):
        vectors[i * SIDE : (i + 1) * SIDE, :] = jnp.broadcast_to(
            vector[...].reshape(1, width), (SIDE, width)
        )


def middle_kernel(
    device, conv, low, high, taps, vectors, w_in_t, b_cols, out_grad, back,
    kept, sent, standard, inverse, grad_pre,
    rows, low_wide, high_wide, normed, preact, hidden
):
    width = conv.shape[1]
    rows[...] = conv[...]
    low_wide[...] = low[...].astype(jnp.float32)
    high_wide[...] = high[...].astype(jnp.float32)
    for lanes in lane_blocks(width):
        near = [low_wide[(HALO + j) * SIDE : (HALO + j + 1) * SIDE, lanes] for j in range(HALO)]
        for j, total in enumerate(convolve(near + [None] * (2 * HALO), taps, lanes, False)):
            rows[j * SIDE : (j + 1) * SIDE, lanes] += total
        near = [high_wide[j * SIDE : (j + 1) * SIDE, lanes] for j in range(HALO)]
        for j, total in enumerate(convolve([None] * (2 * HALO) + near, taps, lanes, False)):
            start = (COLS - HALO + j) * SIDE
            rows[start : start + SIDE, lanes] += total
    gain, bias = vectors[SIDE : SIDE + 1, :], vectors[2 * SIDE : 2 * SIDE + 1, :]
    conv_out = rows[...] + vectors[:1, :]
    centre = conv_out - jnp.mean(conv_out, axis=-1, keepdims=True)
    scale = lax.rsqrt(jnp.mean(centre * centre, axis=-1, keepdims=True) + EPSILON)
    inverse[...] = jnp.broadcast_to(scale, inverse.shape)
    standard[...] = centre * scale
    normed[...] = (standard[...] * gain + bias).astype(jnp.bfloat16)
    preact[...] = matmul(w_in_t[...], normed[...], NT)

    def step(i, carry):
        part = pl.ds(pl.multiple_of(i * CHUNK, CHUNK), CHUNK)
        for lanes in lane_blocks(preact.shape[1]):
            z = preact[part, lanes] + b_cols[part, :]
            below = 0.5 * (1.0 + lax.erf(z * 0.7071067811865476))
            density = jnp.exp(-0.5 * z * z) * 0.3989422804014327
            hidden[part, lanes] = (z * below).astype(jnp.bfloat16)
            slope = below + z * density
            grad_pre[part, lanes] = (back[part, lanes] * slope).astype(jnp.bfloat16)
        return carry

    lax.fori_loop(0, preact.shape[0] // CHUNK, step, 0, unroll=2)
    half = hidden.shape[0] // 2
    core = device[0] & 1
    other = pl.ds(pl.multiple_of((1 - core) * half, half), half)
    own = pl.ds(pl.multiple_of(core * half, half), half)
    sent[:half, :] = matmul(hidden[other, :], out_grad[...]).astype(jnp.bfloat16)
    kept[:half, :] = matmul(hidden[own, :], out_grad[...])
    run = 64 * ROWS
    for i in range(half // run):
        place = half + i * run
        start = pl.multiple_of((2 * i + 1 - core) * run, run)
        sent[place : place + run, :] = matmul(grad_pre[pl.ds(start, run), :], normed[...]).astype(jnp.bfloat16)
        start = pl.multiple_of((2 * i + core) * run, run)
        kept[place : place + run, :] = matmul(grad_pre[pl.ds(start, run), :], normed[...])


def through_norm(grad_std, standard, inverse):
    mean = jnp.mean(grad_std, axis=-1, keepdims=True)
    along = jnp.mean(grad_std * standard, axis=-1, keepdims=True)
    return inverse * (grad_std - mean - standard * along)


def back_kernel(
    grad_pre, w_in, standard, inverse, vectors, w_out, w_in_t, b_cols, taps, own_low, own_high, low, high,
    grad_conv, low_conv, high_conv,
    rows, out_grad, preact, back, halo_pre
):
    conv_bias, gain, bias = (vectors[i * SIDE : i * SIDE + 1, :] for i in range(3))
    grad_std = matmul(w_in[...], grad_pre[...]).T * gain
    grad_conv[...] = through_norm(grad_std, standard[...], inverse[:, :1])

    edge = HALO * SIDE
    rows[...] = jnp.zeros_like(rows)
    for lanes in lane_blocks(rows.shape[1]):
        near, far = ([x[:, lanes].astype(jnp.float32) for x in pair] for pair in ((own_low, own_high), (low, high)))
        for i in range(2):
            column = lambda block, j: block[j * SIDE : (j + 1) * SIDE, :]
            beyond = [column(far[i], j) for j in range(2 * HALO)]
            inside = [column(near[i], j + i * HALO) for j in range(HALO)]
            columns = inside + beyond if i else beyond + inside
            for j, total in enumerate(convolve(columns, taps, lanes, False)):
                start = i * edge + j * SIDE
                rows[start : start + SIDE, lanes] = total
        grads = [block[2 * edge : 3 * edge, :] for block in far]
        grads.append(jnp.zeros((rows.shape[0] - 2 * edge, LANES), jnp.float32))
        out_grad[:, lanes] = jnp.concatenate(grads, axis=0).astype(jnp.bfloat16)
    conv_out = rows[...] + conv_bias
    centre = conv_out - jnp.mean(conv_out, axis=-1, keepdims=True)
    scale = lax.rsqrt(jnp.mean(centre * centre, axis=-1, keepdims=True) + EPSILON)
    norm = centre * scale
    preact[...] = matmul(w_in_t[...], (norm * gain + bias).astype(jnp.bfloat16), NT)
    back[...] = matmul(w_out[...], out_grad[...], NT)

    def step(i, carry):
        part = pl.ds(pl.multiple_of(i * CHUNK, CHUNK), CHUNK)
        z = preact[part, :] + b_cols[part, :]
        below = 0.5 * (1.0 + lax.erf(z * 0.7071067811865476))
        density = jnp.exp(-0.5 * z * z) * 0.3989422804014327
        halo_pre[part, :] = (back[part, :] * (below + z * density)).astype(jnp.bfloat16)
        return carry

    lax.fori_loop(0, preact.shape[0] // CHUNK, step, 0, unroll=4)
    grad_std = matmul(w_in[...], halo_pre[...]).T * gain
    result = through_norm(grad_std, norm, scale)
    low_conv[...] = result[:edge, :]
    high_conv[...] = result[edge : 2 * edge, :]


def last_kernel(grad_conv, low, high, taps, cotangent, grad_features, wide):
    for k, lanes in enumerate(lane_blocks(grad_conv.shape[1])):
        for t in range(COLS // SIDE):
            columns = []
            for j in range(t * SIDE - HALO, (t + 1) * SIDE + HALO):
                if j < 0:
                    source, place = low, j + HALO
                elif j >= COLS:
                    source, place = high, j - COLS
                else:
                    source, place = grad_conv, j
                columns.append(source[place * SIDE : (place + 1) * SIDE, lanes])
            for j, total in enumerate(convolve(columns, taps, lanes, True)):
                wide[k, pl.ds(t * SIDE + j, SIDE, stride=COLS), :] = total
        result = cotangent[:, lanes].astype(jnp.float32) + wide[k]
        grad_features[:, lanes] = result.astype(jnp.bfloat16)


def cube_kernel(kept, received, message):
    members, rows, _ = message.shape
    rows //= 2
    half = members * rows
    for m in range(members):
        part = slice(m * rows, (m + 1) * rows)
        total = kept[part, :] + received[part, :].astype(jnp.float32)
        message[m, :rows, :] = total.astype(jnp.bfloat16)
    run = 2 * ROWS
    for top, bit5 in itertools.product(range(2), repeat=2):
        totals = []
        for i in (2 * top, 2 * top + 1):
            start = half + (2 * i + bit5) * rows
            totals.append(kept[start : start + rows, :] + received[start : start + rows, :].astype(jnp.float32))
        for low in range(4):
            runs = [
                total[(4 * i + low) * run : (4 * i + low + 1) * run, :] for total in totals for i in range(4)
            ]
            place = rows + top * 8 * run
            message[bit5 * 4 + low, place : place + 8 * run, :] = jnp.concatenate(runs, axis=0).astype(jnp.bfloat16)


def add_members(received):
    summed = received[0].astype(jnp.float32)
    for i in range(1, received.shape[0]):
        summed += received[i].astype(jnp.float32)
    return summed


def four_kernel(received, message, total):
    members, rows, width = message.shape
    rows //= 2
    summed = add_members(received)
    for k, lanes in enumerate(lane_blocks(width)):
        total[k] = summed[:, lanes]
        for m in range(members):
            parts = [total[k, m * rows : (m + 1) * rows, :]]
            for r in range(ROWS):
                start = members * rows + (m % 2) * 2 * ROWS + (m // 2) * ROWS + r
                parts.append(total[k, pl.ds(start, SIDE, stride=members * ROWS), :])
            message[m, :, lanes] = jnp.concatenate(parts, axis=0).astype(jnp.bfloat16)


def eight_kernel(received, message, total, block):
    rows = received.shape[1] // 2
    members = message.shape[0]
    summed = add_members(received)
    for k, lanes in enumerate(lane_blocks(received.shape[2])):
        total[k] = summed[:, lanes]
    block[...] = jnp.zeros_like(block)
    block[:rows, :] = summed[:rows, :]
    for m in range(members):
        for k, lanes in enumerate(lane_blocks(received.shape[2])):
            block[rows : rows + ROWS, lanes] = total[k, pl.ds(rows + m, ROWS, stride=members), :]
        message[m] = block[...].astype(jnp.bfloat16)


def turn_kernel(scale, received, message, grad_w_in):
    finished = add_members(received) * scale
    rows = message.shape[1]
    grad_w_in[...] = finished[rows : rows + ROWS, :]
    whole = finished[:rows, :].astype(jnp.bfloat16)
    for m in range(message.shape[0]):
        message[m] = whole


def join_kernel(device, own, other, in_rows, grad_w_out, grad_w_in):
    core = device[0] & 1
    grad_w_in[...] = in_rows[...]
    members, rows, _ = own.shape
    for place, blocks in ((core, own), (1 - core, other)):
        for m in range(0, members, 2):
            pair = [blocks[i].astype(jnp.float32) for i in (m, m + 1)]
            start = pl.multiple_of((place * members + m) * rows, 2 * rows)
            grad_w_out[pl.ds(start, 2 * rows), :] = jnp.concatenate(pair, axis=0).astype(jnp.bfloat16)


def call(kernel, outs, scratch, scalars, arrays, flops, nbytes, space=pltpu.VMEM):
    if space == pltpu.HBM:
        arrays = [pltpu.with_memory_space_constraint(array, pltpu.HBM) for array in arrays]
    in_specs = [pl.BlockSpec(memory_space=pltpu.SMEM)] * len(scalars)
    in_specs += [pl.BlockSpec(memory_space=space)] * len(arrays)
    return pl.pallas_call(
        kernel,
        out_shape=[jax.ShapeDtypeStruct(shape, kind) for shape, kind in outs],
        in_specs=in_specs,
        out_specs=[pl.BlockSpec(memory_space=pltpu.VMEM)] * len(outs),
        scratch_shapes=scratch,
        compiler_params=pltpu.CompilerParams(vmem_limit_bytes=VMEM_LIMIT),
        cost_estimate=pl.CostEstimate(flops=flops, bytes_accessed=nbytes, transcendentals=0),
    )(*scalars, *arrays)


F32, B16 = jnp.float32, jnp.bfloat16


def edges(flags, features, cotangent, layer_scale):
    rows, width = features.shape
    wide = pltpu.VMEM((width // LANES, rows, LANES), F32)
    return call(
        edge_kernel,
        [((EDGE, width), B16), ((EDGE, width), B16)],
        [pltpu.SMEM(flags.shape, jnp.int32), pltpu.VMEM((rows, width), B16), pltpu.VMEM((rows, width), B16),
         pltpu.VMEM((width,), F32), wide, wide, pltpu.SemaphoreType.DMA((4,))],
        [],
        [flags, features, cotangent, layer_scale],
        features.size, 4 * features.size, pltpu.HBM,
    )


def before_halos(flags, features, cotangent, kernel, conv_bias, gain, bias, w_in, b_in, w_out, layer_scale):
    rows, width = features.shape
    hidden = w_out.shape[0]
    return call(
        first_kernel,
        [((rows, width), F32), ((rows, width), B16), ((hidden, rows), F32), ((hidden, width), B16),
         ((hidden, LANES), F32), (w_in.shape, B16), (w_out.shape, B16), (kernel.shape, F32), ((3 * SIDE, width), F32)],
        [pltpu.VMEM((width // LANES, rows, LANES), F32), pltpu.SMEM(flags.shape, jnp.int32),
         pltpu.VMEM((rows, width), B16), pltpu.VMEM((rows, width), B16),
         pltpu.VMEM(b_in.shape, F32), pltpu.VMEM((width,), F32), pltpu.VMEM((width,), F32),
         pltpu.VMEM((width,), F32), pltpu.VMEM((width,), F32),
         pltpu.SemaphoreType.DMA((11,))],
        [],
        [flags, features, cotangent, w_out, w_in, b_in, kernel, layer_scale, conv_bias, gain, bias],
        2 * rows * width * hidden, 8 * 1024 * 1024, pltpu.HBM,
    )


def middle(device, conv, low, high, taps, vectors, w_in_t, b_cols, out_grad, back):
    rows, width = conv.shape
    hidden = w_in_t.shape[0]
    halo = pltpu.VMEM((EDGE, width), F32)
    return call(
        middle_kernel,
        [((hidden, width), F32), ((hidden, width), B16), ((rows, width), F32), ((rows, LANES), F32), ((hidden, rows), B16)],
        [pltpu.VMEM((rows, width), F32), halo, halo, pltpu.VMEM((rows, width), B16),
         pltpu.VMEM((hidden, rows), F32), pltpu.VMEM((hidden, rows), B16)],
        [device],
        [conv, low, high, taps, vectors, w_in_t, b_cols, out_grad, back],
        6 * rows * width * hidden, 12 * 1024 * 1024,
    )


def to_conv(grad_pre, w_in, standard, inverse, vectors, *more):
    rows, width = standard.shape
    hidden = grad_pre.shape[0]
    edge = (HALO * SIDE, width)
    return call(
        back_kernel, [((rows, width), F32), (edge, F32), (edge, F32)],
        [pltpu.VMEM((LANES, width), F32), pltpu.VMEM((LANES, width), B16), pltpu.VMEM((hidden, LANES), F32),
         pltpu.VMEM((hidden, LANES), F32), pltpu.VMEM((hidden, LANES), B16)],
        [],
        [grad_pre, w_in, standard, inverse, vectors, *more],
        2 * grad_pre.size * width, 4 * grad_pre.size,
    )


def to_features(grad_conv, low, high, taps, cotangent):
    rows, width = grad_conv.shape
    return call(
        last_kernel,
        [((rows, width), B16)],
        [pltpu.VMEM((width // LANES, rows, LANES), F32)],
        [],
        [grad_conv, low, high, taps, cotangent],
        2 * 49 * rows * width, 2 * 1024 * 1024,
    )[0]


def to_cube(members, kept, received):
    rows, width = kept.shape
    return call(
        cube_kernel, [((members, rows // members, width), B16)], [], [], [kept, received], 2 * kept.size, 8 * kept.size
    )[0]


def to_four(received, members):
    _, rows, width = received.shape
    return call(
        four_kernel, [((members, rows // members, width), B16)],
        [pltpu.VMEM((width // LANES, rows, LANES), F32)], [], [received],
        received.size, 3 * received.size,
    )[0]


def to_eight(received, members):
    _, rows, width = received.shape
    return call(
        eight_kernel,
        [((members, rows // 2 + SIDE, width), B16)],
        [pltpu.VMEM((width // LANES, rows, LANES), F32), pltpu.VMEM((rows // 2 + SIDE, width), F32)],
        [],
        [received],
        received.size, 4 * received.size,
    )[0]


def turn(scale, received, members):
    _, rows, width = received.shape
    return call(
        functools.partial(turn_kernel, scale),
        [((members, rows - SIDE, width), B16), ((ROWS, width), F32)], [], [], [received],
        received.size, 4 * received.size,
    )


def join(device, own, other, in_rows):
    members, rows, width = own.shape
    return call(
        join_kernel, [((2 * members * rows, width), B16), (in_rows.shape, F32)], [], [device], [own, other, in_rows],
        own.size, 8 * own.size,
    )


def from_left(block):
    count = lax.axis_size(TILE)
    return lax.ppermute(block, TILE, [(i, i + 1) for i in range(count - 1)])


def from_right(block):
    count = lax.axis_size(TILE)
    return lax.ppermute(block, TILE, [(i + 1, i) for i in range(count - 1)])


def exchange(blocks, axes):
    return lax.all_to_all(blocks, axes, split_axis=0, concat_axis=0, tiled=True)


def swap(block):
    return lax.ppermute(block, "c", SWAP)


def body(
    features, cotangent, kernel, conv_bias, ln_gain, ln_bias, w_in, b_in, w_out, layer_scale, tissue
):
    image = features[0]
    height, breadth, channels = image.shape
    rows = image.reshape(-1, channels)
    upstream = cotangent[0].reshape(-1, channels)
    own_low, own_high = edges(tissue, rows, upstream, layer_scale)
    low, high = from_left(own_high), from_right(own_low)
    device = lax.axis_index(EVERY).astype(jnp.int32).reshape(1)
    sizes = {axis: lax.axis_size(axis) for axis in EVERY}
    cube, four, eight = (math.prod(sizes[axis] for axis in axes) for axes in (CUBE, FOUR, EIGHT))
    scale = 1.0 / math.sqrt(height * breadth * math.prod(sizes.values()))

    conv, out_grad, back, w_in_t, b_cols, w_in_here, w_out_here, taps, vectors = before_halos(
        tissue, rows, upstream, kernel, conv_bias, ln_gain, ln_bias, w_in, b_in, w_out, layer_scale
    )
    kept, sent, standard, inverse, grad_pre = middle(
        device, conv, low, high, taps, vectors, w_in_t, b_cols, out_grad, back
    )
    grad_conv, low, high = to_conv(
        grad_pre, w_in_here, standard, inverse, vectors,
        w_out_here, w_in_t, b_cols, taps, own_low, own_high, low, high,
    )
    kept, low, high = lax.optimization_barrier((kept, low, high))
    received = exchange(to_cube(cube, kept, swap(sent)), CUBE)
    received = exchange(to_four(received, four), FOUR)
    received, low, high = lax.optimization_barrier((received, low, high))
    grad_image = to_features(grad_conv, low, high, taps, upstream)
    received = exchange(to_eight(received, eight), EIGHT)
    received, grad_image = lax.optimization_barrier((received, grad_image))
    message, in_rows = turn(scale, received, cube * four)
    own = exchange(message, CUBE + FOUR)
    own, in_rows = lax.optimization_barrier((own, in_rows))
    pairs = [(2 * xh + c, 2 * c + xh) for xh in range(2) for c in range(2)]
    in_rows = lax.ppermute(in_rows, ("xh", "c"), pairs)
    grad_w_out, grad_w_in = join(device, own, swap(own), in_rows)
    return (grad_image.reshape(1, height, breadth, channels), grad_w_in, grad_w_out)


def solution(mesh):
    fine = jax.sharding.Mesh(mesh.devices.reshape(4, 2, 2, 2, 2, 2, 2, 2), EVERY)
    band = P(("zl", "c"), None, TILE, None)
    placed = (band, band) + (P(),) * 8 + (P(("zl", "c"), TILE),)
    return jax.shard_map(
        body,
        mesh=fine,
        in_specs=placed,
        out_specs=(band, P(EVERY, None), P()),
        check_vma=False,
    )
```

```python
import functools
import itertools
import math

import jax
import jax.numpy as jnp
from jax import lax
from jax.experimental import pallas as pl
from jax.experimental.pallas import tpu as pltpu
from jax.sharding import PartitionSpec as P

SIDE = 8
HALO = 3
TAPS = 7
COLS = 32
LANES = 128
CHUNK = 32
ROWS = 3
EDGE = 10 * SIDE
EPSILON = 1e-06
VMEM_LIMIT = 16 * 1024 * 1024
NT = (((1,), (1,)), ((), ()))

TILE = ("zh", "xh", "xl", "y2", "y1", "yl")
CUBE = ("xl", "yl", "zl")
FOUR = ("xh", "y1")
EIGHT = ("zh", "y2")
EVERY = ("zh", "xh", "xl", "y2", "y1", "yl", "zl", "c")
SWAP = [(0, 1), (1, 0)]


def matmul(left, right, dims=(((1,), (0,)), ((), ()))):
    return lax.dot_general(left, right, dims, preferred_element_type=jnp.float32)


def shifted(column, a):
    move = a - HALO
    if move == 0:
        return column
    row = lax.broadcasted_iota(jnp.int32, column.shape, 0)
    inside = (row + move >= 0) & (row + move < SIDE)
    return jnp.where(inside, pltpu.roll(column, (-move) % SIDE, 0), 0.0)


def convolve(columns, taps, lanes, flip):
    count = len(columns) - 2 * HALO
    totals = [None] * count
    for a in range(TAPS):
        sums = [None] * count
        for e in range(TAPS):
            row, place = (TAPS - 1 - a, TAPS - 1 - e) if flip else (a, e)
            tap = taps[row, place : place + 1, lanes]
            for j in range(count):
                if columns[j + e] is None:
                    continue
                term = columns[j + e] * tap
                sums[j] = term if sums[j] is None else sums[j] + term
        for j in range(count):
            if sums[j] is None:
                continue
            moved = shifted(sums[j], a)
            totals[j] = moved if totals[j] is None else totals[j] + moved
    return totals


def lane_blocks(width):
    return [slice(start, start + LANES) for start in range(0, width, LANES)]


def widen(source, wide):
    for k, lanes in enumerate(lane_blocks(source.shape[1])):
        wide[k] = source[:, lanes].astype(jnp.float32)


def edge_kernel(
    flags, features, cotangent, scale, low, high, flags_here, image, upstream, scale_here, wide, wide_grad, sems
):
    pairs = [(features, image), (cotangent, upstream), (scale, scale_here), (flags, flags_here)]
    copies = [pltpu.make_async_copy(src, dst, sems.at[i]) for i, (src, dst) in enumerate(pairs)]
    for copy in copies:
        copy.start()
    for copy in copies:
        copy.wait()
    widen(image, wide)
    widen(upstream, wide_grad)
    by_lane = scale_here[...].reshape(1, features.shape[1])
    for k, lanes in enumerate(lane_blocks(features.shape[1])):
        for first, first_grad, edge in ((0, 0, low), (COLS - 2 * HALO, COLS - HALO, high)):
            columns = [wide[k, pl.ds(first + j, SIDE, stride=COLS), :] for j in range(2 * HALO)]
            gate = flags_here[0, first_grad // SIDE].astype(jnp.float32)
            for j in range(HALO):
                column = wide_grad[k, pl.ds(first_grad + j, SIDE, stride=COLS), :]
                columns.append(column * by_lane[:, lanes] * gate)
            columns.append(jnp.zeros((SIDE, LANES), jnp.float32))
            edge[:, lanes] = jnp.concatenate(columns, axis=0).astype(jnp.bfloat16)


def first_kernel(
    flags, features, cotangent, w_out, w_in, b_in, taps, scale, conv_bias, gain, bias,
    conv, out_grad, back, w_in_t, b_cols, w_in_here, w_out_here, taps_here, vectors,
    wide, flags_here, image, upstream, b_here, scale_here, conv_bias_here, gain_here, bias_here, sems
):
    width = features.shape[1]
    pairs = [
        (flags, flags_here), (cotangent, upstream), (scale, scale_here), (w_out, w_out_here),
        (features, image), (taps, taps_here), (w_in, w_in_here), (b_in, b_here),
        (conv_bias, conv_bias_here), (gain, gain_here), (bias, bias_here),
    ]
    copies = [pltpu.make_async_copy(src, dst, sems.at[i]) for i, (src, dst) in enumerate(pairs)]
    for copy in copies:
        copy.start()
    for copy in copies[:3]:
        copy.wait()
    widen(upstream, wide)
    rows = SIDE * SIDE
    by_lane = scale_here[...].reshape(1, width)
    for k, lanes in enumerate(lane_blocks(width)):
        for t in range(COLS // SIDE):
            gate = flags_here[0, t].astype(jnp.float32)
            tile = jnp.concatenate(
                [wide[k, pl.ds(t * SIDE + j, SIDE, stride=COLS), :] for j in range(SIDE)], axis=0
            )
            tile = (tile * by_lane[:, lanes] * gate).astype(jnp.bfloat16)
            out_grad[t * rows : (t + 1) * rows, lanes] = tile
    copies[3].wait()
    back[...] = matmul(w_out_here[...], out_grad[...], NT)
    copies[4].wait()
    copies[5].wait()
    widen(image, wide)
    def convolve_tile(t):
        for k, lanes in enumerate(lane_blocks(width)):
            columns = []
            for j in range(t * SIDE - HALO, (t + 1) * SIDE + HALO):
                inside = 0 <= j < COLS
                columns.append(wide[k, pl.ds(j, SIDE, stride=COLS), :] if inside else None)
            for j, total in enumerate(convolve(columns, taps_here, lanes, False)):
                start = (t * SIDE + j) * SIDE
                conv[start : start + SIDE, lanes] = total

    for t in range(COLS // SIDE):
        tissue = flags_here[0, t] != 0
        pl.when(tissue)(functools.partial(convolve_tile, t))

        @pl.when(jnp.logical_not(tissue))
        def _(t=t):
            conv[t * rows : (t + 1) * rows, :] = jnp.zeros((rows, width), jnp.float32)

    for copy in copies[6:]:
        copy.wait()
    hidden = w_in.shape[1]
    for start in range(0, hidden, LANES):
        w_in_t[start : start + LANES, :] = w_in_here[:, start : start + LANES].T
        b_cols[start : start + LANES, :] = jnp.broadcast_to(
            b_here[start : start + LANES].reshape(1, LANES), (LANES, LANES)
        ).T
    for i, vector in enumerate((conv_bias_here, gain_here, bias_here)):
        vectors[i * SIDE : (i + 1) * SIDE, :] = jnp.broadcast_to(
            vector[...].reshape(1, width), (SIDE, width)
        )


def middle_kernel(
    device, conv, low, high, taps, vectors, w_in_t, b_cols, out_grad, back,
    kept, sent, standard, inverse, grad_pre,
    rows, low_wide, high_wide, normed, preact, hidden
):
    width = conv.shape[1]
    rows[...] = conv[...]
    low_wide[...] = low[...].astype(jnp.float32)
    high_wide[...] = high[...].astype(jnp.float32)
    for lanes in lane_blocks(width):
        near = [low_wide[(HALO + j) * SIDE : (HALO + j + 1) * SIDE, lanes] for j in range(HALO)]
        for j, total in enumerate(convolve(near + [None] * (2 * HALO), taps, lanes, False)):
            rows[j * SIDE : (j + 1) * SIDE, lanes] += total
        near = [high_wide[j * SIDE : (j + 1) * SIDE, lanes] for j in range(HALO)]
        for j, total in enumerate(convolve([None] * (2 * HALO) + near, taps, lanes, False)):
            start = (COLS - HALO + j) * SIDE
            rows[start : start + SIDE, lanes] += total
    gain, bias = vectors[SIDE : SIDE + 1, :], vectors[2 * SIDE : 2 * SIDE + 1, :]
    conv_out = rows[...] + vectors[:1, :]
    centre = conv_out - jnp.mean(conv_out, axis=-1, keepdims=True)
    scale = lax.rsqrt(jnp.mean(centre * centre, axis=-1, keepdims=True) + EPSILON)
    inverse[...] = jnp.broadcast_to(scale, inverse.shape)
    standard[...] = centre * scale
    normed[...] = (standard[...] * gain + bias).astype(jnp.bfloat16)
    preact[...] = matmul(w_in_t[...], normed[...], NT)

    def step(i, carry):
        part = pl.ds(pl.multiple_of(i * CHUNK, CHUNK), CHUNK)
        for lanes in lane_blocks(preact.shape[1]):
            z = preact[part, lanes] + b_cols[part, :]
            below = 0.5 * (1.0 + lax.erf(z * 0.7071067811865476))
            density = jnp.exp(-0.5 * z * z) * 0.3989422804014327
            hidden[part, lanes] = (z * below).astype(jnp.bfloat16)
            slope = below + z * density
            grad_pre[part, lanes] = (back[part, lanes] * slope).astype(jnp.bfloat16)
        return carry

    lax.fori_loop(0, preact.shape[0] // CHUNK, step, 0, unroll=2)
    half = hidden.shape[0] // 2
    core = device[0] & 1
    other = pl.ds(pl.multiple_of((1 - core) * half, half), half)
    own = pl.ds(pl.multiple_of(core * half, half), half)
    sent[:half, :] = matmul(hidden[other, :], out_grad[...]).astype(jnp.bfloat16)
    kept[:half, :] = matmul(hidden[own, :], out_grad[...])
    run = 64 * ROWS
    for i in range(half // run):
        place = half + i * run
        start = pl.multiple_of((2 * i + 1 - core) * run, run)
        sent[place : place + run, :] = matmul(grad_pre[pl.ds(start, run), :], normed[...]).astype(jnp.bfloat16)
        start = pl.multiple_of((2 * i + core) * run, run)
        kept[place : place + run, :] = matmul(grad_pre[pl.ds(start, run), :], normed[...])


def through_norm(grad_std, standard, inverse):
    mean = jnp.mean(grad_std, axis=-1, keepdims=True)
    along = jnp.mean(grad_std * standard, axis=-1, keepdims=True)
    return inverse * (grad_std - mean - standard * along)


def back_kernel(
    grad_pre, w_in, standard, inverse, vectors, w_out, w_in_t, b_cols, taps, own_low, own_high, low, high,
    grad_conv, low_conv, high_conv,
    rows, out_grad, preact, back, halo_pre
):
    conv_bias, gain, bias = (vectors[i * SIDE : i * SIDE + 1, :] for i in range(3))
    grad_std = matmul(w_in[...], grad_pre[...]).T * gain
    grad_conv[...] = through_norm(grad_std, standard[...], inverse[:, :1])

    edge = HALO * SIDE
    rows[...] = jnp.zeros_like(rows)
    for lanes in lane_blocks(rows.shape[1]):
        near, far = ([x[:, lanes].astype(jnp.float32) for x in pair] for pair in ((own_low, own_high), (low, high)))
        for i in range(2):
            column = lambda block, j: block[j * SIDE : (j + 1) * SIDE, :]
            beyond = [column(far[i], j) for j in range(2 * HALO)]
            inside = [column(near[i], j + i * HALO) for j in range(HALO)]
            columns = inside + beyond if i else beyond + inside
            for j, total in enumerate(convolve(columns, taps, lanes, False)):
                start = i * edge + j * SIDE
                rows[start : start + SIDE, lanes] = total
        grads = [block[2 * edge : 3 * edge, :] for block in far]
        grads.append(jnp.zeros((rows.shape[0] - 2 * edge, LANES), jnp.float32))
        out_grad[:, lanes] = jnp.concatenate(grads, axis=0).astype(jnp.bfloat16)
    conv_out = rows[...] + conv_bias
    centre = conv_out - jnp.mean(conv_out, axis=-1, keepdims=True)
    scale = lax.rsqrt(jnp.mean(centre * centre, axis=-1, keepdims=True) + EPSILON)
    norm = centre * scale
    preact[...] = matmul(w_in_t[...], (norm * gain + bias).astype(jnp.bfloat16), NT)
    back[...] = matmul(w_out[...], out_grad[...], NT)

    def step(i, carry):
        part = pl.ds(pl.multiple_of(i * CHUNK, CHUNK), CHUNK)
        z = preact[part, :] + b_cols[part, :]
        below = 0.5 * (1.0 + lax.erf(z * 0.7071067811865476))
        density = jnp.exp(-0.5 * z * z) * 0.3989422804014327
        halo_pre[part, :] = (back[part, :] * (below + z * density)).astype(jnp.bfloat16)
        return carry

    lax.fori_loop(0, preact.shape[0] // CHUNK, step, 0, unroll=4)
    grad_std = matmul(w_in[...], halo_pre[...]).T * gain
    result = through_norm(grad_std, norm, scale)
    low_conv[...] = result[:edge, :]
    high_conv[...] = result[edge : 2 * edge, :]


def last_kernel(grad_conv, low, high, taps, cotangent, grad_features, wide):
    for k, lanes in enumerate(lane_blocks(grad_conv.shape[1])):
        for t in range(COLS // SIDE):
            columns = []
            for j in range(t * SIDE - HALO, (t + 1) * SIDE + HALO):
                if j < 0:
                    source, place = low, j + HALO
                elif j >= COLS:
                    source, place = high, j - COLS
                else:
                    source, place = grad_conv, j
                columns.append(source[place * SIDE : (place + 1) * SIDE, lanes])
            for j, total in enumerate(convolve(columns, taps, lanes, True)):
                wide[k, pl.ds(t * SIDE + j, SIDE, stride=COLS), :] = total
        result = cotangent[:, lanes].astype(jnp.float32) + wide[k]
        grad_features[:, lanes] = result.astype(jnp.bfloat16)


def cube_kernel(kept, received, message):
    members, rows, _ = message.shape
    rows //= 2
    half = members * rows
    for m in range(members):
        part = slice(m * rows, (m + 1) * rows)
        total = kept[part, :] + received[part, :].astype(jnp.float32)
        message[m, :rows, :] = total.astype(jnp.bfloat16)
    run = 2 * ROWS
    for top, bit5 in itertools.product(range(2), repeat=2):
        totals = []
        for i in (2 * top, 2 * top + 1):
            start = half + (2 * i + bit5) * rows
            totals.append(kept[start : start + rows, :] + received[start : start + rows, :].astype(jnp.float32))
        for low in range(4):
            runs = [
                total[(4 * i + low) * run : (4 * i + low + 1) * run, :] for total in totals for i in range(4)
            ]
            place = rows + top * 8 * run
            message[bit5 * 4 + low, place : place + 8 * run, :] = jnp.concatenate(runs, axis=0).astype(jnp.bfloat16)


def add_members(received):
    summed = received[0].astype(jnp.float32)
    for i in range(1, received.shape[0]):
        summed += received[i].astype(jnp.float32)
    return summed


def four_kernel(received, message, total):
    members, rows, width = message.shape
    rows //= 2
    summed = add_members(received)
    for k, lanes in enumerate(lane_blocks(width)):
        total[k] = summed[:, lanes]
        for m in range(members):
            parts = [total[k, m * rows : (m + 1) * rows, :]]
            for r in range(ROWS):
                start = members * rows + (m % 2) * 2 * ROWS + (m // 2) * ROWS + r
                parts.append(total[k, pl.ds(start, SIDE, stride=members * ROWS), :])
            message[m, :, lanes] = jnp.concatenate(parts, axis=0).astype(jnp.bfloat16)


def eight_kernel(received, message, total, block):
    rows = received.shape[1] // 2
    members = message.shape[0]
    summed = add_members(received)
    for k, lanes in enumerate(lane_blocks(received.shape[2])):
        total[k] = summed[:, lanes]
    block[...] = jnp.zeros_like(block)
    block[:rows, :] = summed[:rows, :]
    for m in range(members):
        for k, lanes in enumerate(lane_blocks(received.shape[2])):
            block[rows : rows + ROWS, lanes] = total[k, pl.ds(rows + m, ROWS, stride=members), :]
        message[m] = block[...].astype(jnp.bfloat16)


def turn_kernel(scale, received, message, grad_w_in):
    finished = add_members(received) * scale
    rows = message.shape[1]
    grad_w_in[...] = finished[rows : rows + ROWS, :]
    whole = finished[:rows, :].astype(jnp.bfloat16)
    for m in range(message.shape[0]):
        message[m] = whole


def join_kernel(device, own, other, in_rows, grad_w_out, grad_w_in):
    core = device[0] & 1
    grad_w_in[...] = in_rows[...]
    members, rows, _ = own.shape
    for place, blocks in ((core, own), (1 - core, other)):
        for m in range(0, members, 2):
            pair = [blocks[i].astype(jnp.float32) for i in (m, m + 1)]
            start = pl.multiple_of((place * members + m) * rows, 2 * rows)
            grad_w_out[pl.ds(start, 2 * rows), :] = jnp.concatenate(pair, axis=0).astype(jnp.bfloat16)


def call(kernel, outs, scratch, scalars, arrays, flops, nbytes, space=pltpu.VMEM):
    if space == pltpu.HBM:
        arrays = [pltpu.with_memory_space_constraint(array, pltpu.HBM) for array in arrays]
    in_specs = [pl.BlockSpec(memory_space=pltpu.SMEM)] * len(scalars)
    in_specs += [pl.BlockSpec(memory_space=space)] * len(arrays)
    return pl.pallas_call(
        kernel,
        out_shape=[jax.ShapeDtypeStruct(shape, kind) for shape, kind in outs],
        in_specs=in_specs,
        out_specs=[pl.BlockSpec(memory_space=pltpu.VMEM)] * len(outs),
        scratch_shapes=scratch,
        compiler_params=pltpu.CompilerParams(vmem_limit_bytes=VMEM_LIMIT),
        cost_estimate=pl.CostEstimate(flops=flops, bytes_accessed=nbytes, transcendentals=0),
    )(*scalars, *arrays)


F32, B16 = jnp.float32, jnp.bfloat16


def edges(flags, features, cotangent, layer_scale):
    rows, width = features.shape
    wide = pltpu.VMEM((width // LANES, rows, LANES), F32)
    return call(
        edge_kernel,
        [((EDGE, width), B16), ((EDGE, width), B16)],
        [pltpu.SMEM(flags.shape, jnp.int32), pltpu.VMEM((rows, width), B16), pltpu.VMEM((rows, width), B16),
         pltpu.VMEM((width,), F32), wide, wide, pltpu.SemaphoreType.DMA((4,))],
        [],
        [flags, features, cotangent, layer_scale],
        features.size, 4 * features.size, pltpu.HBM,
    )


def before_halos(flags, features, cotangent, kernel, conv_bias, gain, bias, w_in, b_in, w_out, layer_scale):
    rows, width = features.shape
    hidden = w_out.shape[0]
    return call(
        first_kernel,
        [((rows, width), F32), ((rows, width), B16), ((hidden, rows), F32), ((hidden, width), B16),
         ((hidden, LANES), F32), (w_in.shape, B16), (w_out.shape, B16), (kernel.shape, F32), ((3 * SIDE, width), F32)],
        [pltpu.VMEM((width // LANES, rows, LANES), F32), pltpu.SMEM(flags.shape, jnp.int32),
         pltpu.VMEM((rows, width), B16), pltpu.VMEM((rows, width), B16),
         pltpu.VMEM(b_in.shape, F32), pltpu.VMEM((width,), F32), pltpu.VMEM((width,), F32),
         pltpu.VMEM((width,), F32), pltpu.VMEM((width,), F32),
         pltpu.SemaphoreType.DMA((11,))],
        [],
        [flags, features, cotangent, w_out, w_in, b_in, kernel, layer_scale, conv_bias, gain, bias],
        2 * rows * width * hidden, 8 * 1024 * 1024, pltpu.HBM,
    )


def middle(device, conv, low, high, taps, vectors, w_in_t, b_cols, out_grad, back):
    rows, width = conv.shape
    hidden = w_in_t.shape[0]
    halo = pltpu.VMEM((EDGE, width), F32)
    return call(
        middle_kernel,
        [((hidden, width), F32), ((hidden, width), B16), ((rows, width), F32), ((rows, LANES), F32), ((hidden, rows), B16)],
        [pltpu.VMEM((rows, width), F32), halo, halo, pltpu.VMEM((rows, width), B16),
         pltpu.VMEM((hidden, rows), F32), pltpu.VMEM((hidden, rows), B16)],
        [device],
        [conv, low, high, taps, vectors, w_in_t, b_cols, out_grad, back],
        6 * rows * width * hidden, 12 * 1024 * 1024,
    )


def to_conv(grad_pre, w_in, standard, inverse, vectors, *more):
    rows, width = standard.shape
    hidden = grad_pre.shape[0]
    edge = (HALO * SIDE, width)
    return call(
        back_kernel, [((rows, width), F32), (edge, F32), (edge, F32)],
        [pltpu.VMEM((LANES, width), F32), pltpu.VMEM((LANES, width), B16), pltpu.VMEM((hidden, LANES), F32),
         pltpu.VMEM((hidden, LANES), F32), pltpu.VMEM((hidden, LANES), B16)],
        [],
        [grad_pre, w_in, standard, inverse, vectors, *more],
        2 * grad_pre.size * width, 4 * grad_pre.size,
    )


def to_features(grad_conv, low, high, taps, cotangent):
    rows, width = grad_conv.shape
    return call(
        last_kernel,
        [((rows, width), B16)],
        [pltpu.VMEM((width // LANES, rows, LANES), F32)],
        [],
        [grad_conv, low, high, taps, cotangent],
        2 * 49 * rows * width, 2 * 1024 * 1024,
    )[0]


def to_cube(members, kept, received):
    rows, width = kept.shape
    return call(
        cube_kernel, [((members, rows // members, width), B16)], [], [], [kept, received], 2 * kept.size, 8 * kept.size
    )[0]


def to_four(received, members):
    _, rows, width = received.shape
    return call(
        four_kernel, [((members, rows // members, width), B16)],
        [pltpu.VMEM((width // LANES, rows, LANES), F32)], [], [received],
        received.size, 3 * received.size,
    )[0]


def to_eight(received, members):
    _, rows, width = received.shape
    return call(
        eight_kernel,
        [((members, rows // 2 + SIDE, width), B16)],
        [pltpu.VMEM((width // LANES, rows, LANES), F32), pltpu.VMEM((rows // 2 + SIDE, width), F32)],
        [],
        [received],
        received.size, 4 * received.size,
    )[0]


def turn(scale, received, members):
    _, rows, width = received.shape
    return call(
        functools.partial(turn_kernel, scale),
        [((members, rows - SIDE, width), B16), ((ROWS, width), F32)], [], [], [received],
        received.size, 4 * received.size,
    )


def join(device, own, other, in_rows):
    members, rows, width = own.shape
    return call(
        join_kernel, [((2 * members * rows, width), B16), (in_rows.shape, F32)], [], [device], [own, other, in_rows],
        own.size, 8 * own.size,
    )


def from_left(block):
    count = lax.axis_size(TILE)
    return lax.ppermute(block, TILE, [(i, i + 1) for i in range(count - 1)])


def from_right(block):
    count = lax.axis_size(TILE)
    return lax.ppermute(block, TILE, [(i + 1, i) for i in range(count - 1)])


def exchange(blocks, axes):
    return lax.all_to_all(blocks, axes, split_axis=0, concat_axis=0, tiled=True)


def swap(block):
    return lax.ppermute(block, "c", SWAP)


def body(
    features, cotangent, kernel, conv_bias, ln_gain, ln_bias, w_in, b_in, w_out, layer_scale, tissue
):
    image = features[0]
    height, breadth, channels = image.shape
    rows = image.reshape(-1, channels)
    upstream = cotangent[0].reshape(-1, channels)
    own_low, own_high = edges(tissue, rows, upstream, layer_scale)
    low, high = from_left(own_high), from_right(own_low)
    device = lax.axis_index(EVERY).astype(jnp.int32).reshape(1)
    sizes = {axis: lax.axis_size(axis) for axis in EVERY}
    cube, four, eight = (math.prod(sizes[axis] for axis in axes) for axes in (CUBE, FOUR, EIGHT))
    scale = 1.0 / math.sqrt(height * breadth * math.prod(sizes.values()))

    conv, out_grad, back, w_in_t, b_cols, w_in_here, w_out_here, taps, vectors = before_halos(
        tissue, rows, upstream, kernel, conv_bias, ln_gain, ln_bias, w_in, b_in, w_out, layer_scale
    )
    kept, sent, standard, inverse, grad_pre = middle(
        device, conv, low, high, taps, vectors, w_in_t, b_cols, out_grad, back
    )
    grad_conv, low, high = to_conv(
        grad_pre, w_in_here, standard, inverse, vectors,
        w_out_here, w_in_t, b_cols, taps, own_low, own_high, low, high,
    )
    kept, low, high = lax.optimization_barrier((kept, low, high))
    received = exchange(to_cube(cube, kept, swap(sent)), CUBE)
    received = exchange(to_four(received, four), FOUR)
    received, low, high = lax.optimization_barrier((received, low, high))
    grad_image = to_features(grad_conv, low, high, taps, upstream)
    received = exchange(to_eight(received, eight), EIGHT)
    received, grad_image = lax.optimization_barrier((received, grad_image))
    message, in_rows = turn(scale, received, cube * four)
    own = exchange(message, CUBE + FOUR)
    pairs = [(2 * xh + c, 2 * c + xh) for xh in range(2) for c in range(2)]
    in_rows = lax.ppermute(in_rows, ("xh", "c"), pairs)
    own, in_rows = lax.optimization_barrier((own, in_rows))
    grad_w_out, grad_w_in = join(device, own, swap(own), in_rows)
    return (grad_image.reshape(1, height, breadth, channels), grad_w_in, grad_w_out)


def solution(mesh):
    fine = jax.sharding.Mesh(mesh.devices.reshape(4, 2, 2, 2, 2, 2, 2, 2), EVERY)
    band = P(("zl", "c"), None, TILE, None)
    placed = (band, band) + (P(),) * 8 + (P(("zl", "c"), TILE),)
    return jax.shard_map(
        body,
        mesh=fine,
        in_specs=placed,
        out_specs=(band, P(EVERY, None), P()),
        check_vma=False,
    )
```

```python
import functools
import itertools
import math

import jax
import jax.numpy as jnp
from jax import lax
from jax.experimental import pallas as pl
from jax.experimental.pallas import tpu as pltpu
from jax.sharding import PartitionSpec as P

SIDE = 8
HALO = 3
TAPS = 7
COLS = 32
LANES = 128
CHUNK = 32
ROWS = 3
EDGE = 10 * SIDE
EPSILON = 1e-06
VMEM_LIMIT = 16 * 1024 * 1024
NT = (((1,), (1,)), ((), ()))

TILE = ("zh", "xh", "xl", "y2", "y1", "yl")
CUBE = ("xl", "yl", "zl")
FOUR = ("xh", "y1")
EIGHT = ("zh", "y2")
EVERY = ("zh", "xh", "xl", "y2", "y1", "yl", "zl", "c")
SWAP = [(0, 1), (1, 0)]


def matmul(left, right, dims=(((1,), (0,)), ((), ()))):
    return lax.dot_general(left, right, dims, preferred_element_type=jnp.float32)


def shifted(column, a):
    move = a - HALO
    if move == 0:
        return column
    row = lax.broadcasted_iota(jnp.int32, column.shape, 0)
    inside = (row + move >= 0) & (row + move < SIDE)
    return jnp.where(inside, pltpu.roll(column, (-move) % SIDE, 0), 0.0)


def convolve(columns, taps, lanes, flip):
    count = len(columns) - 2 * HALO
    totals = [None] * count
    for a in range(TAPS):
        sums = [None] * count
        for e in range(TAPS):
            row, place = (TAPS - 1 - a, TAPS - 1 - e) if flip else (a, e)
            tap = taps[row, place : place + 1, lanes]
            for j in range(count):
                if columns[j + e] is None:
                    continue
                term = columns[j + e] * tap
                sums[j] = term if sums[j] is None else sums[j] + term
        for j in range(count):
            if sums[j] is None:
                continue
            moved = shifted(sums[j], a)
            totals[j] = moved if totals[j] is None else totals[j] + moved
    return totals


def lane_blocks(width):
    return [slice(start, start + LANES) for start in range(0, width, LANES)]


def widen(source, wide):
    for k, lanes in enumerate(lane_blocks(source.shape[1])):
        wide[k] = source[:, lanes].astype(jnp.float32)


def edge_kernel(
    flags, features, cotangent, scale, low, high, flags_here, image, upstream, scale_here, wide, wide_grad, sems
):
    pairs = [(features, image), (cotangent, upstream), (scale, scale_here), (flags, flags_here)]
    copies = [pltpu.make_async_copy(src, dst, sems.at[i]) for i, (src, dst) in enumerate(pairs)]
    for copy in copies:
        copy.start()
    for copy in copies:
        copy.wait()
    widen(image, wide)
    widen(upstream, wide_grad)
    by_lane = scale_here[...].reshape(1, features.shape[1])
    for k, lanes in enumerate(lane_blocks(features.shape[1])):
        for first, first_grad, edge in ((0, 0, low), (COLS - 2 * HALO, COLS - HALO, high)):
            columns = [wide[k, pl.ds(first + j, SIDE, stride=COLS), :] for j in range(2 * HALO)]
            gate = flags_here[0, first_grad // SIDE].astype(jnp.float32)
            for j in range(HALO):
                column = wide_grad[k, pl.ds(first_grad + j, SIDE, stride=COLS), :]
                columns.append(column * by_lane[:, lanes] * gate)
            columns.append(jnp.zeros((SIDE, LANES), jnp.float32))
            edge[:, lanes] = jnp.concatenate(columns, axis=0).astype(jnp.bfloat16)


def first_kernel(
    flags, features, cotangent, w_out, w_in, b_in, taps, scale, conv_bias, gain, bias,
    conv, out_grad, back, w_in_t, b_cols, w_in_here, w_out_here, taps_here, vectors,
    wide, flags_here, image, upstream, b_here, scale_here, conv_bias_here, gain_here, bias_here, sems
):
    width = features.shape[1]
    pairs = [
        (flags, flags_here), (cotangent, upstream), (scale, scale_here), (w_out, w_out_here),
        (features, image), (taps, taps_here), (w_in, w_in_here), (b_in, b_here),
        (conv_bias, conv_bias_here), (gain, gain_here), (bias, bias_here),
    ]
    copies = [pltpu.make_async_copy(src, dst, sems.at[i]) for i, (src, dst) in enumerate(pairs)]
    for copy in copies:
        copy.start()
    for copy in copies[:3]:
        copy.wait()
    widen(upstream, wide)
    rows = SIDE * SIDE
    by_lane = scale_here[...].reshape(1, width)
    for k, lanes in enumerate(lane_blocks(width)):
        for t in range(COLS // SIDE):
            gate = flags_here[0, t].astype(jnp.float32)
            tile = jnp.concatenate(
                [wide[k, pl.ds(t * SIDE + j, SIDE, stride=COLS), :] for j in range(SIDE)], axis=0
            )
            tile = (tile * by_lane[:, lanes] * gate).astype(jnp.bfloat16)
            out_grad[t * rows : (t + 1) * rows, lanes] = tile
    copies[3].wait()
    back[...] = matmul(w_out_here[...], out_grad[...], NT)
    copies[4].wait()
    copies[5].wait()
    widen(image, wide)
    def convolve_tile(t):
        for k, lanes in enumerate(lane_blocks(width)):
            columns = []
            for j in range(t * SIDE - HALO, (t + 1) * SIDE + HALO):
                inside = 0 <= j < COLS
                columns.append(wide[k, pl.ds(j, SIDE, stride=COLS), :] if inside else None)
            for j, total in enumerate(convolve(columns, taps_here, lanes, False)):
                start = (t * SIDE + j) * SIDE
                conv[start : start + SIDE, lanes] = total

    for t in range(COLS // SIDE):
        tissue = flags_here[0, t] != 0
        pl.when(tissue)(functools.partial(convolve_tile, t))

        @pl.when(jnp.logical_not(tissue))
        def _(t=t):
            conv[t * rows : (t + 1) * rows, :] = jnp.zeros((rows, width), jnp.float32)

    for copy in copies[6:]:
        copy.wait()
    hidden = w_in.shape[1]
    for start in range(0, hidden, LANES):
        w_in_t[start : start + LANES, :] = w_in_here[:, start : start + LANES].T
        b_cols[start : start + LANES, :] = jnp.broadcast_to(
            b_here[start : start + LANES].reshape(1, LANES), (LANES, LANES)
        ).T
    for i, vector in enumerate((conv_bias_here, gain_here, bias_here)):
        vectors[i * SIDE : (i + 1) * SIDE, :] = jnp.broadcast_to(
            vector[...].reshape(1, width), (SIDE, width)
        )


def middle_kernel(
    device, conv, low, high, taps, vectors, w_in_t, b_cols, out_grad, back,
    kept, sent, standard, inverse, grad_pre,
    rows, low_wide, high_wide, normed, preact, hidden
):
    width = conv.shape[1]
    rows[...] = conv[...]
    low_wide[...] = low[...].astype(jnp.float32)
    high_wide[...] = high[...].astype(jnp.float32)
    for lanes in lane_blocks(width):
        near = [low_wide[(HALO + j) * SIDE : (HALO + j + 1) * SIDE, lanes] for j in range(HALO)]
        for j, total in enumerate(convolve(near + [None] * (2 * HALO), taps, lanes, False)):
            rows[j * SIDE : (j + 1) * SIDE, lanes] += total
        near = [high_wide[j * SIDE : (j + 1) * SIDE, lanes] for j in range(HALO)]
        for j, total in enumerate(convolve([None] * (2 * HALO) + near, taps, lanes, False)):
            start = (COLS - HALO + j) * SIDE
            rows[start : start + SIDE, lanes] += total
    gain, bias = vectors[SIDE : SIDE + 1, :], vectors[2 * SIDE : 2 * SIDE + 1, :]
    conv_out = rows[...] + vectors[:1, :]
    centre = conv_out - jnp.mean(conv_out, axis=-1, keepdims=True)
    scale = lax.rsqrt(jnp.mean(centre * centre, axis=-1, keepdims=True) + EPSILON)
    inverse[...] = jnp.broadcast_to(scale, inverse.shape)
    standard[...] = centre * scale
    normed[...] = (standard[...] * gain + bias).astype(jnp.bfloat16)
    preact[...] = matmul(w_in_t[...], normed[...], NT)

    def step(i, carry):
        part = pl.ds(pl.multiple_of(i * CHUNK, CHUNK), CHUNK)
        for lanes in lane_blocks(preact.shape[1]):
            z = preact[part, lanes] + b_cols[part, :]
            below = 0.5 * (1.0 + lax.erf(z * 0.7071067811865476))
            density = jnp.exp(-0.5 * z * z) * 0.3989422804014327
            hidden[part, lanes] = (z * below).astype(jnp.bfloat16)
            slope = below + z * density
            grad_pre[part, lanes] = (back[part, lanes] * slope).astype(jnp.bfloat16)
        return carry

    lax.fori_loop(0, preact.shape[0] // CHUNK, step, 0, unroll=2)
    half = hidden.shape[0] // 2
    core = device[0] & 1
    other = pl.ds(pl.multiple_of((1 - core) * half, half), half)
    own = pl.ds(pl.multiple_of(core * half, half), half)
    sent[:half, :] = matmul(hidden[other, :], out_grad[...]).astype(jnp.bfloat16)
    kept[:half, :] = matmul(hidden[own, :], out_grad[...])
    run = 64 * ROWS
    for i in range(half // run):
        place = half + i * run
        start = pl.multiple_of((2 * i + 1 - core) * run, run)
        sent[place : place + run, :] = matmul(grad_pre[pl.ds(start, run), :], normed[...]).astype(jnp.bfloat16)
        start = pl.multiple_of((2 * i + core) * run, run)
        kept[place : place + run, :] = matmul(grad_pre[pl.ds(start, run), :], normed[...])


def through_norm(grad_std, standard, inverse):
    mean = jnp.mean(grad_std, axis=-1, keepdims=True)
    along = jnp.mean(grad_std * standard, axis=-1, keepdims=True)
    return inverse * (grad_std - mean - standard * along)


def back_kernel(
    grad_pre, w_in, standard, inverse, vectors, w_out, w_in_t, b_cols, taps, own_low, own_high, low, high,
    grad_conv, low_conv, high_conv,
    rows, out_grad, preact, back, halo_pre
):
    conv_bias, gain, bias = (vectors[i * SIDE : i * SIDE + 1, :] for i in range(3))
    grad_std = matmul(w_in[...], grad_pre[...]).T * gain
    grad_conv[...] = through_norm(grad_std, standard[...], inverse[:, :1])

    edge = HALO * SIDE
    rows[...] = jnp.zeros_like(rows)
    for lanes in lane_blocks(rows.shape[1]):
        near, far = ([x[:, lanes].astype(jnp.float32) for x in pair] for pair in ((own_low, own_high), (low, high)))
        for i in range(2):
            column = lambda block, j: block[j * SIDE : (j + 1) * SIDE, :]
            beyond = [column(far[i], j) for j in range(2 * HALO)]
            inside = [column(near[i], j + i * HALO) for j in range(HALO)]
            columns = inside + beyond if i else beyond + inside
            for j, total in enumerate(convolve(columns, taps, lanes, False)):
                start = i * edge + j * SIDE
                rows[start : start + SIDE, lanes] = total
        grads = [block[2 * edge : 3 * edge, :] for block in far]
        grads.append(jnp.zeros((rows.shape[0] - 2 * edge, LANES), jnp.float32))
        out_grad[:, lanes] = jnp.concatenate(grads, axis=0).astype(jnp.bfloat16)
    conv_out = rows[...] + conv_bias
    centre = conv_out - jnp.mean(conv_out, axis=-1, keepdims=True)
    scale = lax.rsqrt(jnp.mean(centre * centre, axis=-1, keepdims=True) + EPSILON)
    norm = centre * scale
    preact[...] = matmul(w_in_t[...], (norm * gain + bias).astype(jnp.bfloat16), NT)
    back[...] = matmul(w_out[...], out_grad[...], NT)

    def step(i, carry):
        part = pl.ds(pl.multiple_of(i * CHUNK, CHUNK), CHUNK)
        z = preact[part, :] + b_cols[part, :]
        below = 0.5 * (1.0 + lax.erf(z * 0.7071067811865476))
        density = jnp.exp(-0.5 * z * z) * 0.3989422804014327
        halo_pre[part, :] = (back[part, :] * (below + z * density)).astype(jnp.bfloat16)
        return carry

    lax.fori_loop(0, preact.shape[0] // CHUNK, step, 0, unroll=4)
    grad_std = matmul(w_in[...], halo_pre[...]).T * gain
    result = through_norm(grad_std, norm, scale)
    low_conv[...] = result[:edge, :]
    high_conv[...] = result[edge : 2 * edge, :]


def last_kernel(grad_conv, low, high, taps, cotangent, grad_features, wide):
    for k, lanes in enumerate(lane_blocks(grad_conv.shape[1])):
        for t in range(COLS // SIDE):
            columns = []
            for j in range(t * SIDE - HALO, (t + 1) * SIDE + HALO):
                if j < 0:
                    source, place = low, j + HALO
                elif j >= COLS:
                    source, place = high, j - COLS
                else:
                    source, place = grad_conv, j
                columns.append(source[place * SIDE : (place + 1) * SIDE, lanes])
            for j, total in enumerate(convolve(columns, taps, lanes, True)):
                wide[k, pl.ds(t * SIDE + j, SIDE, stride=COLS), :] = total
        result = cotangent[:, lanes].astype(jnp.float32) + wide[k]
        grad_features[:, lanes] = result.astype(jnp.bfloat16)


def cube_kernel(kept, received, message):
    members, rows, _ = message.shape
    rows //= 2
    half = members * rows
    for m in range(members):
        part = slice(m * rows, (m + 1) * rows)
        total = kept[part, :] + received[part, :].astype(jnp.float32)
        message[m, :rows, :] = total.astype(jnp.bfloat16)
    run = 2 * ROWS
    for top, bit5 in itertools.product(range(2), repeat=2):
        totals = []
        for i in (2 * top, 2 * top + 1):
            start = half + (2 * i + bit5) * rows
            totals.append(kept[start : start + rows, :] + received[start : start + rows, :].astype(jnp.float32))
        for low in range(4):
            runs = [
                total[(4 * i + low) * run : (4 * i + low + 1) * run, :] for total in totals for i in range(4)
            ]
            place = rows + top * 8 * run
            message[bit5 * 4 + low, place : place + 8 * run, :] = jnp.concatenate(runs, axis=0).astype(jnp.bfloat16)


def add_members(received):
    summed = received[0].astype(jnp.float32)
    for i in range(1, received.shape[0]):
        summed += received[i].astype(jnp.float32)
    return summed


def four_kernel(received, message, total):
    members, rows, width = message.shape
    rows //= 2
    summed = add_members(received)
    for k, lanes in enumerate(lane_blocks(width)):
        total[k] = summed[:, lanes]
        for m in range(members):
            parts = [total[k, m * rows : (m + 1) * rows, :]]
            for r in range(ROWS):
                start = members * rows + (m % 2) * 2 * ROWS + (m // 2) * ROWS + r
                parts.append(total[k, pl.ds(start, SIDE, stride=members * ROWS), :])
            message[m, :, lanes] = jnp.concatenate(parts, axis=0).astype(jnp.bfloat16)


def eight_kernel(received, message, total, block):
    rows = received.shape[1] // 2
    members = message.shape[0]
    summed = add_members(received)
    for k, lanes in enumerate(lane_blocks(received.shape[2])):
        total[k] = summed[:, lanes]
    block[...] = jnp.zeros_like(block)
    block[:rows, :] = summed[:rows, :]
    for m in range(members):
        for k, lanes in enumerate(lane_blocks(received.shape[2])):
            block[rows : rows + ROWS, lanes] = total[k, pl.ds(rows + m, ROWS, stride=members), :]
        message[m] = block[...].astype(jnp.bfloat16)


def turn_kernel(scale, received, message, grad_w_in):
    finished = add_members(received) * scale
    rows = message.shape[1]
    grad_w_in[...] = finished[rows : rows + ROWS, :]
    whole = finished[:rows, :].astype(jnp.bfloat16)
    for m in range(message.shape[0]):
        message[m] = whole


def join_kernel(device, own, other, in_rows, grad_w_out, grad_w_in):
    core = device[0] & 1
    grad_w_in[...] = in_rows[...]
    members, rows, _ = own.shape
    for place, blocks in ((core, own), (1 - core, other)):
        for m in range(0, members, 2):
            start = pl.multiple_of((place * members + m) * rows, 2 * rows)
            pair = jnp.concatenate([blocks[m], blocks[m + 1]], axis=0)
            grad_w_out[pl.ds(start, 2 * rows), :] = pair


def call(kernel, outs, scratch, scalars, arrays, flops, nbytes, space=pltpu.VMEM):
    if space == pltpu.HBM:
        arrays = [pltpu.with_memory_space_constraint(array, pltpu.HBM) for array in arrays]
    in_specs = [pl.BlockSpec(memory_space=pltpu.SMEM)] * len(scalars)
    in_specs += [pl.BlockSpec(memory_space=space)] * len(arrays)
    return pl.pallas_call(
        kernel,
        out_shape=[jax.ShapeDtypeStruct(shape, kind) for shape, kind in outs],
        in_specs=in_specs,
        out_specs=[pl.BlockSpec(memory_space=pltpu.VMEM)] * len(outs),
        scratch_shapes=scratch,
        compiler_params=pltpu.CompilerParams(vmem_limit_bytes=VMEM_LIMIT),
        cost_estimate=pl.CostEstimate(flops=flops, bytes_accessed=nbytes, transcendentals=0),
    )(*scalars, *arrays)


F32, B16 = jnp.float32, jnp.bfloat16


def edges(flags, features, cotangent, layer_scale):
    rows, width = features.shape
    wide = pltpu.VMEM((width // LANES, rows, LANES), F32)
    return call(
        edge_kernel,
        [((EDGE, width), B16), ((EDGE, width), B16)],
        [pltpu.SMEM(flags.shape, jnp.int32), pltpu.VMEM((rows, width), B16), pltpu.VMEM((rows, width), B16),
         pltpu.VMEM((width,), F32), wide, wide, pltpu.SemaphoreType.DMA((4,))],
        [],
        [flags, features, cotangent, layer_scale],
        features.size, 4 * features.size, pltpu.HBM,
    )


def before_halos(flags, features, cotangent, kernel, conv_bias, gain, bias, w_in, b_in, w_out, layer_scale):
    rows, width = features.shape
    hidden = w_out.shape[0]
    return call(
        first_kernel,
        [((rows, width), F32), ((rows, width), B16), ((hidden, rows), F32), ((hidden, width), B16),
         ((hidden, LANES), F32), (w_in.shape, B16), (w_out.shape, B16), (kernel.shape, F32), ((3 * SIDE, width), F32)],
        [pltpu.VMEM((width // LANES, rows, LANES), F32), pltpu.SMEM(flags.shape, jnp.int32),
         pltpu.VMEM((rows, width), B16), pltpu.VMEM((rows, width), B16),
         pltpu.VMEM(b_in.shape, F32), pltpu.VMEM((width,), F32), pltpu.VMEM((width,), F32),
         pltpu.VMEM((width,), F32), pltpu.VMEM((width,), F32),
         pltpu.SemaphoreType.DMA((11,))],
        [],
        [flags, features, cotangent, w_out, w_in, b_in, kernel, layer_scale, conv_bias, gain, bias],
        2 * rows * width * hidden, 8 * 1024 * 1024, pltpu.HBM,
    )


def middle(device, conv, low, high, taps, vectors, w_in_t, b_cols, out_grad, back):
    rows, width = conv.shape
    hidden = w_in_t.shape[0]
    halo = pltpu.VMEM((EDGE, width), F32)
    return call(
        middle_kernel,
        [((hidden, width), F32), ((hidden, width), B16), ((rows, width), F32), ((rows, LANES), F32), ((hidden, rows), B16)],
        [pltpu.VMEM((rows, width), F32), halo, halo, pltpu.VMEM((rows, width), B16),
         pltpu.VMEM((hidden, rows), F32), pltpu.VMEM((hidden, rows), B16)],
        [device],
        [conv, low, high, taps, vectors, w_in_t, b_cols, out_grad, back],
        6 * rows * width * hidden, 12 * 1024 * 1024,
    )


def to_conv(grad_pre, w_in, standard, inverse, vectors, *more):
    rows, width = standard.shape
    hidden = grad_pre.shape[0]
    edge = (HALO * SIDE, width)
    return call(
        back_kernel, [((rows, width), F32), (edge, F32), (edge, F32)],
        [pltpu.VMEM((LANES, width), F32), pltpu.VMEM((LANES, width), B16), pltpu.VMEM((hidden, LANES), F32),
         pltpu.VMEM((hidden, LANES), F32), pltpu.VMEM((hidden, LANES), B16)],
        [],
        [grad_pre, w_in, standard, inverse, vectors, *more],
        2 * grad_pre.size * width, 4 * grad_pre.size,
    )


def to_features(grad_conv, low, high, taps, cotangent):
    rows, width = grad_conv.shape
    return call(
        last_kernel,
        [((rows, width), B16)],
        [pltpu.VMEM((width // LANES, rows, LANES), F32)],
        [],
        [grad_conv, low, high, taps, cotangent],
        2 * 49 * rows * width, 2 * 1024 * 1024,
    )[0]


def to_cube(members, kept, received):
    rows, width = kept.shape
    return call(
        cube_kernel, [((members, rows // members, width), B16)], [], [], [kept, received], 2 * kept.size, 8 * kept.size
    )[0]


def to_four(received, members):
    _, rows, width = received.shape
    return call(
        four_kernel, [((members, rows // members, width), B16)],
        [pltpu.VMEM((width // LANES, rows, LANES), F32)], [], [received],
        received.size, 3 * received.size,
    )[0]


def to_eight(received, members):
    _, rows, width = received.shape
    return call(
        eight_kernel,
        [((members, rows // 2 + SIDE, width), B16)],
        [pltpu.VMEM((width // LANES, rows, LANES), F32), pltpu.VMEM((rows // 2 + SIDE, width), F32)],
        [],
        [received],
        received.size, 4 * received.size,
    )[0]


def turn(scale, received, members):
    _, rows, width = received.shape
    return call(
        functools.partial(turn_kernel, scale),
        [((members, rows - SIDE, width), B16), ((ROWS, width), F32)], [], [], [received],
        received.size, 4 * received.size,
    )


def join(device, own, other, in_rows):
    members, rows, width = own.shape
    return call(
        join_kernel, [((2 * members * rows, width), B16), (in_rows.shape, F32)], [], [device], [own, other, in_rows],
        own.size, 8 * own.size,
    )


def from_left(block):
    count = lax.axis_size(TILE)
    return lax.ppermute(block, TILE, [(i, i + 1) for i in range(count - 1)])


def from_right(block):
    count = lax.axis_size(TILE)
    return lax.ppermute(block, TILE, [(i + 1, i) for i in range(count - 1)])


def exchange(blocks, axes):
    return lax.all_to_all(blocks, axes, split_axis=0, concat_axis=0, tiled=True)


def swap(block):
    return lax.ppermute(block, "c", SWAP)


def body(
    features, cotangent, kernel, conv_bias, ln_gain, ln_bias, w_in, b_in, w_out, layer_scale, tissue
):
    image = features[0]
    height, breadth, channels = image.shape
    rows = image.reshape(-1, channels)
    upstream = cotangent[0].reshape(-1, channels)
    own_low, own_high = edges(tissue, rows, upstream, layer_scale)
    low, high = from_left(own_high), from_right(own_low)
    device = lax.axis_index(EVERY).astype(jnp.int32).reshape(1)
    sizes = {axis: lax.axis_size(axis) for axis in EVERY}
    cube, four, eight = (math.prod(sizes[axis] for axis in axes) for axes in (CUBE, FOUR, EIGHT))
    scale = 1.0 / math.sqrt(height * breadth * math.prod(sizes.values()))

    conv, out_grad, back, w_in_t, b_cols, w_in_here, w_out_here, taps, vectors = before_halos(
        tissue, rows, upstream, kernel, conv_bias, ln_gain, ln_bias, w_in, b_in, w_out, layer_scale
    )
    kept, sent, standard, inverse, grad_pre = middle(
        device, conv, low, high, taps, vectors, w_in_t, b_cols, out_grad, back
    )
    grad_conv, low, high = to_conv(
        grad_pre, w_in_here, standard, inverse, vectors,
        w_out_here, w_in_t, b_cols, taps, own_low, own_high, low, high,
    )
    kept, low, high = lax.optimization_barrier((kept, low, high))
    received = exchange(to_cube(cube, kept, swap(sent)), CUBE)
    received = exchange(to_four(received, four), FOUR)
    received = exchange(to_eight(received, eight), EIGHT)
    message, in_rows = turn(scale, received, cube * four)
    own = exchange(message, CUBE + FOUR)
    pairs = [(2 * xh + c, 2 * c + xh) for xh in range(2) for c in range(2)]
    in_rows = lax.ppermute(in_rows, ("xh", "c"), pairs)
    message, low, high = lax.optimization_barrier((message, low, high))
    grad_image = to_features(grad_conv, low, high, taps, upstream)
    own, in_rows, grad_image = lax.optimization_barrier((own, in_rows, grad_image))
    grad_w_out, grad_w_in = join(device, own, swap(own), in_rows)
    return (grad_image.reshape(1, height, breadth, channels), grad_w_in, grad_w_out)


def solution(mesh):
    fine = jax.sharding.Mesh(mesh.devices.reshape(4, 2, 2, 2, 2, 2, 2, 2), EVERY)
    band = P(("zl", "c"), None, TILE, None)
    placed = (band, band) + (P(),) * 8 + (P(("zl", "c"), TILE),)
    return jax.shard_map(
        body,
        mesh=fine,
        in_specs=placed,
        out_specs=(band, P(EVERY, None), P()),
        check_vma=False,
    )
```
